128 devices in a mesh: dp: 64 (over y, x, z), expert: 2 (over core).
Axes of the slice: x: 4, y: 4, z: 4, core: 2. Of those that a mesh axis runs over, the one named last changes fastest.
Arguments:
- tokens: bfloat16 [65536, 768], P(('dp', 'expert')), may hold values from -6 to 6
- item_kind: int32 [1664], P(('dp', 'expert')), may hold values from 0 to 2
- cotangent: bfloat16 [65536, 768], P(('dp', 'expert')), may hold values from -6 to 6
- norm1_gain: bfloat16 [768], replicated, may hold values from 0.5 to 1.5
- norm1_shift: bfloat16 [768], replicated, may hold values from -0.625 to 0.625
- qkv_weight: bfloat16 [768, 2304], replicated, may hold values from -0.21875 to 0.21875
- query_bias: bfloat16 [768], replicated, may hold values from -1.25 to 1.25
- value_bias: bfloat16 [768], replicated, may hold values from -1.25 to 1.25
- out_weight: bfloat16 [768, 768], replicated, may hold values from -0.4375 to 0.4375
- out_bias: bfloat16 [768], replicated, may hold values from -0.625 to 0.625
- norm2_gain: bfloat16 [2, 768], P('expert', 'dp'), may hold values from 0.5 to 1.5
- norm2_shift: bfloat16 [2, 768], P('expert', 'dp'), may hold values from -0.625 to 0.625
- ffn_in: bfloat16 [2, 768, 3072], P('expert', None, 'dp'), may hold values from -0.21875 to 0.21875
- ffn_in_bias: bfloat16 [2, 3072], P('expert', 'dp'), may hold values from -0.625 to 0.625
- ffn_out: bfloat16 [2, 3072, 768], P('expert', 'dp'), may hold values from -0.109375 to 0.109375
- ffn_out_bias: bfloat16 [2, 768], P('expert', 'dp'), may hold values from -0.625 to 0.625
Outputs:
- mixed: bfloat16 [65536, 768], P(('dp', 'expert'))
- tokens_grad: float32 [65536, 768], P(('dp', 'expert'))
- norm1_gain_grad: float32 [768], replicated
- norm1_shift_grad: float32 [768], replicated
- qkv_weight_grad: float32 [768, 2304], replicated
- query_bias_grad: float32 [768], replicated
- value_bias_grad: float32 [768], replicated
- out_weight_grad: float32 [768, 768], replicated
- out_bias_grad: float32 [768], replicated
- norm2_gain_grad: float32 [2, 768], P('expert', 'dp')
- norm2_shift_grad: float32 [2, 768], P('expert', 'dp')
- ffn_in_grad: float32 [2, 768, 3072], P('expert', None, 'dp')
- ffn_in_bias_grad: float32 [2, 3072], P('expert', 'dp')
- ffn_out_grad: float32 [2, 3072, 768], P('expert', 'dp')
- ffn_out_bias_grad: float32 [2, 768], P('expert', 'dp')
The draws below stay inside these ranges and needn't reach their ends.
All inputs are finite; a program needn't handle non-finite values.
Results may differ from the reference program's by a relative error of at most 0.014.
Values may be sent and summed in bfloat16 or wider, within the bound.
No kernel may reach another device: no remote copies, remote signals or barrier semaphores. Data moves between devices by JAX's collectives and lax.ppermute only.
A program may use at most 192 MiB of HBM per device.

```python
import jax
import jax.numpy as jnp
from jax import lax

D = 768
HEADS = 12
HEAD_DIM = 64
FF = 3072
IMG_LEN = 197
TXT_LEN = 40
TOK_DEV = 512
ITEMS_DEV = 13
TOKENS = 65536
ITEMS = 1664


def with_ends(values, key, smallest, high):
    place = [jax.random.randint(jax.random.fold_in(key, axis), (), 0, length) for axis, length in enumerate(values.shape)]
    main_axis = values.shape.index(max(values.shape))
    beside = place[:main_axis] + [(place[main_axis] + 1) % values.shape[main_axis]] + place[main_axis + 1:]
    return values.at[tuple(place)].set(smallest).at[tuple(beside)].set(high)


def block_levels(own_key, extent, cuts, least, largest):
    def one(dim, parts):
        draws = jax.random.uniform(jax.random.fold_in(jax.random.fold_in(own_key, 6), dim), (parts,), jnp.float32, least / len(cuts), largest / len(cuts))
        return jnp.repeat(jnp.exp(draws), extent[dim] // parts).reshape((-1,) + (1,) * (len(extent) - dim - 1))

    loudness = one(*cuts[0])
    for cut in cuts[1:]:
        loudness = loudness * one(*cut)
    return loudness


def scatter_about(stream_key, shape, width, reach, pieces=(), held_as=jnp.bfloat16):
    loudness = block_levels(stream_key, shape, pieces, -0.22, 0.18) if pieces else 1.0
    array = jax.random.normal(stream_key, shape, jnp.float32) * width * loudness
    return jnp.minimum(jnp.maximum(array, -reach), reach).astype(held_as)


def setup_inputs(seed: int = 0) -> dict:
    key_list = jax.random.split(jax.random.key(seed), 17)
    return {
        "tokens": scatter_about(key_list[0], (TOKENS, D), 1.0, 6.0, ((0, 128),)),
        "item_kind": with_ends(jax.random.randint(key_list[1], (ITEMS,), 0, 3), jax.random.fold_in(key_list[1], 1), 0, 2).astype(jnp.int32),
        "cotangent": scatter_about(key_list[2], (TOKENS, D), 1.0, 6.0, ((0, 128),)),
        "norm1_gain": jnp.clip(1.0 + 0.1 * jax.random.normal(key_list[3], (D,), jnp.float32), 0.5, 1.5).astype(jnp.bfloat16),
        "norm1_shift": scatter_about(key_list[4], (D,), 0.1, 0.625),
        "qkv_weight": scatter_about(key_list[5], (D, 3 * D), D ** -0.5, 0.21875),
        "query_bias": scatter_about(key_list[6], (D,), 0.2, 1.25),
        "value_bias": scatter_about(key_list[7], (D,), 0.2, 1.25),
        "out_weight": scatter_about(key_list[8], (D, D), (D // 4) ** -0.5, 0.4375),
        "out_bias": scatter_about(key_list[9], (D,), 0.1, 0.625),
        "norm2_gain": jnp.clip(1.0 + 0.1 * jax.random.normal(key_list[10], (2, D), jnp.float32), 0.5, 1.5).astype(jnp.bfloat16),
        "norm2_shift": scatter_about(key_list[11], (2, D), 0.1, 0.625, ((0, 2), (1, 64))),
        "ffn_in": scatter_about(key_list[12], (2, D, FF), D ** -0.5, 0.21875, ((0, 2), (2, 64))),
        "ffn_in_bias": scatter_about(key_list[13], (2, FF), 0.1, 0.625, ((0, 2), (1, 64))),
        "ffn_out": scatter_about(key_list[14], (2, FF, D), FF ** -0.5, 0.109375, ((0, 2), (1, 64))),
        "ffn_out_bias": scatter_about(key_list[15], (2, D), 0.1, 0.625, ((0, 2), (1, 64))),
    }


epsilon = 1e-05
masked_score = -1e+30

@jax.custom_vjp
def low(v):
    return lax.optimization_barrier(v.astype(jnp.bfloat16)).astype(jnp.float32)

@jax.custom_vjp
def low_back(v):
    return v

def low_keep(v):
    return (low(v), None)

def low_pass(kept, grad):
    return (grad,)

def back_keep(v):
    return (v, None)

def back_low(kept, grad):
    return (low(grad),)
low.defvjp(low_keep, low_pass)
low_back.defvjp(back_keep, back_low)

def layer_norm(values, gain_row, shift_row):
    average = lax.optimization_barrier(jnp.mean(values, axis=-1, keepdims=True))
    centred = values - average
    variance = lax.optimization_barrier(jnp.mean(centred * centred, axis=-1, keepdims=True))
    return centred * lax.rsqrt(variance + epsilon) * gain_row + shift_row

def item_layout(kinds, row_count):
    lengths = jnp.where(kinds == 0, IMG_LEN, jnp.where(kinds == 1, TXT_LEN, IMG_LEN + TXT_LEN)).astype(jnp.int32)
    item_ends = jnp.cumsum(lengths).astype(jnp.int32)
    item_starts = item_ends - lengths
    places = lax.iota(jnp.int32, row_count)
    inside = (places[:, None] >= item_starts[None, :]) & (places[:, None] < item_ends[None, :])
    item_of = lax.optimization_barrier(jnp.sum((places[:, None] >= item_ends[None, :]).astype(jnp.int32), axis=1)).astype(jnp.int32)
    offsets = places - lax.optimization_barrier(jnp.sum(jnp.where(inside, item_starts[None, :], 0), axis=1)).astype(jnp.int32)
    kind_rows = lax.optimization_barrier(jnp.sum(jnp.where(inside, kinds[None, :], 0), axis=1)).astype(jnp.int32)
    language = (kind_rows == 1) | (kind_rows == 2) & (offsets >= IMG_LEN)
    return (item_of, language)

def product(left, right):
    return jnp.dot(left, right, precision=lax.Precision.HIGHEST, preferred_element_type=jnp.float32)

def layer_pack(weights, block_rows, kinds):
    gain_one, shift_one, qkv_weight, query_bias, value_bias, out_weight, out_bias, gain_two, shift_two, ffn_in, ffn_in_bias, ffn_out, ffn_out_bias = weights
    item_of, language = item_layout(kinds, TOK_DEV)
    normed = low(layer_norm(block_rows, gain_one, shift_one))
    triple_bias = jnp.concatenate([query_bias, jnp.zeros_like(query_bias), value_bias])
    triple = low_back(low(product(normed, qkv_weight) + triple_bias))
    triple = triple.reshape(TOK_DEV, 3, HEADS, HEAD_DIM)
    query, key_part, value_part = (triple[:, 0], triple[:, 1], triple[:, 2])
    raw_scores = jnp.einsum('qhd,khd->hqk', query, key_part, precision=lax.Precision.HIGHEST)
    scores = low_back(raw_scores * HEAD_DIM ** (-0.5))
    same_item = item_of[:, None] == item_of[None, :]
    scores = jnp.where(same_item[None], scores, masked_score)
    top_score = lax.optimization_barrier(jnp.max(scores, axis=-1, keepdims=True))
    exponent = jnp.exp(scores - top_score)
    probs = low(exponent / lax.optimization_barrier(jnp.sum(exponent, axis=-1, keepdims=True)))
    context = jnp.einsum('hqk,khd->qhd', probs, value_part, precision=lax.Precision.HIGHEST).reshape(TOK_DEV, D)
    context = low_back(low(context))
    hidden_one = block_rows + low_back(product(context, out_weight)) + out_bias
    routed = low_back(low(hidden_one))
    branches = []
    for expert_index in range(2):
        normed_two = low(layer_norm(routed, gain_two[expert_index], shift_two[expert_index]))
        pre_active = low_back(product(normed_two, ffn_in[expert_index]) + ffn_in_bias[expert_index])
        active = low(jax.nn.gelu(pre_active, approximate=False))
        branches.append(low_back(low(product(active, ffn_out[expert_index]) + ffn_out_bias[expert_index])))
    return hidden_one + jnp.where(language[:, None], branches[1], branches[0])

def reference(tokens, item_kind, cotangent, norm1_gain, norm1_shift, qkv_weight, query_bias, value_bias, out_weight, out_bias, norm2_gain, norm2_shift, ffn_in, ffn_in_bias, ffn_out, ffn_out_bias):
    params = tuple((entry.astype(jnp.float32) for entry in (norm1_gain, norm1_shift, qkv_weight, query_bias, value_bias, out_weight, out_bias, norm2_gain, norm2_shift, ffn_in, ffn_in_bias, ffn_out, ffn_out_bias)))
    kind_packs = item_kind.reshape(-1, ITEMS_DEV)

    def forward(rows_all, weights):
        packs = rows_all.reshape(-1, TOK_DEV, D)

        def one_pack(inputs_pair):
            return layer_pack(weights, inputs_pair[0], inputs_pair[1])
        return lax.map(jax.checkpoint(one_pack), (packs, kind_packs)).reshape(-1, D)
    result, pullback = jax.vjp(forward, tokens.astype(jnp.float32), params)
    grad_tokens, grads = pullback(cotangent.astype(jnp.float32))
    return (result.astype(jnp.bfloat16), grad_tokens, grads[0], grads[1], grads[2], grads[3], grads[4], grads[5], grads[6], grads[7], grads[8], grads[9], grads[10], grads[11], grads[12])
```

```python
import functools

import jax
import jax.numpy as jnp
from jax import lax
from jax.experimental import pallas as pl
from jax.experimental.pallas import tpu as pltpu
from jax.sharding import PartitionSpec as P

HEADS = 12
IMG_LEN = 197
TXT_LEN = 40
ROWS = 512
CHIP_ROWS = 1024
D = 768
FF = 3072
ITEMS_DEV = 13
PAIRS = HEADS // 2
LANES = 128
BLOCK = 256
MASKED = -1e30
EPS = 1e-5
PLANS = {
    "qkv": (20, False),
    "attend": (16, False),
    "outproj": (12, False),
    "select": (20, False),
    "sort": (12, False),
    "expert": (44, True),
    "post": (24, False),
    "attend_back": (20, False),
    "final": (32, False),
    "split": (16, False),
    "join": (12, False),
    "assemble": (24, False),
}
AR_ROWS = 3264
SMALL_ROWS = AR_ROWS - 4 * D
AR_PIECE = AR_ROWS // 12
HALF = D // 2

bf16 = jnp.bfloat16
f32 = jnp.float32


def dot(left, right):
    return jnp.dot(left, right, preferred_element_type=f32)


def dot_t(left, right):
    return lax.dot_general(left, right, (((1,), (1,)), ((), ())), preferred_element_type=f32)


def dot_0(left, right):
    return lax.dot_general(left, right, (((0,), (0,)), ((), ())), preferred_element_type=f32)


def params(mebibytes):
    return pltpu.CompilerParams(vmem_limit_bytes=mebibytes * 1024 * 1024)


def cost(flops, byts, trans=0):
    return pl.CostEstimate(flops=int(flops), bytes_accessed=int(byts), transcendentals=int(trans))


def shape(dims, dtype):
    return jax.ShapeDtypeStruct(dims, dtype)


VM = pl.BlockSpec(memory_space=pltpu.VMEM)
SM = pl.BlockSpec(memory_space=pltpu.SMEM)
HB = pl.BlockSpec(memory_space=pl.ANY)


def staged_call(body, name, smem, small, loads, outs, plain=(), scratch=(), flops=1e9, raw=()):
    n_out = len(outs)
    limit, staged = PLANS[name]
    big = HB if staged else VM

    def plain_kernel(*refs):
        at = len(smem) + len(small)
        s_refs, v_refs = refs[: len(smem)], refs[len(smem) : at]
        ins, rest = refs[at : at + len(loads)], refs[at + len(loads) :]
        results, extra = rest[: n_out + len(plain)], rest[n_out + len(plain) :]
        body(s_refs, v_refs, lambda i: ins[i], results, lambda j: None, extra)

    def kernel(*refs):
        refs = list(refs)
        take = lambda n: [refs.pop(0) for _ in range(n)]
        s_refs, v_refs, hbm, raw_refs = take(len(smem)), take(len(small)), take(len(loads)), take(len(raw))
        out_hbm = take(n_out)
        plain_refs, bufs, out_bufs, extra = take(len(plain)), take(len(loads)), take(n_out), take(len(scratch))
        in_sem, out_sem = refs
        copies = [pltpu.make_async_copy(a, b, in_sem.at[i]) for i, (a, b) in enumerate(zip(hbm, bufs))]
        for copy in copies:
            copy.start()
        waiting, sent = set(range(len(copies))), []

        def get(i):
            if i in waiting:
                copies[i].wait()
                waiting.discard(i)
            return bufs[i]

        def put(j):
            copy = pltpu.make_async_copy(out_bufs[j], out_hbm[j], out_sem.at[j])
            copy.start()
            sent.append(copy)

        body(s_refs, v_refs, get, out_bufs + plain_refs, put, ([raw_refs] if raw else []) + extra)
        assert not waiting and len(sent) == n_out
        for copy in sent:
            copy.wait()

    bytes_moved = sum(v.size * v.dtype.itemsize for v in (*loads, *outs))
    buffers = [pltpu.VMEM(v.shape, v.dtype) for v in (*loads, *outs)] if staged else []
    sems = [pltpu.SemaphoreType.DMA((len(loads),)), pltpu.SemaphoreType.DMA((n_out,))] if staged else []
    return pl.pallas_call(
        kernel if staged else plain_kernel,
        out_shape=(*outs, *(struct for struct, _ in plain)),
        in_specs=[SM] * len(smem) + [VM] * len(small) + [big] * len(loads) + [HB] * len(raw),
        out_specs=(big,) * n_out + tuple(spec for _, spec in plain),
        scratch_shapes=buffers + list(scratch) + sems,
        compiler_params=params(limit),
        cost_estimate=cost(flops, bytes_moved),
        name=name,
    )(*smem, *small, *loads, *raw)


def norm_stats(x):
    centred = x - jnp.mean(x, axis=-1, keepdims=True)
    rstd = lax.rsqrt(jnp.mean(centred * centred, axis=-1, keepdims=True) + EPS)
    return centred * rstd, rstd


def item_lengths(kind):
    vision = jnp.where(kind == 1, 0, IMG_LEN)
    language = jnp.where(kind == 0, 0, TXT_LEN)
    return vision, language


def qkv_kernel(smem, small, get, outs, put, scratch):
    (kind_ref,), (vec_ref,) = smem, small
    n1_ref, tri_ref, bias_ref, lang_ref = outs
    gain, shift, q_bias, v_bias = (vec_ref[i * D : (i + 1) * D].reshape(1, D) for i in range(4))
    tok_ref = get(0)
    for r in range(0, ROWS, LANES):
        xhat, _ = norm_stats(tok_ref[r : r + LANES, :].astype(f32))
        n1_ref[r : r + LANES, :] = (xhat * gain + shift).astype(bf16)
    put(0)
    n1 = n1_ref[...]
    w_ref = get(1)
    q = dot(n1, w_ref[:, 0:D]) + q_bias
    tri_ref[:, 0:D] = q.astype(bf16) * jnp.asarray(0.125, bf16)
    tri_ref[:, D : 2 * D] = dot(n1, w_ref[:, D : 2 * D]).astype(bf16)
    tri_ref[:, 2 * D :] = (dot(n1, w_ref[:, 2 * D :]) + v_bias).astype(bf16)
    put(1)
    down = lax.broadcasted_iota(jnp.int32, (ROWS, LANES), 0)
    across = lax.broadcasted_iota(jnp.int32, (8, ROWS), 1)
    item_down = jnp.zeros((ROWS, LANES), jnp.int32)
    item_across = jnp.zeros((8, ROWS), jnp.int32)
    lang = jnp.zeros((ROWS, LANES), f32)
    start = 0
    for i in range(ITEMS_DEV):
        vision, language = item_lengths(kind_ref[0, i])
        middle = start + vision
        end = middle + language
        item_down += (down >= end).astype(jnp.int32)
        item_across += (across >= end).astype(jnp.int32)
        lang = jnp.where((down >= middle) & (down < end), 1.0, lang)
        start = end
    lang_ref[...] = lang
    put(3)
    for c in range(0, ROWS, LANES):
        same = item_down == item_across[0:1, c : c + LANES]
        bias_ref[:, c : c + LANES] = jnp.where(same, 0.0, MASKED)
    put(2)


def qkv_call(kinds, tokens, vecs, weight):
    outs = (shape((ROWS, D), bf16), shape((ROWS, 3 * D), bf16), shape((ROWS, ROWS), f32), shape((ROWS, LANES), f32))
    return staged_call(qkv_kernel, "qkv", [kinds], [vecs], [tokens, weight], outs, flops=2 * ROWS * D * 3 * D * 2)


def half_lanes(head):
    lane = lax.broadcasted_iota(jnp.int32, (1, LANES), 1)
    return (lane < LANES // 2) if head == 0 else (lane >= LANES // 2)


def attend_kernel(q_ref, k_ref, v_ref, bias_ref, ctx_ref, lse_ref):
    q, k, v = q_ref[...], k_ref[...], v_ref[...]
    zero = jnp.zeros_like(q)
    rows = lax.broadcasted_iota(jnp.int32, (LANES, 1), 0)
    parts = []
    for head in range(2):
        qm = jnp.where(half_lanes(head), q, zero)
        s = dot_t(k, qm) + bias_ref[...]
        top = jnp.max(s, axis=0, keepdims=True)
        e = jnp.exp(s - top)
        total = jnp.sum(e, axis=0, keepdims=True)
        lse_ref[0, head : head + 1, :] = top + jnp.log(total)
        parts.append(dot_0(v, e.astype(bf16)) * (1.0 / total))
    ctx = jnp.where(rows < LANES // 2, parts[0], parts[1])
    ctx_ref[...] = ctx.T.astype(bf16)


def attend_call(triple, bias, first, count):
    def col(offset):
        return pl.BlockSpec((ROWS, LANES), lambda p: (0, offset + first + p))

    return pl.pallas_call(
        attend_kernel,
        grid=(count,),
        out_shape=(shape((ROWS, count * LANES), bf16), shape((count, 8, ROWS), f32)),
        in_specs=[col(0), col(PAIRS), col(2 * PAIRS), pl.BlockSpec((ROWS, ROWS), lambda p: (0, 0))],
        out_specs=(
            pl.BlockSpec((ROWS, LANES), lambda p: (0, p)),
            pl.BlockSpec((1, 8, ROWS), lambda p: (p, 0, 0)),
        ),
        compiler_params=params(PLANS["attend"][0]),
        cost_estimate=cost(count * 2 * 4e9, count * 6e6),
        name="attend",
    )(triple, triple, triple, bias)


def out_kernel(smem, small, get, outs, put, scratch):
    hid_ref, routed_ref = outs
    half = D // 2
    ca_ref, cb_ref, w_ref = get(0), get(1), get(2)
    h = dot(ca_ref[...], w_ref[:half, :]) + dot(cb_ref[...], w_ref[half:, :])
    h = get(3)[...].astype(f32) + h + small[0][4 * D :].reshape(1, D)
    routed_ref[...] = h.astype(bf16)
    put(1)
    hid_ref[...] = h
    put(0)


def out_call(ctx_a, ctx_b, weight, vecs, tokens):
    outs = (shape((ROWS, D), f32), shape((ROWS, D), bf16))
    return staged_call(
        out_kernel, "outproj", [], [vecs], [ctx_a, ctx_b, weight, tokens], outs, flops=2 * ROWS * D * D * 2
    )


def select_kernel(smem, small, get, outs, put, scratch):
    (kind_ref,) = smem
    sel_ref, turned_ref, up_ref, nv_ref = outs
    spans = []
    vision_total = 0
    for pack in range(2):
        start = 0
        for i in range(ITEMS_DEV):
            vision, language = item_lengths(kind_ref[pack, i])
            first = jnp.minimum(start, ROWS)
            middle = jnp.minimum(start + vision, ROWS)
            end = jnp.minimum(start + vision + language, ROWS)
            spans.append((pack, first, middle, end))
            vision_total = vision_total + middle - first
            start = start + vision + language
    nv_ref[0] = vision_total
    place = lax.broadcasted_iota(jnp.int32, (1, ROWS), 1)
    target = [jnp.zeros((1, ROWS), jnp.int32) for _ in range(2)]
    at_vision, at_language = 0, vision_total
    for pack, first, middle, end in spans:
        t = target[pack]
        t = jnp.where((place >= first) & (place < middle), place + (at_vision - first), t)
        t = jnp.where((place >= middle) & (place < end), place + (at_language - middle), t)
        target[pack] = t
        at_vision = at_vision + middle - first
        at_language = at_language + end - middle
    own, other = get(0)[...], get(1)[...]
    for r in range(0, CHIP_ROWS, BLOCK):
        down = lax.broadcasted_iota(jnp.int32, (BLOCK, ROWS), 0) + r
        for pack in range(2):
            sel_ref[r : r + BLOCK, pack * ROWS : (pack + 1) * ROWS] = (
                (down == target[pack]).astype(f32).astype(bf16)
            )
        turned_ref[:, r : r + BLOCK] = sel_ref[r : r + BLOCK, :].T
        up_ref[r : r + BLOCK, :] = (
            dot(sel_ref[r : r + BLOCK, :ROWS], own) + dot(sel_ref[r : r + BLOCK, ROWS:], other)
        ).astype(bf16)
    for j in range(3):
        put(j)


def select_call(kinds, own, other):
    square = shape((CHIP_ROWS, CHIP_ROWS), bf16)
    outs = (square, square, shape((CHIP_ROWS, D), bf16))
    plain = ((shape((1,), jnp.int32), SM),)
    flops = 2 * 2 * CHIP_ROWS * CHIP_ROWS * D
    return staged_call(select_kernel, "select", [kinds], [], [own, other], outs, plain, flops=flops)


def sort_kernel(smem, small, get, outs, put, scratch):
    sel_ref = get(0)
    own, other = get(1)[...], get(2)[...]
    for r in range(0, CHIP_ROWS, BLOCK):
        x = dot(sel_ref[r : r + BLOCK, :ROWS], own) + dot(sel_ref[r : r + BLOCK, ROWS:], other)
        outs[0][r : r + BLOCK, :] = x.astype(bf16)
    put(0)


def sort_call(select, own, other):
    return staged_call(
        sort_kernel,
        "sort",
        [],
        [],
        [select, own, other],
        (shape((CHIP_ROWS, D), bf16),),
        flops=2 * CHIP_ROWS * CHIP_ROWS * D,
    )[0]


def gelu_parts(x):
    z = jnp.abs(x) * 0.7071067811865476
    t = 1.0 / (1.0 + 0.3275911 * z)
    poly = t * (
        0.254829592 + t * (-0.284496736 + t * (1.421413741 + t * (-1.453152027 + t * 1.061405429)))
    )
    bell = jnp.exp(x * x * -0.5)
    tail = 0.5 * poly * bell
    phi = jnp.where(x >= 0, 1.0 - tail, tail)
    return x * phi, phi + x * bell * 0.3989422804014327


THIRDS = 3
PIECE = 128
HALF_HID = THIRDS * 2 * PIECE


def expert_kernel(first, smem, small, get, outs, put, scratch):
    (nv_ref,), bias_ref = smem, small[0]
    w_hbm, scratch = scratch[0], scratch[1:]
    if first:
        branch_ref, gn2_ref, n2_ref, db_ref = outs[:4]
        dw_hbm = outs[4:]
    else:
        own_ref, other_ref, db_ref = outs[:3]
        dw_hbm = outs[3:]
        branch_ref, gn2_ref, scratch = scratch[0], scratch[1], scratch[2:]
    w_ref, acc_ref, out_ref, act_ref, gp_ref, in_sem, out_sem = scratch
    loads = []
    for k in range(THIRDS):
        for j in range(2):
            at = k * 2 * PIECE + j * PIECE
            ref = w_hbm[2 * k + j if first else k]
            for m in range(4):
                block = m if first else 4 * j + m
                part = ref.at[block] if len(ref.shape) == 3 else ref.at[pl.ds(block * PIECE, PIECE), :]
                copy = pltpu.make_async_copy(
                    part, w_ref.at[m, pl.ds(at, PIECE), :], in_sem.at[8 * k + 4 * j + m]
                )
                copy.start()
                loads.append(copy)
    branch_ref[...] = jnp.zeros_like(branch_ref)
    gn2_ref[...] = jnp.zeros_like(gn2_ref)
    x_ref = get(0)
    if first:
        par = small[1][...].astype(f32)
        for r in range(0, CHIP_ROWS, LANES):
            xhat, _ = norm_stats(x_ref[r : r + LANES, :].astype(f32))
            vision = (lax.broadcasted_iota(jnp.int32, (LANES, 1), 0) + r) < nv_ref[0]
            gain = jnp.where(vision, par[0:1, :], par[1:2, :])
            shift = jnp.where(vision, par[2:3, :], par[3:4, :])
            n2_ref[r : r + LANES, :] = (xhat * gain + shift).astype(bf16)
        put(2)
    else:
        n2_ref = x_ref
    up_ref = get(1)
    db_ref[...] = jnp.zeros_like(db_ref)
    for copy in loads:
        copy.wait()
    nv = nv_ref[0]
    stores = []
    for e in range(2):
        low = jnp.int32(0) if e == 0 else nv // BLOCK
        high = (nv + BLOCK - 1) // BLOCK if e == 0 else jnp.int32(CHIP_ROWS // BLOCK)
        acc_ref[...] = jnp.zeros_like(acc_ref)

        def visit(block, size, e=e):
            at = pl.multiple_of(block * BLOCK, BLOCK)
            rows = pl.ds(at, size)
            index = lax.broadcasted_iota(jnp.int32, (size, 1), 0) + at
            valid = (index < nv) if e == 0 else (index >= nv)
            n2 = n2_ref[rows, :]
            up = up_ref[rows, :]
            for k in range(THIRDS):
                hid = slice(k * BLOCK, (k + 1) * BLOCK)
                pre = dot_t(n2, w_ref[2 * e, hid, :]) + bias_ref[e : e + 1, hid].astype(f32)
                back = dot_t(up, w_ref[2 * e + 1, hid, :])
                active, slope = gelu_parts(pre)
                act = jnp.where(valid, active, 0.0).astype(bf16)
                gp = jnp.where(valid, back * slope, 0.0).astype(bf16)
                act_ref[:size, hid] = act
                gp_ref[:size, hid] = gp
                db_ref[e : e + 1, hid] += jnp.sum(gp.astype(f32), axis=0, keepdims=True)
            acc_ref[0] += dot_0(gp_ref[:size, :], n2)
            acc_ref[1] += dot_0(act_ref[:size, :], up)
            branch_ref[rows, :] += dot(act_ref[:size, :], w_ref[2 * e + 1])
            gn2_ref[rows, :] += dot(gp_ref[:size, :], w_ref[2 * e])

        count = high - low

        def two(i, carry, visit=visit, low=low):
            visit(low + 2 * i, 2 * BLOCK)
            return carry

        lax.fori_loop(0, count // 2, two, 0)

        @pl.when(count % 2 == 1)
        def _(visit=visit, high=high):
            visit(high - 1, BLOCK)

        out_ref[2 * e] = acc_ref[0].astype(bf16)
        out_ref[2 * e + 1] = acc_ref[1].astype(bf16)
        for k in range(THIRDS):
            for j in range(2):
                at = k * 2 * PIECE + j * PIECE
                copy = pltpu.make_async_copy(
                    out_ref.at[pl.ds(2 * e, 2), pl.ds(at, PIECE), :],
                    dw_hbm[2 * k + j].at[pl.ds(2 * e, 2)],
                    out_sem.at[6 * e + 2 * k + j],
                )
                copy.start()
                stores.append(copy)
    if first:
        put(0)
        put(1)
    else:
        turned_ref = get(2)
        for i, total in enumerate((branch_ref, gn2_ref)):
            y = (get(3 + i)[...] + total[...]).astype(bf16)
            other_ref[i] = dot(turned_ref[ROWS:, :], y).astype(bf16)
            own_ref[i] = dot(turned_ref[:ROWS, :], y).astype(bf16)
        put(1)
        put(0)
    for copy in stores:
        copy.wait()


def expert_call(nv, rows, up, bias, weights, small=None, sums=None):
    first = sums is None
    db = (shape((2, HALF_HID), f32), VM)
    part = shape((CHIP_ROWS, D), f32)
    back = shape((2, ROWS, D), bf16)
    plain = (db,) + ((shape((4, PIECE, D), bf16), HB),) * 6
    work = [
        pltpu.VMEM((4, HALF_HID, D), bf16),
        pltpu.VMEM((2, HALF_HID, D), f32),
        pltpu.VMEM((4, HALF_HID, D), bf16),
        pltpu.VMEM((2 * BLOCK, HALF_HID), bf16),
        pltpu.VMEM((2 * BLOCK, HALF_HID), bf16),
        pltpu.SemaphoreType.DMA((24,)),
        pltpu.SemaphoreType.DMA((12,)),
    ]
    if first:
        outs = staged_call(
            functools.partial(expert_kernel, True), "expert", [nv], [bias, small], [rows, up],
            (part, part, shape((CHIP_ROWS, D), bf16)), plain, work, 20e9, raw=weights,
        )
    else:
        outs = staged_call(
            functools.partial(expert_kernel, False), "expert", [nv], [bias], [rows, up, *sums],
            (back, back), plain, [pltpu.VMEM((CHIP_ROWS, D), f32)] * 2 + work, 20e9, raw=weights,
        )
    return outs[:-6], outs[-6:]


def post_kernel(smem, small, get, outs, put, scratch):
    mixed_ref, gh_ref, gctx_ref, dw_ref, delta_ref, small_ref = outs
    g_ref, prod_ref = scratch
    par = small[0][...].astype(f32)
    gains, bouts = par[0:2, :], par[4:6, :]
    own_ref, recv_ref, hid_ref, cot_ref, lang_ref = (get(i) for i in range(5))
    small_ref[...] = jnp.zeros_like(small_ref)
    for r in range(0, ROWS, LANES):
        rows = slice(r, r + LANES)
        lang = lang_ref[rows, 0:1]
        is_lang = lang > 0.5
        branch = own_ref[0, rows, :].astype(f32) + recv_ref[0, rows, :].astype(f32)
        branch = branch + jnp.where(is_lang, bouts[1:2, :], bouts[0:1, :])
        mixed_ref[rows, :] = (hid_ref[rows, :] + branch.astype(bf16).astype(f32)).astype(bf16)
        gn2 = own_ref[1, rows, :].astype(f32) + recv_ref[1, rows, :].astype(f32)
        xhat, rstd = norm_stats(hid_ref[rows, :].astype(bf16).astype(f32))
        gg = gn2 * jnp.where(is_lang, gains[1:2, :], gains[0:1, :])
        mean_a = jnp.mean(gg, axis=-1, keepdims=True)
        mean_b = jnp.mean(gg * xhat, axis=-1, keepdims=True)
        grad_routed = (rstd * (gg - mean_a - xhat * mean_b)).astype(bf16).astype(f32)
        cot = cot_ref[rows, :].astype(f32)
        gh = cot + grad_routed
        gh_ref[rows, :] = gh
        g_ref[rows, :] = gh.astype(bf16)
        prod = gn2 * xhat
        for i, (value, mask) in enumerate(((gh, None), (prod, 0), (prod, 1), (gn2, 0), (gn2, 1), (cot, 0), (cot, 1))):
            if mask is not None:
                value = jnp.where(is_lang, value, 0.0) if mask == 1 else jnp.where(is_lang, 0.0, value)
            small_ref[i : i + 1, :] += jnp.sum(value, axis=0, keepdims=True)
    put(0)
    put(1)
    g = g_ref[...]
    half = D // 2
    w_ref, ca_ref, cb_ref = get(5), get(6), get(7)
    dw_ref[:half, :] = dot_0(ca_ref[...], g).astype(bf16)
    dw_ref[half:, :] = dot_0(cb_ref[...], g).astype(bf16)
    put(3)
    gctx_ref[...] = dot_t(g, w_ref[...]).astype(bf16)
    put(2)
    prod_ref[:, :half] = gctx_ref[:, :half].astype(f32) * ca_ref[...].astype(f32)
    prod_ref[:, half:] = gctx_ref[:, half:].astype(f32) * cb_ref[...].astype(f32)
    head = lax.broadcasted_iota(jnp.int32, (16, D), 0)
    lane = lax.broadcasted_iota(jnp.int32, (16, D), 1)
    pick = (lane // 64 == head).astype(f32).astype(bf16)
    prod = prod_ref[...]
    upper = prod.astype(bf16)
    lower = (prod - upper.astype(f32)).astype(bf16)
    delta = dot_t(pick, upper) + dot_t(pick, lower)
    delta_ref[...] = jnp.zeros_like(delta_ref)
    for h in range(HEADS):
        delta_ref[h // 2, h % 2 : h % 2 + 1, :] = delta[h : h + 1, :]


def post_call(own, recv, hidden, cot, lang, small, weight, ctx_a, ctx_b):
    rows = shape((ROWS, D), bf16)
    outs = (rows, shape((ROWS, D), f32), rows, shape((D, D), bf16))
    plain = ((shape((PAIRS, 8, ROWS), f32), VM), (shape((8, D), f32), VM))
    work = [pltpu.VMEM((ROWS, D), bf16), pltpu.VMEM((ROWS, D), f32)]
    loads = [own, recv, hidden, cot, lang, weight, ctx_a, ctx_b]
    return staged_call(post_kernel, "post", [], [small], loads, outs, plain, work, 6e9)


def attend_back_kernel(q_ref, k_ref, v_ref, g_ref, lse_ref, delta_ref, bias_ref, dq_ref, dk_ref, dv_ref):
    q, k, v, g = q_ref[...], k_ref[...], v_ref[...], g_ref[...]
    zero = jnp.zeros_like(q)
    dq = dk = dv = 0.0
    for head in range(2):
        lanes = half_lanes(head)
        qm, km, gm = (jnp.where(lanes, x, zero) for x in (q, k, g))
        s = dot_t(k, qm) + bias_ref[...]
        p = jnp.exp(s - lse_ref[0, head : head + 1, :])
        dp = dot_t(v, gm)
        ds = (p * (dp - delta_ref[0, head : head + 1, :])).astype(bf16)
        dv = dv + dot(p.astype(bf16), gm)
        dk = dk + dot(ds, qm)
        dq = dq + dot_0(ds, km)
    dq_ref[...] = (dq * 0.125).astype(bf16)
    dk_ref[...] = dk.astype(bf16)
    dv_ref[...] = dv.astype(bf16)


def attend_back_call(triple, gctx, lse, delta, bias, first, count):
    def col(offset):
        return pl.BlockSpec((ROWS, LANES), lambda p: (0, offset + first + p))

    out = pl.BlockSpec((ROWS, LANES), lambda p: (0, p))
    return pl.pallas_call(
        attend_back_kernel,
        grid=(count,),
        out_shape=(shape((ROWS, count * LANES), bf16),) * 3,
        in_specs=[
            col(0),
            col(PAIRS),
            col(2 * PAIRS),
            col(0),
            pl.BlockSpec((1, 8, ROWS), lambda p: (p, 0, 0)),
            pl.BlockSpec((1, 8, ROWS), lambda p: (first + p, 0, 0)),
            pl.BlockSpec((ROWS, ROWS), lambda p: (0, 0)),
        ],
        out_specs=(out,) * 3,
        compiler_params=params(PLANS["attend_back"][0]),
        cost_estimate=cost(count * 2 * 5e9, count * 8e6),
        name="attend_back",
    )(triple, triple, triple, gctx, lse, delta, bias)


def final_kernel(smem, small, get, outs, put_out, scratch):
    (core_ref,), (vec_ref, sb_ref, db_ref) = smem, small
    mine_ref, theirs_ref, out_ref = outs
    gn_ref, small_ref = scratch
    core = core_ref[0]
    n1 = get(0)[...]

    def put(j, at, value):
        rows = slice(at, at + value.shape[0])

        @pl.when(core == j)
        def _():
            mine_ref[rows, :] = value

        @pl.when(core != j)
        def _():
            theirs_ref[rows, :] = value

    small_ref[...] = jnp.zeros_like(small_ref)
    for i in range(3):
        total = None
        for j in range(2):
            cols = slice(j * HALF, (j + 1) * HALF)
            piece = get(1 + 3 * j + i)[...]
            w_ref = get(7)
            at = i * D + j * HALF
            put(j, i * D, dot_0(n1, piece).astype(bf16))
            part = dot_t(piece, w_ref[:, at : at + HALF])
            total = part if total is None else total + part
            if i != 1:
                small_ref[2 + i // 2 : 3 + i // 2, cols] = jnp.sum(piece.astype(f32), axis=0, keepdims=True)
        if i == 0:
            gn_ref[...] = total
        else:
            gn_ref[...] += total
    gain = vec_ref[:D].reshape(1, D)
    tok_ref, gh_ref = get(8), get(9)
    for r in range(0, ROWS, LANES):
        rows = slice(r, r + LANES)
        xhat, rstd = norm_stats(tok_ref[rows, :].astype(f32))
        gn = gn_ref[rows, :]
        small_ref[0:1, :] += jnp.sum(gn * xhat, axis=0, keepdims=True)
        small_ref[1:2, :] += jnp.sum(gn, axis=0, keepdims=True)
        gg = gn * gain
        mean_a = jnp.mean(gg, axis=-1, keepdims=True)
        mean_b = jnp.mean(gg * xhat, axis=-1, keepdims=True)
        out_ref[rows, :] = gh_ref[rows, :] + rstd * (gg - mean_a - xhat * mean_b)
    put_out(2)
    dwo_ref = get(10)
    small_ref[8:16, :] = sb_ref[...]
    small_ref[16:24, :] = db_ref[...]
    for j in range(2):
        cols = slice(j * HALF, (j + 1) * HALF)
        put(j, 3 * D, dwo_ref[:, cols])
        put(j, 4 * D, small_ref[:, cols].astype(bf16))
    put_out(1)
    put_out(0)


def final_call(core, n1, tokens, vecs, weight, gh, dw_out, small_b, db, parts):
    half = shape((AR_ROWS, HALF), bf16)
    outs = (half, half, shape((ROWS, D), f32))
    work = [pltpu.VMEM((ROWS, D), f32), pltpu.VMEM((SMALL_ROWS, D), f32)]
    loads = [n1, *parts, weight, tokens, gh, dw_out]
    flops = 2 * 2 * 2 * ROWS * D * 3 * D
    return staged_call(final_kernel, "final", [core], [vecs, small_b, db], loads, outs, (), work, flops)


def split_kernel(order_ref, mine_ref, got_ref, *outs):
    for k in range(THIRDS):
        for i in range(4):
            rows = pl.ds(pl.multiple_of(k * 4 * AR_PIECE + order_ref[4 * k + i] * AR_PIECE, 16), AR_PIECE)
            total = mine_ref[rows, :].astype(f32) + got_ref[rows, :].astype(f32)
            outs[2 * k + i // 2][i % 2] = total.astype(bf16)


def split_call(order, mine, got):
    return pl.pallas_call(
        split_kernel,
        out_shape=(shape((2, AR_PIECE, HALF), bf16),) * 6,
        in_specs=[SM, VM, VM],
        out_specs=(VM,) * 6,
        compiler_params=params(PLANS["split"][0]),
        cost_estimate=cost(3e6, 8e6),
        name="split",
    )(order, mine, got)


def join_kernel(order_ref, *refs):
    out_ref = refs[-1]
    for k in range(THIRDS):
        for i in range(4):
            rows = pl.ds(pl.multiple_of(k * 4 * AR_PIECE + order_ref[4 * k + i] * AR_PIECE, 16), AR_PIECE)
            out_ref[rows, :] = refs[2 * k + i // 2][i % 2]


def join_call(order, pieces):
    return pl.pallas_call(
        join_kernel,
        out_shape=shape((AR_ROWS, HALF), bf16),
        in_specs=[SM] + [VM] * 6,
        out_specs=VM,
        compiler_params=params(PLANS["join"][0]),
        cost_estimate=cost(3e6, 5e6),
        name="join",
    )(order, *pieces)


def assemble_kernel(core_ref, *refs):
    ins, (qkv_ref, out_ref, small_ref) = refs[:10], refs[10:]
    zero = core_ref[0] == 0
    for i in range(5):
        mine, theirs = ins[2 * i][...].astype(f32), ins[2 * i + 1][...].astype(f32)
        for j in range(2):
            value = jnp.where(zero, mine, theirs) if j == 0 else jnp.where(zero, theirs, mine)
            cols = slice(j * HALF, (j + 1) * HALF)
            if i < 3:
                qkv_ref[:, i * D + j * HALF : i * D + (j + 1) * HALF] = value
            elif i == 3:
                out_ref[:, cols] = value
            else:
                small_ref[:, cols] = value


def assemble_call(core, mine, theirs):
    step = SMALL_ROWS
    specs, args = [], []
    for i in range(5):
        for ref in (mine, theirs):
            specs.append(pl.BlockSpec((step, HALF), (lambda r, i=i: (4 * i + r, 0)) if i < 4 else (lambda r: (16, 0))))
            args.append(ref)
    return pl.pallas_call(
        assemble_kernel,
        grid=(D // step,),
        out_shape=(shape((D, 3 * D), f32), shape((D, D), f32), shape((SMALL_ROWS, D), f32)),
        in_specs=[SM] + specs,
        out_specs=(
            pl.BlockSpec((step, 3 * D), lambda r: (r, 0)),
            pl.BlockSpec((step, D), lambda r: (r, 0)),
            pl.BlockSpec((SMALL_ROWS, D), lambda r: (0, 0)),
        ),
        compiler_params=params(PLANS["assemble"][0]),
        cost_estimate=cost(3e6, 15e6),
        name="assemble",
    )(core, *args)


AXES = ("y", "x", "z")
STRIDE = {"y": 16, "x": 4, "z": 1}
ORDERS = (("x", "y", "z"), ("y", "z", "x"), ("z", "x", "y"))
FLIPS = (1, 3)


def coordinate(index, axis):
    return (index // STRIDE[axis]) % 4


def pair_up(values, axis, step):
    pairs = []
    for dp in range(64):
        for core in range(2):
            place = coordinate(dp, axis)
            flip = FLIPS[step ^ core]
            other = dp + ((place ^ flip) - place) * STRIDE[axis]
            pairs.append((2 * dp + core, 2 * other + core))
    return lax.ppermute(values, ("dp", "expert"), pairs)


def swap_cores(values):
    return lax.ppermute(values, "expert", [(0, 1), (1, 0)])


def relative_table(dp, core):
    bits = lax.iota(jnp.int32, 64)
    flip0 = jnp.where(core == 0, FLIPS[0], FLIPS[1])
    flip1 = jnp.where(core == 0, FLIPS[1], FLIPS[0])
    tables = []
    for order in ORDERS:
        source = jnp.zeros((64,), jnp.int32)
        for i, axis in enumerate(order):
            low = (bits >> (2 * i)) & 1
            high = (bits >> (2 * i + 1)) & 1
            here = coordinate(dp, axis) ^ (low * flip0) ^ (high * flip1)
            source = source + here * STRIDE[axis]
        tables.append((source[:, None] == bits[None, :]).astype(bf16))
    return jnp.stack(tables)


def plus(left, right):
    return (left.astype(f32) + right.astype(f32)).astype(bf16)


def choose(flag, when, otherwise):
    return jnp.where(flag, when, otherwise)


def after(value, *deps):
    return lax.optimization_barrier((value, *deps))[0]


def near_sends(pieces):
    return [pair_up(pieces[k], ORDERS[k][2], 0) for k in range(3)]


def far_sends(pieces):
    return [pair_up(pieces[k], ORDERS[k][2], 1) for k in range(3)]


def gather_step(bufs, small, t, kernel):
    n = bufs[0].shape[1]
    sends = [jnp.concatenate([bufs[0].reshape(4 * n, D), small]), bufs[1], bufs[2]]
    got = [pair_up(sends[k], ORDERS[k][t // 2], t % 2) for k in range(3)]
    small, *bufs = lax.optimization_barrier((small, *bufs, kernel))[:4]
    small = small + got[0][4 * n :]
    got[0] = got[0][: 4 * n].reshape(4, n, D)
    return [jnp.concatenate([bufs[k], got[k]], axis=1) for k in range(3)], small


def reduce_pair(bufs, live, axis, step, *kernel):
    which = [k for k in range(3) if axis in ORDERS[k][:2]]
    bufs, keeps, sends = list(bufs), [], []
    for k in which:
        place = live[k].index((axis, step))
        left = len(live[k])
        live[k] = [bit for bit in live[k] if bit != (axis, step)]
        v = bufs[k].reshape(4, 2**place, 2, 2 ** (left - place - 1), 8, D)
        keeps.append(v[:, :, 0].reshape(-1, 8, D))
        sends.append(v[:, :, 1].reshape(-1, 8, D))
    got = pair_up(jnp.concatenate(sends), axis, step)
    keeps = [after(keep, *kernel) for keep in keeps]
    at = 0
    for k, keep in zip(which, keeps):
        total = keep.astype(f32) + got[at : at + keep.shape[0]].astype(f32)
        at += keep.shape[0]
        bufs[k] = (total if not live[k] else total.astype(bf16)).reshape(4, -1, 8, D)
    return bufs


def all_sum(mine, theirs, dp, core, rest, beside):
    flip0 = choose(core == 0, FLIPS[0], FLIPS[1])
    flip1 = choose(core == 0, FLIPS[1], FLIPS[0])
    order = []
    for k in range(3):
        at = coordinate(dp, ORDERS[k][0])
        order += [at, at ^ flip1, at ^ flip0, at ^ flip0 ^ flip1]
    order = jnp.stack(order).astype(jnp.int32)
    outs = split_call(order, mine, swap_cores(theirs))
    keep, send = outs[0::2], outs[1::2]
    got = [pair_up(send[k], ORDERS[k][0], 0) for k in range(3)]
    rest = beside(0, rest, *send)
    got = list(lax.optimization_barrier(tuple(got)))
    send = [plus(keep[k][1], got[k][1]) for k in range(3)]
    keep = [plus(keep[k][0], got[k][0]) for k in range(3)]
    send = [after(v, *rest) for v in send]
    got = [pair_up(send[k], ORDERS[k][0], 1) for k in range(3)]
    rest = beside(1, rest, *send)
    got = list(lax.optimization_barrier(tuple(got)))
    bufs = [after(plus(keep[k], got[k]), *rest) for k in range(3)]
    for t in range(4):
        got = [pair_up(bufs[k], ORDERS[k][1 + t // 2], t % 2) for k in range(3)]
        if t < 2:
            rest = beside(2 + t, rest, *bufs)
        got = list(lax.optimization_barrier(tuple(got)))
        bufs = [plus(bufs[k], got[k]) for k in range(3)]
        if t < 2:
            bufs = [after(v, *rest) for v in bufs]
    got = [pair_up(bufs[k], ORDERS[k][0], 1) for k in range(3)]
    got = list(lax.optimization_barrier(tuple(got)))
    bufs = [jnp.stack([bufs[k], got[k]]) for k in range(3)]
    got = [pair_up(bufs[k], ORDERS[k][0], 0) for k in range(3)]
    mine = join_call(order, [v for k in range(3) for v in (bufs[k], got[k])])
    return (*assemble_call(core.reshape(1), mine, swap_cores(mine)), rest)


def body(
    tokens,
    item_kind,
    cotangent,
    norm1_gain,
    norm1_shift,
    qkv_weight,
    query_bias,
    value_bias,
    out_weight,
    out_bias,
    norm2_gain,
    norm2_shift,
    ffn_in,
    ffn_in_bias,
    ffn_out,
    ffn_out_bias,
):
    dp = lax.axis_index("dp")
    core = lax.axis_index("expert")
    small = jnp.zeros((3, 2, 64, 12), bf16)
    mine = jnp.stack([norm2_gain, norm2_shift, ffn_out_bias]).reshape(3, 1, 1, 12)
    small = lax.dynamic_update_slice(small, mine, (0, core, dp, 0)).reshape(6, D)
    hidden_bias = lax.dynamic_update_slice(
        jnp.zeros((2, 64, 48), bf16), ffn_in_bias.reshape(1, 1, 48), (core, dp, 0)
    ).reshape(8, D)
    small = jnp.concatenate([small, hidden_bias, jnp.zeros((2, D), bf16)])

    shard = jnp.stack([ffn_in[0].T, ffn_out[0]]).reshape(2, 3, 2, 8, D)
    stay = choose(core == 0, shard[:, :, 0], shard[:, :, 1])
    leave = choose(core == 0, shard[:, :, 1], shard[:, :, 0])
    came = swap_cores(jnp.concatenate([leave.reshape(48, D), small]))
    small = small + came[48:]
    came_w = came[:48].reshape(2, 3, 8, D)
    both = choose(core == 0, jnp.stack([stay, came_w]), jnp.stack([came_w, stay]))
    bufs = [both[:, :, k].reshape(4, 8, D) for k in range(3)]

    kinds = item_kind.reshape(1, ITEMS_DEV)
    vecs = jnp.concatenate([norm1_gain, norm1_shift, query_bias, value_bias, out_bias]).astype(f32)
    n1, triple, bias, lang = qkv_call(kinds, after(tokens, came), vecs, qkv_weight)
    other_kinds = swap_cores(kinds)
    other_cot = swap_cores(cotangent)
    bufs, small = gather_step(bufs, small, 0, n1)
    ctx_a, lse_a = attend_call(after(triple, small, *bufs), bias, 0, 3)
    bufs, small = gather_step(bufs, small, 1, ctx_a)
    ctx_b, lse_b = attend_call(after(triple, small, *bufs), bias, 3, 3)
    bufs, small = gather_step(bufs, small, 2, ctx_b)
    hidden, routed = out_call(ctx_a, after(ctx_b, small, *bufs), out_weight, vecs, tokens)
    other_routed = swap_cores(routed)
    select, turned, up, nv = select_call(
        after(jnp.concatenate([kinds, other_kinds]), routed), cotangent, other_cot
    )
    bufs, small = gather_step(bufs, small, 3, up)
    near = near_sends(bufs)
    rows = sort_call(after(select, small, *bufs), routed, other_routed)
    small = small + pair_up(small, "z", 0)
    small = small + pair_up(small, "z", 1)
    near = [after(v, rows, small) for v in near]
    far = far_sends([jnp.concatenate([bufs[k], near[k]]) for k in range(3)])

    hidden_bias = small[6:14].reshape(2, 64, 3, 2, 8)
    hidden_bias = choose(core == 0, hidden_bias[:, :, :, 0], hidden_bias[:, :, :, 1])
    table = relative_table(dp, core)
    spread = jnp.einsum("kps,esku->ekpu", table, hidden_bias, preferred_element_type=f32)
    hidden_bias = spread.reshape(2, 3, 2, 2 * PIECE).transpose(2, 0, 1, 3).reshape(2, 2, HALF_HID)

    pick = lambda a, b: [v for k in range(3) for v in (a[k], b[k])]
    (branch, gn2, n2, db0), dw0 = expert_call(nv, rows, up, hidden_bias[0], pick(bufs, near), small=small)
    (back_own, back_other, db1), dw1 = expert_call(
        nv, n2, up, hidden_bias[1], far, sums=(turned, branch, gn2)
    )

    got0 = near_sends(dw0[1::2])
    back_recv = swap_cores(after(back_other, *got0))
    got = near_sends([after(v, *got0) for v in dw1[1::2]])
    mixed, gh, gctx, dw_out, delta, small_b = post_call(
        back_own, back_recv, hidden, cotangent, lang, small, out_weight, ctx_a, ctx_b
    )
    send = [plus(after(dw1[2 * k], gh), got[k]) for k in range(3)]
    got = far_sends(send)
    parts_a = attend_back_call(after(triple, *send), gctx, lse_a, delta, bias, 0, 3)
    bufs = [
        (after(dw0[2 * k], parts_a[0]).astype(f32) + got0[k].astype(f32) + got[k].astype(f32)).astype(bf16)
        for k in range(3)
    ]
    live = [[(ORDERS[k][i], t) for i in (1, 0) for t in (1, 0)] for k in range(3)]
    parts_b = attend_back_call(after(triple, *bufs), gctx, lse_b, delta, bias, 3, 3)
    bufs = reduce_pair(bufs, live, "z", 1, parts_b[0])

    db = jnp.stack([db0, db1]).reshape(2, 2, 3, 256).transpose(2, 0, 3, 1).reshape(3, 2, 32, 8, 2)
    db = db.reshape(3, 64, 8, 2).astype(bf16)
    db = jnp.einsum("kps,kpue->esku", table, db, preferred_element_type=f32)
    zero = jnp.zeros_like(db)
    db = choose(core == 0, jnp.stack([db, zero], 3), jnp.stack([zero, db], 3)).reshape(8, D)

    mine, theirs, tokens_grad = final_call(
        core.reshape(1), n1, tokens, vecs, qkv_weight, after(gh, *bufs), dw_out, small_b, db, (*parts_a, *parts_b)
    )

    bufs = reduce_pair(bufs, live, "z", 0, mine)
    theirs = after(theirs, *bufs)

    def beside(i, bufs, *round_sends):
        axis, step = (("y", 1), ("y", 0), ("x", 1), ("x", 0))[i]
        return reduce_pair([after(v, *round_sends) for v in bufs], live, axis, step)

    grad_qkv, grad_out, tail, bufs = all_sum(mine, theirs, dp, core, bufs, beside)
    shards = jnp.stack(bufs).reshape(3, 2, 2, 8, D)
    stay = choose(core == 0, shards[:, 0], shards[:, 1])
    leave = choose(core == 0, shards[:, 1], shards[:, 0])
    came = swap_cores(leave)
    full = choose(core == 0, jnp.stack([stay, came], 2), jnp.stack([came, stay], 2))
    full = full.transpose(1, 0, 2, 3, 4).reshape(2, 48, D)
    mine = lax.dynamic_slice(tail[9:15].reshape(3, 2, 64, 12), (0, core, dp, 0), (3, 1, 1, 12))
    mine = mine.reshape(3, 1, 12)
    bias_grad = lax.dynamic_slice(tail[16:24].reshape(2, 64, 48), (core, dp, 0), (1, 1, 48)).reshape(1, 48)

    return (
        mixed,
        tokens_grad,
        tail[0],
        tail[1],
        grad_qkv,
        tail[2],
        tail[3],
        grad_out,
        tail[8],
        mine[0],
        mine[1],
        full[0].T[None],
        bias_grad,
        full[1][None],
        mine[2],
    )


def solution(mesh):
    both = ("dp", "expert")
    in_specs = (
        P(both, None),
        P(both),
        P(both, None),
        P(),
        P(),
        P(),
        P(),
        P(),
        P(),
        P(),
        P("expert", "dp"),
        P("expert", "dp"),
        P("expert", None, "dp"),
        P("expert", "dp"),
        P("expert", "dp", None),
        P("expert", "dp"),
    )
    out_specs = (
        P(both, None),
        P(both, None),
        P(),
        P(),
        P(),
        P(),
        P(),
        P(),
        P(),
        P("expert", "dp"),
        P("expert", "dp"),
        P("expert", None, "dp"),
        P("expert", "dp"),
        P("expert", "dp", None),
        P("expert", "dp"),
    )
    return jax.shard_map(body, mesh=mesh, in_specs=in_specs, out_specs=out_specs, check_vma=False)
```

```python
import functools

import jax
import jax.numpy as jnp
from jax import lax
from jax.experimental import pallas as pl
from jax.experimental.pallas import tpu as pltpu
from jax.sharding import PartitionSpec as P

HEADS = 12
IMG_LEN = 197
TXT_LEN = 40
ROWS = 512
CHIP_ROWS = 1024
D = 768
FF = 3072
ITEMS_DEV = 13
PAIRS = HEADS // 2
LANES = 128
BLOCK = 256
MASKED = -1e30
EPS = 1e-5
PLANS = {
    "qkv": (20, False),
    "attend": (16, False),
    "outproj": (12, False),
    "select": (20, False),
    "sort": (12, False),
    "expert": (56, True),
    "post": (56, True),
    "attend_back": (56, False),
    "final": (56, True),
    "split": (16, False),
    "join": (12, False),
    "assemble": (24, False),
}
AR_ROWS = 3264
SMALL_ROWS = AR_ROWS - 4 * D
AR_PIECE = AR_ROWS // 12
HALF = D // 2

bf16 = jnp.bfloat16
f32 = jnp.float32


def dot(left, right):
    return jnp.dot(left, right, preferred_element_type=f32)


def dot_t(left, right):
    return lax.dot_general(left, right, (((1,), (1,)), ((), ())), preferred_element_type=f32)


def dot_0(left, right):
    return lax.dot_general(left, right, (((0,), (0,)), ((), ())), preferred_element_type=f32)


def params(mebibytes):
    return pltpu.CompilerParams(vmem_limit_bytes=mebibytes * 1024 * 1024)


def cost(flops, byts, trans=0):
    return pl.CostEstimate(flops=int(flops), bytes_accessed=int(byts), transcendentals=int(trans))


def shape(dims, dtype):
    return jax.ShapeDtypeStruct(dims, dtype)


VM = pl.BlockSpec(memory_space=pltpu.VMEM)
SM = pl.BlockSpec(memory_space=pltpu.SMEM)
HB = pl.BlockSpec(memory_space=pl.ANY)


def staged_call(
    body, name, smem, small, loads, outs, plain=(), scratch=(), flops=1e9, raw=(), cuts=None, out_cuts=None, first=()
):
    n_out = len(outs)
    limit, staged = PLANS[name]
    big = HB if staged else VM
    cuts, out_cuts = cuts or {}, out_cuts or {}

    def plain_kernel(*refs):
        at = len(smem) + len(small)
        s_refs, v_refs = refs[: len(smem)], refs[len(smem) : at]
        ins, rest = refs[at : at + len(loads)], refs[at + len(loads) :]
        results, extra = rest[: n_out + len(plain)], rest[n_out + len(plain) :]
        body(s_refs, v_refs, lambda i, c=None: ins[i], results, lambda j, c=None: None, extra)

    def part(ref, c, count, axis):
        if count == 1:
            return ref
        size = ref.shape[axis] // count
        return ref.at[(slice(None),) * axis + (pl.ds(c * size, size),)]

    def kernel(*refs):
        refs = list(refs)
        take = lambda n: [refs.pop(0) for _ in range(n)]
        s_refs, v_refs, hbm, raw_refs = take(len(smem)), take(len(small)), take(len(loads)), take(len(raw))
        out_hbm = take(n_out)
        plain_refs, bufs, out_bufs, extra = take(len(plain)), take(len(loads)), take(n_out), take(len(scratch))
        in_sem, out_sem = refs
        copies, sent = {}, []
        for i in range(len(loads)):
            count, axis = cuts.get(i, (1, 0))
            for c in range(count):
                pieces = part(hbm[i], c, count, axis), part(bufs[i], c, count, axis)
                copies[i, c] = pltpu.make_async_copy(*pieces, in_sem.at[len(copies)])
        for key in sorted(copies, key=lambda key: (key[1], key[0]) if key[0] in first else (99, key)):
            copies[key].start()

        def get(i, c=None):
            for key in [key for key in copies if key[0] == i and c in (None, key[1])]:
                copies.pop(key).wait()
            return bufs[i]

        def put(j, c=None):
            count, axis = out_cuts.get(j, (1, 0))
            for piece in range(count) if c is None else [c]:
                pieces = part(out_bufs[j], piece, count, axis), part(out_hbm[j], piece, count, axis)
                copy = pltpu.make_async_copy(*pieces, out_sem.at[len(sent)])
                copy.start()
                sent.append(copy)

        body(s_refs, v_refs, get, out_bufs + plain_refs, put, ([raw_refs] if raw else []) + extra)
        assert not copies
        for copy in sent:
            copy.wait()

    n_in = sum(cuts.get(i, (1, 0))[0] for i in range(len(loads)))
    n_sent = sum(out_cuts.get(j, (1, 0))[0] for j in range(n_out))
    bytes_moved = sum(v.size * v.dtype.itemsize for v in (*loads, *outs))
    buffers = [pltpu.VMEM(v.shape, v.dtype) for v in (*loads, *outs)] if staged else []
    sems = [pltpu.SemaphoreType.DMA((n_in,)), pltpu.SemaphoreType.DMA((max(n_sent, 1),))] if staged else []
    return pl.pallas_call(
        kernel if staged else plain_kernel,
        out_shape=(*outs, *(struct for struct, _ in plain)),
        in_specs=[SM] * len(smem) + [VM] * len(small) + [big] * len(loads) + [HB] * len(raw),
        out_specs=(big,) * n_out + tuple(spec for _, spec in plain),
        scratch_shapes=buffers + list(scratch) + sems,
        compiler_params=params(limit),
        cost_estimate=cost(flops, bytes_moved),
        name=name,
    )(*smem, *small, *loads, *raw)


def as_row(ref):
    return ref[...].astype(f32).reshape(1, D)


def norm_stats(x):
    centred = x - jnp.mean(x, axis=-1, keepdims=True)
    rstd = lax.rsqrt(jnp.mean(centred * centred, axis=-1, keepdims=True) + EPS)
    return centred * rstd, rstd


def item_lengths(kind):
    vision = jnp.where(kind == 1, 0, IMG_LEN)
    language = jnp.where(kind == 0, 0, TXT_LEN)
    return vision, language


def qkv_kernel(smem, small, get, outs, put, scratch):
    (kind_ref,) = smem
    n1_ref, tri_ref, bias_ref, lang_ref = outs
    gain, shift, q_bias, v_bias = (as_row(ref) for ref in small)
    tok_ref = get(0)
    for r in range(0, ROWS, LANES):
        xhat, _ = norm_stats(tok_ref[r : r + LANES, :].astype(f32))
        n1_ref[r : r + LANES, :] = (xhat * gain + shift).astype(bf16)
    put(0)
    n1 = n1_ref[...]
    w_ref = get(1)
    q = dot(n1, w_ref[:, 0:D]) + q_bias
    tri_ref[:, 0:D] = q.astype(bf16) * jnp.asarray(0.125, bf16)
    tri_ref[:, D : 2 * D] = dot(n1, w_ref[:, D : 2 * D]).astype(bf16)
    tri_ref[:, 2 * D :] = (dot(n1, w_ref[:, 2 * D :]) + v_bias).astype(bf16)
    put(1)
    down = lax.broadcasted_iota(jnp.int32, (ROWS, LANES), 0)
    across = lax.broadcasted_iota(jnp.int32, (8, ROWS), 1)
    item_down = jnp.zeros((ROWS, LANES), jnp.int32)
    item_across = jnp.zeros((8, ROWS), jnp.int32)
    lang = jnp.zeros((ROWS, LANES), f32)
    start = 0
    for i in range(ITEMS_DEV):
        vision, language = item_lengths(kind_ref[0, i])
        middle = start + vision
        end = middle + language
        item_down += (down >= end).astype(jnp.int32)
        item_across += (across >= end).astype(jnp.int32)
        lang = jnp.where((down >= middle) & (down < end), 1.0, lang)
        start = end
    lang_ref[...] = lang
    put(3)
    for c in range(0, ROWS, LANES):
        same = item_down == item_across[0:1, c : c + LANES]
        bias_ref[:, c : c + LANES] = jnp.where(same, 0.0, MASKED)
    put(2)


def qkv_call(kinds, tokens, vectors, weight):
    outs = (shape((ROWS, D), bf16), shape((ROWS, 3 * D), bf16), shape((ROWS, ROWS), f32), shape((ROWS, LANES), f32))
    return staged_call(qkv_kernel, "qkv", [kinds], vectors, [tokens, weight], outs, flops=2 * ROWS * D * 3 * D * 2)


def half_lanes(head):
    lane = lax.broadcasted_iota(jnp.int32, (1, LANES), 1)
    return (lane < LANES // 2) if head == 0 else (lane >= LANES // 2)


def attend_kernel(q_ref, k_ref, v_ref, bias_ref, ctx_ref, lse_ref):
    q, k, v = q_ref[...], k_ref[...], v_ref[...]
    zero = jnp.zeros_like(q)
    rows = lax.broadcasted_iota(jnp.int32, (LANES, 1), 0)
    parts = []
    for head in range(2):
        qm = jnp.where(half_lanes(head), q, zero)
        s = dot_t(k, qm) + bias_ref[...]
        top = jnp.max(s, axis=0, keepdims=True)
        e = jnp.exp(s - top)
        total = jnp.sum(e, axis=0, keepdims=True)
        lse_ref[0, head : head + 1, :] = top + jnp.log(total)
        parts.append(dot_0(v, e.astype(bf16)) * (1.0 / total))
    ctx = jnp.where(rows < LANES // 2, parts[0], parts[1])
    ctx_ref[...] = ctx.T.astype(bf16)


def attend_call(triple, bias, first, count):
    def col(offset):
        return pl.BlockSpec((ROWS, LANES), lambda p: (0, offset + first + p))

    return pl.pallas_call(
        attend_kernel,
        grid=(count,),
        out_shape=(shape((ROWS, count * LANES), bf16), shape((count, 8, ROWS), f32)),
        in_specs=[col(0), col(PAIRS), col(2 * PAIRS), pl.BlockSpec((ROWS, ROWS), lambda p: (0, 0))],
        out_specs=(
            pl.BlockSpec((ROWS, LANES), lambda p: (0, p)),
            pl.BlockSpec((1, 8, ROWS), lambda p: (p, 0, 0)),
        ),
        compiler_params=params(PLANS["attend"][0]),
        cost_estimate=cost(count * 2 * 4e9, count * 6e6),
        name="attend",
    )(triple, triple, triple, bias)


def out_kernel(smem, small, get, outs, put, scratch):
    hid_ref, routed_ref = outs
    half = D // 2
    ca_ref, cb_ref, w_ref = get(0), get(1), get(2)
    h = dot(ca_ref[...], w_ref[:half, :]) + dot(cb_ref[...], w_ref[half:, :])
    h = get(3)[...].astype(f32) + h + as_row(small[0])
    routed_ref[...] = h.astype(bf16)
    put(1)
    hid_ref[...] = h
    put(0)


def out_call(ctx_a, ctx_b, weight, bias, tokens):
    outs = (shape((ROWS, D), f32), shape((ROWS, D), bf16))
    return staged_call(
        out_kernel, "outproj", [], [bias], [ctx_a, ctx_b, weight, tokens], outs, flops=2 * ROWS * D * D * 2
    )


def select_kernel(smem, small, get, outs, put, scratch):
    (kind_ref,) = smem
    sel_ref, turned_ref, up_ref, nv_ref = outs
    spans = []
    vision_total = 0
    for pack in range(2):
        start = 0
        for i in range(ITEMS_DEV):
            vision, language = item_lengths(kind_ref[pack, i])
            first = jnp.minimum(start, ROWS)
            middle = jnp.minimum(start + vision, ROWS)
            end = jnp.minimum(start + vision + language, ROWS)
            spans.append((pack, first, middle, end))
            vision_total = vision_total + middle - first
            start = start + vision + language
    nv_ref[0] = vision_total
    place = lax.broadcasted_iota(jnp.int32, (1, ROWS), 1)
    target = [jnp.zeros((1, ROWS), jnp.int32) for _ in range(2)]
    at_vision, at_language = 0, vision_total
    for pack, first, middle, end in spans:
        t = target[pack]
        t = jnp.where((place >= first) & (place < middle), place + (at_vision - first), t)
        t = jnp.where((place >= middle) & (place < end), place + (at_language - middle), t)
        target[pack] = t
        at_vision = at_vision + middle - first
        at_language = at_language + end - middle
    own, other = get(0)[...], get(1)[...]
    for r in range(0, CHIP_ROWS, BLOCK):
        down = lax.broadcasted_iota(jnp.int32, (BLOCK, ROWS), 0) + r
        for pack in range(2):
            sel_ref[r : r + BLOCK, pack * ROWS : (pack + 1) * ROWS] = (
                (down == target[pack]).astype(f32).astype(bf16)
            )
        turned_ref[:, r : r + BLOCK] = sel_ref[r : r + BLOCK, :].T
        up_ref[r : r + BLOCK, :] = (
            dot(sel_ref[r : r + BLOCK, :ROWS], own) + dot(sel_ref[r : r + BLOCK, ROWS:], other)
        ).astype(bf16)
    for j in range(3):
        put(j)


def select_call(kinds, own, other):
    square = shape((CHIP_ROWS, CHIP_ROWS), bf16)
    outs = (square, square, shape((CHIP_ROWS, D), bf16))
    plain = ((shape((1,), jnp.int32), SM),)
    flops = 2 * 2 * CHIP_ROWS * CHIP_ROWS * D
    return staged_call(select_kernel, "select", [kinds], [], [own, other], outs, plain, flops=flops)


def sort_kernel(smem, small, get, outs, put, scratch):
    sel_ref = get(0)
    own, other = get(1)[...], get(2)[...]
    for r in range(0, CHIP_ROWS, BLOCK):
        x = dot(sel_ref[r : r + BLOCK, :ROWS], own) + dot(sel_ref[r : r + BLOCK, ROWS:], other)
        outs[0][r : r + BLOCK, :] = x.astype(bf16)
    put(0)


def sort_call(select, own, other):
    return staged_call(
        sort_kernel,
        "sort",
        [],
        [],
        [select, own, other],
        (shape((CHIP_ROWS, D), bf16),),
        flops=2 * CHIP_ROWS * CHIP_ROWS * D,
    )[0]


def gelu_parts(x):
    z = jnp.abs(x) * 0.7071067811865476
    t = 1.0 / (1.0 + 0.3275911 * z)
    poly = t * (
        0.254829592 + t * (-0.284496736 + t * (1.421413741 + t * (-1.453152027 + t * 1.061405429)))
    )
    bell = jnp.exp(x * x * -0.5)
    tail = 0.5 * poly * bell
    phi = jnp.where(x >= 0, 1.0 - tail, tail)
    return x * phi, phi + x * bell * 0.3989422804014327


THIRDS = 3
PIECE = 128
HALF_HID = THIRDS * 2 * PIECE


def expert_kernel(first, smem, small, get, outs, put, scratch):
    (nv_ref,), bias_ref = smem, small[0]
    w_hbm, scratch = scratch[0], scratch[1:]
    if first:
        n2_ref, *sums_hbm, db_ref = outs[:4]
        dw_hbm = outs[4:]
    else:
        own_ref, other_ref, db_ref = outs[:3]
        dw_hbm = outs[3:]
    branch_ref, gn2_ref, sum_sem, scratch = scratch[0], scratch[1], scratch[2], scratch[3:]
    w_ref, acc_ref, out_ref, act_ref, gp_ref, in_sem, out_sem = scratch
    loads = []
    for k in range(THIRDS):
        for j in range(2):
            at = k * 2 * PIECE + j * PIECE
            ref = w_hbm[2 * k + j if first else k]
            for m in range(4):
                block = m if first else 4 * j + m
                part = ref.at[block] if len(ref.shape) == 3 else ref.at[pl.ds(block * PIECE, PIECE), :]
                copy = pltpu.make_async_copy(
                    part, w_ref.at[m, pl.ds(at, PIECE), :], in_sem.at[8 * k + 4 * j + m]
                )
                copy.start()
                loads.append(copy)
    branch_ref[...] = jnp.zeros_like(branch_ref)
    gn2_ref[...] = jnp.zeros_like(gn2_ref)
    x_ref = get(0)
    if first:
        par = small[1][...].astype(f32)
        for r in range(0, CHIP_ROWS, LANES):
            xhat, _ = norm_stats(x_ref[r : r + LANES, :].astype(f32))
            vision = (lax.broadcasted_iota(jnp.int32, (LANES, 1), 0) + r) < nv_ref[0]
            gain = jnp.where(vision, par[0:1, :], par[1:2, :])
            shift = jnp.where(vision, par[2:3, :], par[3:4, :])
            n2_ref[r : r + LANES, :] = (xhat * gain + shift).astype(bf16)
        put(0)
    else:
        n2_ref = x_ref
    up_ref = get(1)
    db_ref[...] = jnp.zeros_like(db_ref)
    for copy in loads:
        copy.wait()
    nv = nv_ref[0]
    stores = []
    for e in range(2):
        low = jnp.int32(0) if e == 0 else nv // BLOCK
        high = (nv + BLOCK - 1) // BLOCK if e == 0 else jnp.int32(CHIP_ROWS // BLOCK)
        acc_ref[...] = jnp.zeros_like(acc_ref)

        def visit(block, size, e=e):
            at = pl.multiple_of(block * BLOCK, BLOCK)
            rows = pl.ds(at, size)
            index = lax.broadcasted_iota(jnp.int32, (size, 1), 0) + at
            valid = (index < nv) if e == 0 else (index >= nv)
            n2 = n2_ref[rows, :]
            up = up_ref[rows, :]
            for k in range(THIRDS):
                hid = slice(k * BLOCK, (k + 1) * BLOCK)
                pre = dot_t(n2, w_ref[2 * e, hid, :]) + bias_ref[e : e + 1, hid].astype(f32)
                back = dot_t(up, w_ref[2 * e + 1, hid, :])
                active, slope = gelu_parts(pre)
                act = jnp.where(valid, active, 0.0).astype(bf16)
                gp = jnp.where(valid, back * slope, 0.0).astype(bf16)
                act_ref[:size, hid] = act
                gp_ref[:size, hid] = gp
                db_ref[e : e + 1, hid] += jnp.sum(gp.astype(f32), axis=0, keepdims=True)
            acc_ref[0] += dot_0(gp_ref[:size, :], n2)
            acc_ref[1] += dot_0(act_ref[:size, :], up)
            branch_ref[rows, :] += dot(act_ref[:size, :], w_ref[2 * e + 1])
            gn2_ref[rows, :] += dot(gp_ref[:size, :], w_ref[2 * e])
            if not first:
                return
            for b in range(size // BLOCK):
                done = pl.ds(pl.multiple_of(at + b * BLOCK, BLOCK), BLOCK)

                @pl.when((at + (b + 1) * BLOCK <= nv) if e == 0 else (at >= 0))
                def _(done=done):
                    for i, ref in enumerate((branch_ref, gn2_ref)):
                        pltpu.make_async_copy(ref.at[done, :], sums_hbm[i].at[done, :], sum_sem.at[i]).start()

        count = high - low

        def two(i, carry, visit=visit, low=low):
            visit(low + 2 * i, 2 * BLOCK)
            return carry

        lax.fori_loop(0, count // 2, two, 0)

        @pl.when(count % 2 == 1)
        def _(visit=visit, high=high):
            visit(high - 1, BLOCK)

        out_ref[2 * e] = acc_ref[0].astype(bf16)
        out_ref[2 * e + 1] = acc_ref[1].astype(bf16)
        for k in range(THIRDS):
            for j in range(2):
                at = k * 2 * PIECE + j * PIECE
                copy = pltpu.make_async_copy(
                    out_ref.at[pl.ds(2 * e, 2), pl.ds(at, PIECE), :],
                    dw_hbm[2 * k + j].at[pl.ds(2 * e, 2)],
                    out_sem.at[6 * e + 2 * k + j],
                )
                copy.start()
                stores.append(copy)
    if first:
        for i, ref in enumerate((branch_ref, gn2_ref)):
            pltpu.make_async_copy(ref, sums_hbm[i], sum_sem.at[i]).wait()
    else:
        turned_ref = get(2)
        for i, total in enumerate((branch_ref, gn2_ref)):
            y = (get(3 + i)[...] + total[...]).astype(bf16)
            other_ref[i] = dot(turned_ref[ROWS:, :], y).astype(bf16)
            own_ref[i] = dot(turned_ref[:ROWS, :], y).astype(bf16)
        put(1)
        put(0)
    for copy in stores:
        copy.wait()


def expert_call(nv, rows, up, bias, weights, small=None, sums=None):
    first = sums is None
    db = (shape((2, HALF_HID), f32), VM)
    part = shape((CHIP_ROWS, D), f32)
    back = shape((2, ROWS, D), bf16)
    pieces = ((shape((4, PIECE, D), bf16), HB),) * 6
    work = [
        pltpu.VMEM((CHIP_ROWS, D), f32),
        pltpu.VMEM((CHIP_ROWS, D), f32),
        pltpu.SemaphoreType.DMA((2,)),
        pltpu.VMEM((4, HALF_HID, D), bf16),
        pltpu.VMEM((2, HALF_HID, D), f32),
        pltpu.VMEM((4, HALF_HID, D), bf16),
        pltpu.VMEM((2 * BLOCK, HALF_HID), bf16),
        pltpu.VMEM((2 * BLOCK, HALF_HID), bf16),
        pltpu.SemaphoreType.DMA((24,)),
        pltpu.SemaphoreType.DMA((12,)),
    ]
    if first:
        outs = staged_call(
            functools.partial(expert_kernel, True), "expert", [nv], [bias, small], [rows, up],
            (shape((CHIP_ROWS, D), bf16),), ((part, HB), (part, HB), db, *pieces), work, 20e9, raw=weights,
        )
    else:
        outs = staged_call(
            functools.partial(expert_kernel, False), "expert", [nv], [bias], [rows, up, *sums],
            (back, back), (db, *pieces), work, 20e9, raw=weights,
        )
    return outs[:-6], outs[-6:]


def post_kernel(smem, small, get, outs, put, scratch):
    mixed_ref, gh_ref, gctx_ref, dw_ref, delta_ref, small_ref = outs
    g_ref, prod_ref = scratch
    par = small[0][...].astype(f32)
    gains, bouts = par[0:2, :], par[4:6, :]
    small_ref[...] = jnp.zeros_like(small_ref)
    for r in range(0, ROWS, LANES):
        rows = slice(r, r + LANES)
        own_ref, recv_ref, hid_ref, cot_ref, lang_ref = (get(i, r // LANES) for i in range(5))
        lang = lang_ref[rows, 0:1]
        is_lang = lang > 0.5
        branch = own_ref[0, rows, :].astype(f32) + recv_ref[0, rows, :].astype(f32)
        branch = branch + jnp.where(is_lang, bouts[1:2, :], bouts[0:1, :])
        mixed_ref[rows, :] = (hid_ref[rows, :] + branch.astype(bf16).astype(f32)).astype(bf16)
        gn2 = own_ref[1, rows, :].astype(f32) + recv_ref[1, rows, :].astype(f32)
        xhat, rstd = norm_stats(hid_ref[rows, :].astype(bf16).astype(f32))
        gg = gn2 * jnp.where(is_lang, gains[1:2, :], gains[0:1, :])
        mean_a = jnp.mean(gg, axis=-1, keepdims=True)
        mean_b = jnp.mean(gg * xhat, axis=-1, keepdims=True)
        grad_routed = (rstd * (gg - mean_a - xhat * mean_b)).astype(bf16).astype(f32)
        cot = cot_ref[rows, :].astype(f32)
        gh = cot + grad_routed
        gh_ref[rows, :] = gh
        put(0, r // LANES)
        put(1, r // LANES)
        g_ref[rows, :] = gh.astype(bf16)
        prod = gn2 * xhat
        for i, (value, mask) in enumerate(((gh, None), (prod, 0), (prod, 1), (gn2, 0), (gn2, 1), (cot, 0), (cot, 1))):
            if mask is not None:
                value = jnp.where(is_lang, value, 0.0) if mask == 1 else jnp.where(is_lang, 0.0, value)
            small_ref[i : i + 1, :] += jnp.sum(value, axis=0, keepdims=True)
    g = g_ref[...]
    half = D // 2
    w_ref, ca_ref, cb_ref = get(5), get(6), get(7)
    dw_ref[:half, :] = dot_0(ca_ref[...], g).astype(bf16)
    dw_ref[half:, :] = dot_0(cb_ref[...], g).astype(bf16)
    put(3)
    gctx_ref[...] = dot_t(g, w_ref[...]).astype(bf16)
    put(2)
    prod_ref[:, :half] = gctx_ref[:, :half].astype(f32) * ca_ref[...].astype(f32)
    prod_ref[:, half:] = gctx_ref[:, half:].astype(f32) * cb_ref[...].astype(f32)
    head = lax.broadcasted_iota(jnp.int32, (16, D), 0)
    lane = lax.broadcasted_iota(jnp.int32, (16, D), 1)
    pick = (lane // 64 == head).astype(f32).astype(bf16)
    prod = prod_ref[...]
    upper = prod.astype(bf16)
    lower = (prod - upper.astype(f32)).astype(bf16)
    delta = dot_t(pick, upper) + dot_t(pick, lower)
    delta_ref[...] = jnp.zeros_like(delta_ref)
    for h in range(HEADS):
        delta_ref[h // 2, h % 2 : h % 2 + 1, :] = delta[h : h + 1, :]


def post_call(own, recv, hidden, cot, lang, small, weight, ctx_a, ctx_b):
    rows = shape((ROWS, D), bf16)
    outs = (rows, shape((ROWS, D), f32), rows, shape((D, D), bf16))
    plain = ((shape((PAIRS, 8, ROWS), f32), VM), (shape((8, D), f32), VM))
    work = [pltpu.VMEM((ROWS, D), bf16), pltpu.VMEM((ROWS, D), f32)]
    loads = [own, recv, hidden, cot, lang, weight, ctx_a, ctx_b]
    cuts = {0: (4, 1), 1: (4, 1), 2: (4, 0), 3: (4, 0), 4: (4, 0)}
    return staged_call(
        post_kernel, "post", [], [small], loads, outs, plain, work, 6e9,
        cuts=cuts, out_cuts={0: (4, 0), 1: (4, 0)}, first=range(5),
    )


def attend_back_kernel(q_ref, k_ref, v_ref, g_ref, lse_a, lse_b, delta_ref, bias_ref, dq_ref, dk_ref, dv_ref):
    q, k, v, g = q_ref[...], k_ref[...], v_ref[...], g_ref[...]
    zero = jnp.zeros_like(q)
    lse = jnp.where(pl.program_id(0) < PAIRS // 2, lse_a[0], lse_b[0])
    dq = dk = dv = 0.0
    for head in range(2):
        lanes = half_lanes(head)
        qm, km, gm = (jnp.where(lanes, x, zero) for x in (q, k, g))
        s = dot_t(k, qm) + bias_ref[...]
        p = jnp.exp(s - lse[head : head + 1, :])
        dp = dot_t(v, gm)
        ds = (p * (dp - delta_ref[0, head : head + 1, :])).astype(bf16)
        dv = dv + dot(p.astype(bf16), gm)
        dk = dk + dot(ds, qm)
        dq = dq + dot_0(ds, km)
    dq_ref[...] = (dq * 0.125).astype(bf16)
    dk_ref[...] = dk.astype(bf16)
    dv_ref[...] = dv.astype(bf16)


def attend_back_call(triple, gctx, lse_a, lse_b, delta, bias):
    def col(offset):
        return pl.BlockSpec((ROWS, LANES), lambda p: (0, offset + p))

    half = PAIRS // 2
    return pl.pallas_call(
        attend_back_kernel,
        grid=(PAIRS,),
        out_shape=(shape((ROWS, D), bf16),) * 3,
        in_specs=[
            col(0),
            col(PAIRS),
            col(2 * PAIRS),
            col(0),
            pl.BlockSpec((1, 8, ROWS), lambda p: (jnp.minimum(p, half - 1), 0, 0)),
            pl.BlockSpec((1, 8, ROWS), lambda p: (jnp.maximum(p - half, 0), 0, 0)),
            pl.BlockSpec((1, 8, ROWS), lambda p: (p, 0, 0)),
            pl.BlockSpec((ROWS, ROWS), lambda p: (0, 0)),
        ],
        out_specs=(col(0),) * 3,
        compiler_params=params(PLANS["attend_back"][0]),
        cost_estimate=cost(20e9, 10e6),
        name="attend_back",
    )(triple, triple, triple, gctx, lse_a, lse_b, delta, bias)


def final_kernel(smem, small, get, outs, put, scratch):
    (core_ref,), (gain_ref, sb_ref, db_ref) = smem, small
    out_ref, *targets = outs
    gn_ref, small_ref, buf_ref, rows_ref, sem = scratch
    core = core_ref[0]
    lanes = [pl.ds(pl.multiple_of(h * HALF, LANES), HALF) for h in (core, 1 - core)]
    sent = []

    def send(source, t, at, size):
        copy = pltpu.make_async_copy(source, targets[t].at[pl.ds(at, size), :], sem.at[len(sent)])
        copy.start()
        sent.append(copy)

    small_ref[...] = jnp.zeros_like(small_ref)
    n1 = get(0)[...]
    for t in (1, 0):
        for i in range(3):
            buf_ref[t, i * D : (i + 1) * D, :] = dot_0(n1, get(1 + i)[:, lanes[t]]).astype(bf16)
            send(buf_ref.at[t, pl.ds(i * D, D), :], t, i * D, D)
        if t == 0:
            break
        for i in range(3):
            piece = get(1 + i)[...]
            part = dot_t(piece, get(4)[:, i * D : (i + 1) * D])
            if i == 0:
                gn_ref[...] = part
            else:
                gn_ref[...] += part
            if i != 1:
                small_ref[2 + i // 2 : 3 + i // 2, :] = jnp.sum(piece.astype(f32), axis=0, keepdims=True)
    gain = as_row(gain_ref)
    for r in range(0, ROWS, LANES):
        rows = slice(r, r + LANES)
        tok_ref, gh_ref = get(5, r // LANES), get(6, r // LANES)
        xhat, rstd = norm_stats(tok_ref[rows, :].astype(f32))
        gn = gn_ref[rows, :]
        small_ref[0:1, :] += jnp.sum(gn * xhat, axis=0, keepdims=True)
        small_ref[1:2, :] += jnp.sum(gn, axis=0, keepdims=True)
        gg = gn * gain
        mean_a = jnp.mean(gg, axis=-1, keepdims=True)
        mean_b = jnp.mean(gg * xhat, axis=-1, keepdims=True)
        out_ref[rows, :] = gh_ref[rows, :] + rstd * (gg - mean_a - xhat * mean_b)
        put(0, r // LANES)
    small_ref[8:16, :] = sb_ref[...]
    small_ref[16:24, :] = db_ref[...]
    for t in (1, 0):
        rows_ref[t] = small_ref[:, lanes[t]].astype(bf16)
        send(rows_ref.at[t], t, 4 * D, SMALL_ROWS)
    for t in (1, 0):
        buf_ref[t, 3 * D : 4 * D, :] = get(7)[:, lanes[t]]
        send(buf_ref.at[t, pl.ds(3 * D, D), :], t, 3 * D, D)
    for copy in sent:
        copy.wait()


def final_call(core, n1, tokens, gain, weight, gh, dw_out, small_b, db, parts):
    half = shape((AR_ROWS, HALF), bf16)
    work = [
        pltpu.VMEM((ROWS, D), f32),
        pltpu.VMEM((SMALL_ROWS, D), f32),
        pltpu.VMEM((2, 4 * D, HALF), bf16),
        pltpu.VMEM((2, SMALL_ROWS, HALF), bf16),
        pltpu.SemaphoreType.DMA((10,)),
    ]
    loads = [n1, *parts, weight, tokens, gh, dw_out]
    out, mine, theirs = staged_call(
        final_kernel, "final", [core], [gain, small_b, db], loads, (shape((ROWS, D), f32),),
        ((half, HB), (half, HB)), work, 2 * 2 * 2 * ROWS * D * 3 * D,
        cuts={5: (4, 0), 6: (4, 0)}, out_cuts={0: (4, 0)},
    )
    return mine, theirs, out


def split_kernel(order_ref, mine_ref, got_ref, *outs):
    for k in range(THIRDS):
        for i in range(4):
            rows = pl.ds(pl.multiple_of(k * 4 * AR_PIECE + order_ref[4 * k + i] * AR_PIECE, 16), AR_PIECE)
            total = mine_ref[rows, :].astype(f32) + got_ref[rows, :].astype(f32)
            outs[2 * k + i // 2][i % 2] = total.astype(bf16)


def split_call(order, mine, got):
    return pl.pallas_call(
        split_kernel,
        out_shape=(shape((2, AR_PIECE, HALF), bf16),) * 6,
        in_specs=[SM, VM, VM],
        out_specs=(VM,) * 6,
        compiler_params=params(PLANS["split"][0]),
        cost_estimate=cost(3e6, 8e6),
        name="split",
    )(order, mine, got)


def join_kernel(order_ref, *refs):
    out_ref = refs[-1]
    for k in range(THIRDS):
        for i in range(4):
            rows = pl.ds(pl.multiple_of(k * 4 * AR_PIECE + order_ref[4 * k + i] * AR_PIECE, 16), AR_PIECE)
            out_ref[rows, :] = refs[2 * k + i // 2][i % 2]


def join_call(order, pieces):
    return pl.pallas_call(
        join_kernel,
        out_shape=shape((AR_ROWS, HALF), bf16),
        in_specs=[SM] + [VM] * 6,
        out_specs=VM,
        compiler_params=params(PLANS["join"][0]),
        cost_estimate=cost(3e6, 5e6),
        name="join",
    )(order, *pieces)


def assemble_kernel(place_ref, *refs):
    ins, (qkv_ref, out_ref), vectors, shards, bias_ref = refs[:10], refs[10:12], refs[12:17], refs[17:20], refs[20]
    core, dp = place_ref[0], place_ref[1]
    zero = core == 0

    def halves(i):
        mine, theirs = ins[2 * i][...].astype(f32), ins[2 * i + 1][...].astype(f32)
        return jnp.where(zero, mine, theirs), jnp.where(zero, theirs, mine)

    for i in range(4):
        for j, value in enumerate(halves(i)):
            if i < 3:
                qkv_ref[:, i * D + j * HALF : i * D + (j + 1) * HALF] = value
            else:
                out_ref[:, j * HALF : (j + 1) * HALF] = value

    @pl.when(pl.program_id(0) == 0)
    def _():
        rows = jnp.concatenate([value[:24, :] for value in halves(4)], axis=1)
        for ref, r in zip(vectors, (0, 1, 2, 3, 8)):
            ref[...] = rows[r : r + 1, :].reshape(D)
        down = lax.broadcasted_iota(jnp.int32, (D, LANES), 0)
        lane = lax.broadcasted_iota(jnp.int32, (D, LANES), 1)

        def pick(offset):
            return dot(rows.astype(bf16), (down - offset == lane).astype(f32).astype(bf16))

        norms = pick(12 * dp)
        for i, ref in enumerate(shards):
            both = norms[9 + 2 * i : 11 + 2 * i, :12]
            ref[...] = jnp.where(zero, both[0:1, :], both[1:2, :])
        biases = pick(48 * (dp % 16))
        at = lax.broadcasted_iota(jnp.int32, (24, LANES), 0)
        here = jnp.where(at == 16 + 4 * core + dp // 16, biases, 0.0)
        bias_ref[...] = jnp.sum(here, axis=0, keepdims=True)[:, :48]


def assemble_call(place, mine, theirs):
    step = SMALL_ROWS
    specs, args = [], []
    for i in range(5):
        for ref in (mine, theirs):
            specs.append(pl.BlockSpec((step, HALF), (lambda r, i=i: (4 * i + r, 0)) if i < 4 else (lambda r: (16, 0))))
            args.append(ref)
    outs = pl.pallas_call(
        assemble_kernel,
        grid=(D // step,),
        out_shape=(shape((D, 3 * D), f32), shape((D, D), f32))
        + (shape((D,), f32),) * 5
        + (shape((1, 12), f32),) * 3
        + (shape((1, 48), f32),),
        in_specs=[SM] + specs,
        out_specs=(
            pl.BlockSpec((step, 3 * D), lambda r: (r, 0)),
            pl.BlockSpec((step, D), lambda r: (r, 0)),
        )
        + (VM,) * 9,
        compiler_params=params(PLANS["assemble"][0]),
        cost_estimate=cost(3e6, 15e6),
        name="assemble",
    )(place, *args)
    return outs[0], outs[1], outs[2:7], outs[7:10], outs[10]


AXES = ("y", "x", "z")
STRIDE = {"y": 16, "x": 4, "z": 1}
ORDERS = (("x", "y", "z"), ("y", "z", "x"), ("z", "x", "y"))
FLIPS = (1, 3)


def coordinate(index, axis):
    return (index // STRIDE[axis]) % 4


def pair_up(values, axis, step):
    pairs = []
    for dp in range(64):
        for core in range(2):
            place = coordinate(dp, axis)
            flip = FLIPS[step ^ core]
            other = dp + ((place ^ flip) - place) * STRIDE[axis]
            pairs.append((2 * dp + core, 2 * other + core))
    return lax.ppermute(values, ("dp", "expert"), pairs)


def swap_cores(values):
    return lax.ppermute(values, "expert", [(0, 1), (1, 0)])


def relative_table(dp, core):
    bits = lax.iota(jnp.int32, 64)
    flip0 = jnp.where(core == 0, FLIPS[0], FLIPS[1])
    flip1 = jnp.where(core == 0, FLIPS[1], FLIPS[0])
    tables = []
    for order in ORDERS:
        source = jnp.zeros((64,), jnp.int32)
        for i, axis in enumerate(order):
            low = (bits >> (2 * i)) & 1
            high = (bits >> (2 * i + 1)) & 1
            here = coordinate(dp, axis) ^ (low * flip0) ^ (high * flip1)
            source = source + here * STRIDE[axis]
        tables.append((source[:, None] == bits[None, :]).astype(bf16))
    return jnp.stack(tables)


def plus(left, right):
    return (left.astype(f32) + right.astype(f32)).astype(bf16)


def choose(flag, when, otherwise):
    return jnp.where(flag, when, otherwise)


def tie(values, deps):
    flat = lax.optimization_barrier((*values, *deps))
    return list(flat[: len(values)]), list(flat[len(values) :])


def near_sends(pieces):
    return [pair_up(pieces[k], ORDERS[k][2], 0) for k in range(3)]


def far_sends(pieces):
    return [pair_up(pieces[k], ORDERS[k][2], 1) for k in range(3)]


def gather_step(bufs, small, t, kernel):
    n = bufs[0].shape[1]
    sends = [jnp.concatenate([bufs[0].reshape(4 * n, D), small]), bufs[1], bufs[2]]
    got = [pair_up(sends[k], ORDERS[k][t // 2], t % 2) for k in range(3)]
    (small, *bufs), (kernel,) = tie([small, *bufs], [kernel])
    small = small + got[0][4 * n :]
    got[0] = got[0][: 4 * n].reshape(4, n, D)
    return [jnp.concatenate([bufs[k], got[k]], axis=1) for k in range(3)], small, kernel


def reduce_parts(bufs, live, axis, step):
    which = [k for k in range(3) if axis in ORDERS[k][:2]]
    keeps, sends = [], []
    for k in which:
        place = live[k].index((axis, step))
        left = len(live[k])
        live[k] = [bit for bit in live[k] if bit != (axis, step)]
        v = bufs[k].reshape(4, 2**place, 2, 2 ** (left - place - 1), 8, D)
        keeps.append(v[:, :, 0].reshape(-1, 8, D))
        sends.append(v[:, :, 1].reshape(-1, 8, D))
    return which, keeps, jnp.concatenate(sends)


def reduce_sums(bufs, live, which, keeps, got):
    bufs = list(bufs)
    at = 0
    for k, keep in zip(which, keeps):
        total = keep.astype(f32) + got[at : at + keep.shape[0]].astype(f32)
        at += keep.shape[0]
        bufs[k] = (total if not live[k] else total.astype(bf16)).reshape(4, -1, 8, D)
    return bufs


def all_sum(mine, theirs, dp, core, rest, live):
    flip0 = choose(core == 0, FLIPS[0], FLIPS[1])
    flip1 = choose(core == 0, FLIPS[1], FLIPS[0])
    order = []
    for k in range(3):
        at = coordinate(dp, ORDERS[k][0])
        order += [at, at ^ flip1, at ^ flip0, at ^ flip0 ^ flip1]
    order = jnp.stack(order).astype(jnp.int32)
    outs = split_call(order, mine, swap_cores(theirs))
    keep, bufs = list(outs[0::2]), list(outs[1::2])
    first = [None] * 3
    steps = [("z", 0), ("y", 1), ("y", 0), ("x", 1), ("x", 0)]
    for t in range(8):
        axes = [ORDERS[k][(0, 0, 1, 1, 2, 2, 0, 0)[t]] for k in range(3)]
        got = [pair_up(bufs[k], axes[k], (0, 1, 0, 1, 0, 1, 1, 0)[t]) for k in range(3)]
        if t < len(steps):
            which, kept, sent = reduce_parts(rest, live, *steps[t])
            back = pair_up(sent, *steps[t])
        if t == 7:
            break
        for k in range(3):
            own = keep if t < 2 else bufs
            if t == 0 and k == 0:
                pass
            elif k == 0:
                if t <= len(steps):
                    j = last[0]
                    (own[0],), (rest[j],) = tie([own[0]], [rest[j]])
                else:
                    (own[0],), (bufs[2],) = tie([own[0]], [bufs[2]])
            else:
                (own[k],), (bufs[k - 1],) = tie([own[k]], [bufs[k - 1]])
            if t == 0:
                first[k] = got[k]
                bufs[k] = plus(keep[k][1], got[k][1])
            elif t == 1:
                total = keep[k][0].astype(f32) + first[k][0].astype(f32) + got[k].astype(f32)
                bufs[k] = total.astype(bf16)
            elif t < 6:
                bufs[k] = plus(bufs[k], got[k])
            else:
                bufs[k] = jnp.stack([bufs[k], got[k]])
        if t < len(steps):
            (back,), (bufs[2],) = tie([back], [bufs[2]])
            rest = reduce_sums(rest, live, which, kept, back)
            last = which
    mine = join_call(order, [v for k in range(3) for v in (bufs[k], got[k])])
    return (*assemble_call(jnp.stack([core, dp]).astype(jnp.int32), mine, swap_cores(mine)), rest)


def body(
    tokens,
    item_kind,
    cotangent,
    norm1_gain,
    norm1_shift,
    qkv_weight,
    query_bias,
    value_bias,
    out_weight,
    out_bias,
    norm2_gain,
    norm2_shift,
    ffn_in,
    ffn_in_bias,
    ffn_out,
    ffn_out_bias,
):
    dp = lax.axis_index("dp")
    core = lax.axis_index("expert")
    small = jnp.zeros((3, 2, 64, 12), bf16)
    mine = jnp.stack([norm2_gain, norm2_shift, ffn_out_bias]).reshape(3, 1, 1, 12)
    small = lax.dynamic_update_slice(small, mine, (0, core, dp, 0)).reshape(6, D)
    hidden_bias = lax.dynamic_update_slice(
        jnp.zeros((2, 64, 48), bf16), ffn_in_bias.reshape(1, 1, 48), (core, dp, 0)
    ).reshape(8, D)
    small = jnp.concatenate([small, hidden_bias, jnp.zeros((2, D), bf16)])

    shard = jnp.stack([ffn_in[0].T, ffn_out[0]]).reshape(2, 3, 2, 8, D)
    stay = choose(core == 0, shard[:, :, 0], shard[:, :, 1])
    leave = choose(core == 0, shard[:, :, 1], shard[:, :, 0])
    came = swap_cores(jnp.concatenate([leave.reshape(48, D), small]))
    kinds = item_kind.reshape(1, ITEMS_DEV)
    vectors = [norm1_gain, norm1_shift, query_bias, value_bias]
    (tokens,), (came,) = tie([tokens], [came])
    small = small + came[48:]
    came_w = came[:48].reshape(2, 3, 8, D)
    both = choose(core == 0, jnp.stack([stay, came_w]), jnp.stack([came_w, stay]))
    bufs = [both[:, :, k].reshape(4, 8, D) for k in range(3)]
    n1, triple, bias, lang = qkv_call(kinds, tokens, vectors, qkv_weight)
    other_kinds = swap_cores(kinds)
    other_cot = swap_cores(cotangent)
    bufs, small, n1 = gather_step(bufs, small, 0, n1)
    (triple,), bufs = tie([triple], bufs)
    ctx_a, lse_a = attend_call(triple, bias, 0, 3)
    bufs, small, ctx_a = gather_step(bufs, small, 1, ctx_a)
    (triple,), bufs = tie([triple], bufs)
    ctx_b, lse_b = attend_call(triple, bias, 3, 3)
    bufs, small, ctx_b = gather_step(bufs, small, 2, ctx_b)
    (ctx_b,), bufs = tie([ctx_b], bufs)
    hidden, routed = out_call(ctx_a, ctx_b, out_weight, out_bias, tokens)
    other_routed = swap_cores(routed)
    (other_kinds,), (routed,) = tie([other_kinds], [routed])
    select, turned, up, nv = select_call(jnp.concatenate([kinds, other_kinds]), cotangent, other_cot)
    bufs, small, up = gather_step(bufs, small, 3, up)
    near = near_sends(bufs)
    (select,), bufs = tie([select], bufs)
    rows = sort_call(select, routed, other_routed)
    (small,), (rows,) = tie([small], [rows])
    small = small + pair_up(small, "z", 0)
    small = small + pair_up(small, "z", 1)
    pairs = []
    for k in range(3):
        pairs.append(jnp.concatenate([bufs[k], near[k]]))
        if k < 2:
            (near[k + 1],), (pairs[k],) = tie([near[k + 1]], [pairs[k]])
    far = far_sends(pairs)

    hidden_bias = small[6:14].reshape(2, 64, 3, 2, 8)
    hidden_bias = choose(core == 0, hidden_bias[:, :, :, 0], hidden_bias[:, :, :, 1])
    table = relative_table(dp, core)
    spread = jnp.einsum("kps,esku->ekpu", table, hidden_bias, preferred_element_type=f32)
    hidden_bias = spread.reshape(2, 3, 2, 2 * PIECE).transpose(2, 0, 1, 3).reshape(2, 2, HALF_HID)

    pick = lambda a, b: [v for k in range(3) for v in (a[k], b[k])]
    (n2, branch, gn2, db0), dw0 = expert_call(nv, rows, up, hidden_bias[0], pick(bufs, near), small=small)
    (back_own, back_other, db1), dw1 = expert_call(
        nv, n2, up, hidden_bias[1], far, sums=(turned, branch, gn2)
    )

    got0 = near_sends(dw0[1::2])
    dw1_own, dw1_near = list(dw1[0::2]), list(dw1[1::2])
    (back_other, *dw1_near), got0 = tie([back_other, *dw1_near], got0)
    back_recv = swap_cores(back_other)
    got = near_sends(dw1_near)
    mixed, gh, gctx, dw_out, delta, small_b = post_call(
        back_own, back_recv, hidden, cotangent, lang, small, out_weight, ctx_a, ctx_b
    )
    dw1_own, (gh,) = tie(dw1_own, [gh])
    send = [plus(dw1_own[k], got[k]) for k in range(3)]
    (triple,), send = tie([triple], send)
    got = far_sends(send)
    parts = list(attend_back_call(triple, gctx, lse_a, lse_b, delta, bias))
    dw0_own, (parts[0],) = tie(dw0[0::2], [parts[0]])
    bufs = [
        (dw0_own[k].astype(f32) + got0[k].astype(f32) + got[k].astype(f32)).astype(bf16) for k in range(3)
    ]
    live = [[(ORDERS[k][i], t) for i in (1, 0) for t in (1, 0)] for k in range(3)]
    (gh,), bufs = tie([gh], bufs)
    which, kept, sent = reduce_parts(bufs, live, "z", 1)
    (gh,), (sent,) = tie([gh], [sent])
    back = pair_up(sent, "z", 1)

    (db0,), (gh,) = tie([db0], [gh])
    db = jnp.stack([db0, db1]).reshape(2, 2, 3, 256).transpose(2, 0, 3, 1).reshape(3, 2, 32, 8, 2)
    db = db.reshape(3, 64, 8, 2).astype(bf16)
    db = jnp.einsum("kps,kpue->esku", table, db, preferred_element_type=f32)
    zero = jnp.zeros_like(db)
    db = choose(core == 0, jnp.stack([db, zero], 3), jnp.stack([zero, db], 3)).reshape(8, D)

    mine, theirs, tokens_grad = final_call(
        core.reshape(1), n1, tokens, norm1_gain, qkv_weight, gh, dw_out, small_b, db, parts
    )

    (theirs,), (back,) = tie([theirs], [back])
    bufs = reduce_sums(bufs, live, which, kept, back)
    grad_qkv, grad_out, vectors, mine, bias_grad, bufs = all_sum(mine, theirs, dp, core, bufs, live)
    shards = jnp.stack(bufs).reshape(3, 2, 2, 8, D)
    stay = choose(core == 0, shards[:, 0], shards[:, 1])
    leave = choose(core == 0, shards[:, 1], shards[:, 0])
    came = swap_cores(leave)
    full = choose(core == 0, jnp.stack([stay, came], 2), jnp.stack([came, stay], 2))
    full = full.transpose(1, 0, 2, 3, 4).reshape(2, 48, D)

    return (
        mixed,
        tokens_grad,
        vectors[0],
        vectors[1],
        grad_qkv,
        vectors[2],
        vectors[3],
        grad_out,
        vectors[4],
        mine[0],
        mine[1],
        full[0].T[None],
        bias_grad,
        full[1][None],
        mine[2],
    )


def solution(mesh):
    both = ("dp", "expert")
    in_specs = (
        P(both, None),
        P(both),
        P(both, None),
        P(),
        P(),
        P(),
        P(),
        P(),
        P(),
        P(),
        P("expert", "dp"),
        P("expert", "dp"),
        P("expert", None, "dp"),
        P("expert", "dp"),
        P("expert", "dp", None),
        P("expert", "dp"),
    )
    out_specs = (
        P(both, None),
        P(both, None),
        P(),
        P(),
        P(),
        P(),
        P(),
        P(),
        P(),
        P("expert", "dp"),
        P("expert", "dp"),
        P("expert", None, "dp"),
        P("expert", "dp"),
        P("expert", "dp", None),
        P("expert", "dp"),
    )
    return jax.shard_map(body, mesh=mesh, in_specs=in_specs, out_specs=out_specs, check_vma=False)
```

```python
import functools

import jax
import jax.numpy as jnp
from jax import lax
from jax.experimental import pallas as pl
from jax.experimental.pallas import tpu as pltpu
from jax.sharding import PartitionSpec as P

HEADS = 12
IMG_LEN = 197
TXT_LEN = 40
ROWS = 512
CHIP_ROWS = 1024
D = 768
FF = 3072
ITEMS_DEV = 13
PAIRS = HEADS // 2
LANES = 128
BLOCK = 256
MASKED = -1e30
EPS = 1e-5
PLANS = {
    "qkv": (20, False),
    "attend": (16, False),
    "outproj": (12, False),
    "select": (20, False),
    "sort": (12, False),
    "expert": (56, True),
    "post": (56, True),
    "attend_back": (56, False),
    "final": (56, True),
    "split": (16, False),
    "join": (12, False),
    "assemble": (24, False),
}
AR_ROWS = 3264
SMALL_ROWS = AR_ROWS - 4 * D
AR_PIECE = AR_ROWS // 12
HALF = D // 2

bf16 = jnp.bfloat16
f32 = jnp.float32


def dot(left, right):
    return jnp.dot(left, right, preferred_element_type=f32)


def dot_t(left, right):
    return lax.dot_general(left, right, (((1,), (1,)), ((), ())), preferred_element_type=f32)


def dot_0(left, right):
    return lax.dot_general(left, right, (((0,), (0,)), ((), ())), preferred_element_type=f32)


def params(mebibytes):
    return pltpu.CompilerParams(vmem_limit_bytes=mebibytes * 1024 * 1024)


def cost(flops, byts, trans=0):
    return pl.CostEstimate(flops=int(flops), bytes_accessed=int(byts), transcendentals=int(trans))


def shape(dims, dtype):
    return jax.ShapeDtypeStruct(dims, dtype)


VM = pl.BlockSpec(memory_space=pltpu.VMEM)
SM = pl.BlockSpec(memory_space=pltpu.SMEM)
HB = pl.BlockSpec(memory_space=pl.ANY)


def staged_call(
    body, name, smem, small, loads, outs, plain=(), scratch=(), flops=1e9, raw=(), cuts=None, out_cuts=None, first=()
):
    n_out = len(outs)
    limit, staged = PLANS[name]
    big = HB if staged else VM
    cuts, out_cuts = cuts or {}, out_cuts or {}

    def plain_kernel(*refs):
        at = len(smem) + len(small)
        s_refs, v_refs = refs[: len(smem)], refs[len(smem) : at]
        ins, rest = refs[at : at + len(loads)], refs[at + len(loads) :]
        results, extra = rest[: n_out + len(plain)], rest[n_out + len(plain) :]
        body(s_refs, v_refs, lambda i, c=None: ins[i], results, lambda j, c=None: None, extra)

    def part(ref, c, count, axis):
        if count == 1:
            return ref
        size = ref.shape[axis] // count
        return ref.at[(slice(None),) * axis + (pl.ds(c * size, size),)]

    def kernel(*refs):
        refs = list(refs)
        take = lambda n: [refs.pop(0) for _ in range(n)]
        s_refs, v_refs, hbm, raw_refs = take(len(smem)), take(len(small)), take(len(loads)), take(len(raw))
        out_hbm = take(n_out)
        plain_refs, bufs, out_bufs, extra = take(len(plain)), take(len(loads)), take(n_out), take(len(scratch))
        in_sem, out_sem = refs
        copies, sent = {}, []
        for i in range(len(loads)):
            count, axis = cuts.get(i, (1, 0))
            for c in range(count):
                pieces = part(hbm[i], c, count, axis), part(bufs[i], c, count, axis)
                copies[i, c] = pltpu.make_async_copy(*pieces, in_sem.at[len(copies)])
        for key in sorted(copies, key=lambda key: (key[1], key[0]) if key[0] in first else (99, key)):
            copies[key].start()

        def get(i, c=None):
            for key in [key for key in copies if key[0] == i and c in (None, key[1])]:
                copies.pop(key).wait()
            return bufs[i]

        def put(j, c=None):
            count, axis = out_cuts.get(j, (1, 0))
            for piece in range(count) if c is None else [c]:
                pieces = part(out_bufs[j], piece, count, axis), part(out_hbm[j], piece, count, axis)
                copy = pltpu.make_async_copy(*pieces, out_sem.at[len(sent)])
                copy.start()
                sent.append(copy)

        body(s_refs, v_refs, get, out_bufs + plain_refs, put, ([raw_refs] if raw else []) + extra)
        assert not copies
        for copy in sent:
            copy.wait()

    n_in = sum(cuts.get(i, (1, 0))[0] for i in range(len(loads)))
    n_sent = sum(out_cuts.get(j, (1, 0))[0] for j in range(n_out))
    bytes_moved = sum(v.size * v.dtype.itemsize for v in (*loads, *outs))
    buffers = [pltpu.VMEM(v.shape, v.dtype) for v in (*loads, *outs)] if staged else []
    sems = [pltpu.SemaphoreType.DMA((n_in,)), pltpu.SemaphoreType.DMA((max(n_sent, 1),))] if staged else []
    return pl.pallas_call(
        kernel if staged else plain_kernel,
        out_shape=(*outs, *(struct for struct, _ in plain)),
        in_specs=[SM] * len(smem) + [VM] * len(small) + [big] * len(loads) + [HB] * len(raw),
        out_specs=(big,) * n_out + tuple(spec for _, spec in plain),
        scratch_shapes=buffers + list(scratch) + sems,
        compiler_params=params(limit),
        cost_estimate=cost(flops, bytes_moved),
        name=name,
    )(*smem, *small, *loads, *raw)


def as_row(ref):
    return ref[...].astype(f32).reshape(1, D)


def norm_stats(x):
    centred = x - jnp.mean(x, axis=-1, keepdims=True)
    rstd = lax.rsqrt(jnp.mean(centred * centred, axis=-1, keepdims=True) + EPS)
    return centred * rstd, rstd


def item_lengths(kind):
    vision = jnp.where(kind == 1, 0, IMG_LEN)
    language = jnp.where(kind == 0, 0, TXT_LEN)
    return vision, language


def qkv_kernel(smem, small, get, outs, put, scratch):
    (kind_ref,) = smem
    n1_ref, tri_ref, bias_ref, lang_ref = outs
    gain, shift, q_bias, v_bias = (as_row(ref) for ref in small)
    tok_ref = get(0)
    for r in range(0, ROWS, LANES):
        xhat, _ = norm_stats(tok_ref[r : r + LANES, :].astype(f32))
        n1_ref[r : r + LANES, :] = (xhat * gain + shift).astype(bf16)
    put(0)
    n1 = n1_ref[...]
    w_ref = get(1)
    q = dot(n1, w_ref[:, 0:D]) + q_bias
    tri_ref[:, 0:D] = q.astype(bf16) * jnp.asarray(0.125, bf16)
    tri_ref[:, D : 2 * D] = dot(n1, w_ref[:, D : 2 * D]).astype(bf16)
    tri_ref[:, 2 * D :] = (dot(n1, w_ref[:, 2 * D :]) + v_bias).astype(bf16)
    put(1)
    down = lax.broadcasted_iota(jnp.int32, (ROWS, LANES), 0)
    across = lax.broadcasted_iota(jnp.int32, (8, ROWS), 1)
    item_down = jnp.zeros((ROWS, LANES), jnp.int32)
    item_across = jnp.zeros((8, ROWS), jnp.int32)
    lang = jnp.zeros((ROWS, LANES), f32)
    start = 0
    for i in range(ITEMS_DEV):
        vision, language = item_lengths(kind_ref[0, i])
        middle = start + vision
        end = middle + language
        item_down += (down >= end).astype(jnp.int32)
        item_across += (across >= end).astype(jnp.int32)
        lang = jnp.where((down >= middle) & (down < end), 1.0, lang)
        start = end
    lang_ref[...] = lang
    put(3)
    for c in range(0, ROWS, LANES):
        same = item_down == item_across[0:1, c : c + LANES]
        bias_ref[:, c : c + LANES] = jnp.where(same, 0.0, MASKED)
    put(2)


def qkv_call(kinds, tokens, vectors, weight):
    outs = (shape((ROWS, D), bf16), shape((ROWS, 3 * D), bf16), shape((ROWS, ROWS), f32), shape((ROWS, LANES), f32))
    return staged_call(qkv_kernel, "qkv", [kinds], vectors, [tokens, weight], outs, flops=2 * ROWS * D * 3 * D * 2)


def half_lanes(head):
    lane = lax.broadcasted_iota(jnp.int32, (1, LANES), 1)
    return (lane < LANES // 2) if head == 0 else (lane >= LANES // 2)


def attend_kernel(q_ref, k_ref, v_ref, bias_ref, ctx_ref, lse_ref):
    q, k, v = q_ref[...], k_ref[...], v_ref[...]
    zero = jnp.zeros_like(q)
    rows = lax.broadcasted_iota(jnp.int32, (LANES, 1), 0)
    parts = []
    for head in range(2):
        qm = jnp.where(half_lanes(head), q, zero)
        s = dot_t(k, qm) + bias_ref[...]
        top = jnp.max(s, axis=0, keepdims=True)
        e = jnp.exp(s - top)
        total = jnp.sum(e, axis=0, keepdims=True)
        lse_ref[0, head : head + 1, :] = top + jnp.log(total)
        parts.append(dot_0(v, e.astype(bf16)) * (1.0 / total))
    ctx = jnp.where(rows < LANES // 2, parts[0], parts[1])
    ctx_ref[...] = ctx.T.astype(bf16)


def attend_call(triple, bias, first, count):
    def col(offset):
        return pl.BlockSpec((ROWS, LANES), lambda p: (0, offset + first + p))

    return pl.pallas_call(
        attend_kernel,
        grid=(count,),
        out_shape=(shape((ROWS, count * LANES), bf16), shape((count, 8, ROWS), f32)),
        in_specs=[col(0), col(PAIRS), col(2 * PAIRS), pl.BlockSpec((ROWS, ROWS), lambda p: (0, 0))],
        out_specs=(
            pl.BlockSpec((ROWS, LANES), lambda p: (0, p)),
            pl.BlockSpec((1, 8, ROWS), lambda p: (p, 0, 0)),
        ),
        compiler_params=params(PLANS["attend"][0]),
        cost_estimate=cost(count * 2 * 4e9, count * 6e6),
        name="attend",
    )(triple, triple, triple, bias)


def out_kernel(smem, small, get, outs, put, scratch):
    hid_ref, routed_ref = outs
    half = D // 2
    ca_ref, cb_ref, w_ref = get(0), get(1), get(2)
    h = dot(ca_ref[...], w_ref[:half, :]) + dot(cb_ref[...], w_ref[half:, :])
    h = get(3)[...].astype(f32) + h + as_row(small[0])
    routed_ref[...] = h.astype(bf16)
    put(1)
    hid_ref[...] = h
    put(0)


def out_call(ctx_a, ctx_b, weight, bias, tokens):
    outs = (shape((ROWS, D), f32), shape((ROWS, D), bf16))
    return staged_call(
        out_kernel, "outproj", [], [bias], [ctx_a, ctx_b, weight, tokens], outs, flops=2 * ROWS * D * D * 2
    )


def select_kernel(smem, small, get, outs, put, scratch):
    (kind_ref,) = smem
    sel_ref, up_ref, nv_ref = outs
    spans = []
    vision_total = 0
    for pack in range(2):
        start = 0
        for i in range(ITEMS_DEV):
            vision, language = item_lengths(kind_ref[pack, i])
            first = jnp.minimum(start, ROWS)
            middle = jnp.minimum(start + vision, ROWS)
            end = jnp.minimum(start + vision + language, ROWS)
            spans.append((pack, first, middle, end))
            vision_total = vision_total + middle - first
            start = start + vision + language
    nv_ref[0] = vision_total
    place = lax.broadcasted_iota(jnp.int32, (1, ROWS), 1)
    target = [jnp.zeros((1, ROWS), jnp.int32) for _ in range(2)]
    at_vision, at_language = 0, vision_total
    for pack, first, middle, end in spans:
        t = target[pack]
        t = jnp.where((place >= first) & (place < middle), place + (at_vision - first), t)
        t = jnp.where((place >= middle) & (place < end), place + (at_language - middle), t)
        target[pack] = t
        at_vision = at_vision + middle - first
        at_language = at_language + end - middle
    own, other = get(0)[...], get(1)[...]
    for r in range(0, CHIP_ROWS, BLOCK):
        down = lax.broadcasted_iota(jnp.int32, (BLOCK, ROWS), 0) + r
        for pack in range(2):
            sel_ref[r : r + BLOCK, pack * ROWS : (pack + 1) * ROWS] = (
                (down == target[pack]).astype(f32).astype(bf16)
            )
        up_ref[r : r + BLOCK, :] = (
            dot(sel_ref[r : r + BLOCK, :ROWS], own) + dot(sel_ref[r : r + BLOCK, ROWS:], other)
        ).astype(bf16)
    put(0)
    put(1)


def select_call(kinds, own, other):
    square = shape((CHIP_ROWS, CHIP_ROWS), bf16)
    outs = (square, shape((CHIP_ROWS, D), bf16))
    plain = ((shape((1,), jnp.int32), SM),)
    flops = 2 * 2 * CHIP_ROWS * CHIP_ROWS * D
    return staged_call(select_kernel, "select", [kinds], [], [own, other], outs, plain, flops=flops)


def sort_kernel(smem, small, get, outs, put, scratch):
    sel_ref = get(0)
    own, other = get(1)[...], get(2)[...]
    for r in range(0, CHIP_ROWS, BLOCK):
        x = dot(sel_ref[r : r + BLOCK, :ROWS], own) + dot(sel_ref[r : r + BLOCK, ROWS:], other)
        outs[0][r : r + BLOCK, :] = x.astype(bf16)
    put(0)


def sort_call(select, own, other):
    return staged_call(
        sort_kernel,
        "sort",
        [],
        [],
        [select, own, other],
        (shape((CHIP_ROWS, D), bf16),),
        flops=2 * CHIP_ROWS * CHIP_ROWS * D,
    )[0]


def gelu_parts(x):
    t = 1.0 / (1.0 + 0.2316418882663604 * jnp.abs(x))
    poly = 0.127414796 + t * (-0.142248368 + t * (0.7107068705 + t * (-0.7265760135 + t * 0.5307027145)))
    bell = jnp.exp2(x * x * -0.7213475204444817)
    tail = t * poly * bell
    phi = jnp.where(x >= 0, 1.0 - tail, tail)
    return x * phi, phi + (x * 0.3989422804014327) * bell


THIRDS = 3
PIECE = 128
HALF_HID = THIRDS * 2 * PIECE


def expert_kernel(first, smem, small, get, outs, put, scratch):
    (nv_ref,), bias_ref = smem, small[0]
    w_hbm, scratch = scratch[0], scratch[1:]
    if first:
        n2_ref, *sums_hbm, db_ref = outs[:4]
        dw_hbm = outs[4:]
    else:
        own_ref, other_ref, db_ref = outs[:3]
        dw_hbm = outs[3:]
    branch_ref, gn2_ref, sum_sem, scratch = scratch[0], scratch[1], scratch[2], scratch[3:]
    w_ref, acc_ref, out_ref, act_ref, gp_ref, in_sem, out_sem = scratch
    loads = []
    for k in range(THIRDS):
        for j in range(2):
            at = k * 2 * PIECE + j * PIECE
            ref = w_hbm[2 * k + j if first else k]
            for m in range(4):
                block = m if first else 4 * j + m
                part = ref.at[block] if len(ref.shape) == 3 else ref.at[pl.ds(block * PIECE, PIECE), :]
                copy = pltpu.make_async_copy(
                    part, w_ref.at[m, pl.ds(at, PIECE), :], in_sem.at[8 * k + 4 * j + m]
                )
                copy.start()
                loads.append(copy)
    branch_ref[...] = jnp.zeros_like(branch_ref)
    gn2_ref[...] = jnp.zeros_like(gn2_ref)
    x_ref = get(0)
    if first:
        par = small[1][...].astype(f32)
        for r in range(0, CHIP_ROWS, LANES):
            xhat, _ = norm_stats(x_ref[r : r + LANES, :].astype(f32))
            vision = (lax.broadcasted_iota(jnp.int32, (LANES, 1), 0) + r) < nv_ref[0]
            gain = jnp.where(vision, par[0:1, :], par[1:2, :])
            shift = jnp.where(vision, par[2:3, :], par[3:4, :])
            n2_ref[r : r + LANES, :] = (xhat * gain + shift).astype(bf16)
        put(0)
    else:
        n2_ref = x_ref
    up_ref = get(1)
    db_ref[...] = jnp.zeros_like(db_ref)
    for copy in loads:
        copy.wait()
    nv = nv_ref[0]
    stores = []
    for e in range(2):
        low = jnp.int32(0) if e == 0 else nv // BLOCK
        high = (nv + BLOCK - 1) // BLOCK if e == 0 else jnp.int32(CHIP_ROWS // BLOCK)
        acc_ref[...] = jnp.zeros_like(acc_ref)

        def visit(block, size, e=e):
            at = pl.multiple_of(block * BLOCK, BLOCK)
            rows = pl.ds(at, size)
            index = lax.broadcasted_iota(jnp.int32, (size, 1), 0) + at
            valid = (index < nv) if e == 0 else (index >= nv)
            n2 = n2_ref[rows, :]
            up = up_ref[rows, :]
            for k in range(THIRDS):
                hid = slice(k * BLOCK, (k + 1) * BLOCK)
                pre = dot_t(n2, w_ref[2 * e, hid, :]) + bias_ref[e : e + 1, hid].astype(f32)
                back = dot_t(up, w_ref[2 * e + 1, hid, :])
                active, slope = gelu_parts(pre)
                act = jnp.where(valid, active, 0.0).astype(bf16)
                gp = jnp.where(valid, back * slope, 0.0).astype(bf16)
                act_ref[:size, hid] = act
                gp_ref[:size, hid] = gp
                db_ref[e : e + 1, hid] += jnp.sum(gp.astype(f32), axis=0, keepdims=True)
            acc_ref[0] += dot_0(gp_ref[:size, :], n2)
            acc_ref[1] += dot_0(act_ref[:size, :], up)
            branch_ref[rows, :] += dot(act_ref[:size, :], w_ref[2 * e + 1])
            gn2_ref[rows, :] += dot(gp_ref[:size, :], w_ref[2 * e])
            if not first:
                return
            for b in range(size // BLOCK):
                done = pl.ds(pl.multiple_of(at + b * BLOCK, BLOCK), BLOCK)

                @pl.when((at + (b + 1) * BLOCK <= nv) if e == 0 else (at >= 0))
                def _(done=done):
                    for i, ref in enumerate((branch_ref, gn2_ref)):
                        pltpu.make_async_copy(ref.at[done, :], sums_hbm[i].at[done, :], sum_sem.at[i]).start()

        count = high - low

        def two(i, carry, visit=visit, low=low):
            visit(low + 2 * i, 2 * BLOCK)
            return carry

        lax.fori_loop(0, count // 2, two, 0)

        @pl.when(count % 2 == 1)
        def _(visit=visit, high=high):
            visit(high - 1, BLOCK)

        out_ref[2 * e] = acc_ref[0].astype(bf16)
        out_ref[2 * e + 1] = acc_ref[1].astype(bf16)
        for k in range(THIRDS):
            for j in range(2):
                at = k * 2 * PIECE + j * PIECE
                copy = pltpu.make_async_copy(
                    out_ref.at[pl.ds(2 * e, 2), pl.ds(at, PIECE), :],
                    dw_hbm[2 * k + j].at[pl.ds(2 * e, 2)],
                    out_sem.at[6 * e + 2 * k + j],
                )
                copy.start()
                stores.append(copy)
    if first:
        for i, ref in enumerate((branch_ref, gn2_ref)):
            pltpu.make_async_copy(ref, sums_hbm[i], sum_sem.at[i]).wait()
    else:
        sel_ref = get(2)
        for i, total in enumerate((branch_ref, gn2_ref)):
            y = (get(3 + i)[...] + total[...]).astype(bf16)
            other_ref[i] = dot_0(sel_ref[:, ROWS:], y).astype(bf16)
            own_ref[i] = dot_0(sel_ref[:, :ROWS], y).astype(bf16)
        put(1)
        put(0)
    for copy in stores:
        copy.wait()


def expert_call(nv, rows, up, bias, weights, small=None, sums=None):
    first = sums is None
    db = (shape((2, HALF_HID), f32), VM)
    part = shape((CHIP_ROWS, D), f32)
    back = shape((2, ROWS, D), bf16)
    pieces = ((shape((4, PIECE, D), bf16), HB),) * 6
    work = [
        pltpu.VMEM((CHIP_ROWS, D), f32),
        pltpu.VMEM((CHIP_ROWS, D), f32),
        pltpu.SemaphoreType.DMA((2,)),
        pltpu.VMEM((4, HALF_HID, D), bf16),
        pltpu.VMEM((2, HALF_HID, D), f32),
        pltpu.VMEM((4, HALF_HID, D), bf16),
        pltpu.VMEM((2 * BLOCK, HALF_HID), bf16),
        pltpu.VMEM((2 * BLOCK, HALF_HID), bf16),
        pltpu.SemaphoreType.DMA((24,)),
        pltpu.SemaphoreType.DMA((12,)),
    ]
    if first:
        outs = staged_call(
            functools.partial(expert_kernel, True), "expert", [nv], [bias, small], [rows, up],
            (shape((CHIP_ROWS, D), bf16),), ((part, HB), (part, HB), db, *pieces), work, 20e9, raw=weights,
        )
    else:
        outs = staged_call(
            functools.partial(expert_kernel, False), "expert", [nv], [bias], [rows, up, *sums],
            (back, back), (db, *pieces), work, 20e9, raw=weights,
        )
    return outs[:-6], outs[-6:]


def post_kernel(smem, small, get, outs, put, scratch):
    mixed_ref, gh_ref, gctx_ref, dw_ref, delta_ref, small_ref = outs
    g_ref, prod_ref = scratch
    par = small[0][...].astype(f32)
    gains, bouts = par[0:2, :], par[4:6, :]
    small_ref[...] = jnp.zeros_like(small_ref)
    for r in range(0, ROWS, LANES):
        rows = slice(r, r + LANES)
        own_ref, recv_ref, hid_ref, cot_ref, lang_ref = (get(i, r // LANES) for i in range(5))
        lang = lang_ref[rows, 0:1]
        is_lang = lang > 0.5
        branch = own_ref[0, rows, :].astype(f32) + recv_ref[0, rows, :].astype(f32)
        branch = branch + jnp.where(is_lang, bouts[1:2, :], bouts[0:1, :])
        mixed_ref[rows, :] = (hid_ref[rows, :] + branch.astype(bf16).astype(f32)).astype(bf16)
        gn2 = own_ref[1, rows, :].astype(f32) + recv_ref[1, rows, :].astype(f32)
        xhat, rstd = norm_stats(hid_ref[rows, :].astype(bf16).astype(f32))
        gg = gn2 * jnp.where(is_lang, gains[1:2, :], gains[0:1, :])
        mean_a = jnp.mean(gg, axis=-1, keepdims=True)
        mean_b = jnp.mean(gg * xhat, axis=-1, keepdims=True)
        grad_routed = (rstd * (gg - mean_a - xhat * mean_b)).astype(bf16).astype(f32)
        cot = cot_ref[rows, :].astype(f32)
        gh = cot + grad_routed
        gh_ref[rows, :] = gh
        put(0, r // LANES)
        put(1, r // LANES)
        g_ref[rows, :] = gh.astype(bf16)
        prod = gn2 * xhat
        for i, (value, mask) in enumerate(((gh, None), (prod, 0), (prod, 1), (gn2, 0), (gn2, 1), (cot, 0), (cot, 1))):
            if mask is not None:
                value = jnp.where(is_lang, value, 0.0) if mask == 1 else jnp.where(is_lang, 0.0, value)
            small_ref[i : i + 1, :] += jnp.sum(value, axis=0, keepdims=True)
    g = g_ref[...]
    half = D // 2
    w_ref, ca_ref, cb_ref = get(5), get(6), get(7)
    dw_ref[:half, :] = dot_0(ca_ref[...], g).astype(bf16)
    dw_ref[half:, :] = dot_0(cb_ref[...], g).astype(bf16)
    put(3)
    gctx_ref[...] = dot_t(g, w_ref[...]).astype(bf16)
    put(2)
    prod_ref[:, :half] = gctx_ref[:, :half].astype(f32) * ca_ref[...].astype(f32)
    prod_ref[:, half:] = gctx_ref[:, half:].astype(f32) * cb_ref[...].astype(f32)
    head = lax.broadcasted_iota(jnp.int32, (16, D), 0)
    lane = lax.broadcasted_iota(jnp.int32, (16, D), 1)
    pick = (lane // 64 == head).astype(f32).astype(bf16)
    prod = prod_ref[...]
    upper = prod.astype(bf16)
    lower = (prod - upper.astype(f32)).astype(bf16)
    delta = dot_t(pick, upper) + dot_t(pick, lower)
    delta_ref[...] = jnp.zeros_like(delta_ref)
    for h in range(HEADS):
        delta_ref[h // 2, h % 2 : h % 2 + 1, :] = delta[h : h + 1, :]


def post_call(own, recv, hidden, cot, lang, small, weight, ctx_a, ctx_b):
    rows = shape((ROWS, D), bf16)
    outs = (rows, shape((ROWS, D), f32), rows, shape((D, D), bf16))
    plain = ((shape((PAIRS, 8, ROWS), f32), VM), (shape((8, D), f32), VM))
    work = [pltpu.VMEM((ROWS, D), bf16), pltpu.VMEM((ROWS, D), f32)]
    loads = [own, recv, hidden, cot, lang, weight, ctx_a, ctx_b]
    cuts = {0: (4, 1), 1: (4, 1), 2: (4, 0), 3: (4, 0), 4: (4, 0)}
    return staged_call(
        post_kernel, "post", [], [small], loads, outs, plain, work, 6e9,
        cuts=cuts, out_cuts={0: (4, 0), 1: (4, 0)}, first=range(5),
    )


def attend_back_kernel(q_ref, k_ref, v_ref, g_ref, lse_a, lse_b, delta_ref, bias_ref, dq_ref, dk_ref, dv_ref):
    q, k, v, g = q_ref[...], k_ref[...], v_ref[...], g_ref[...]
    zero = jnp.zeros_like(q)
    lse = jnp.where(pl.program_id(0) < PAIRS // 2, lse_a[0], lse_b[0])
    parts = []
    dk = dv = 0.0
    for c in range(0, ROWS, BLOCK):
        cols = slice(c, c + BLOCK)
        dq = 0.0
        for head in range(2):
            lanes = half_lanes(head)
            qm, gm = (jnp.where(lanes, x[cols, :], zero[cols, :]) for x in (q, g))
            km = jnp.where(lanes, k, zero)
            s = dot_t(k, qm) + bias_ref[:, cols]
            p = jnp.exp(s - lse[head : head + 1, cols])
            dp = dot_t(v, gm)
            ds = (p * (dp - delta_ref[0, head : head + 1, cols])).astype(bf16)
            dv = dv + dot(p.astype(bf16), gm)
            dk = dk + dot(ds, qm)
            dq = dq + dot_0(ds, km)
        parts.append(dq)
    dq = jnp.concatenate(parts, axis=0)
    dq_ref[...] = (dq * 0.125).astype(bf16)
    dk_ref[...] = dk.astype(bf16)
    dv_ref[...] = dv.astype(bf16)


def attend_back_call(triple, gctx, lse_a, lse_b, delta, bias):
    def col(offset):
        return pl.BlockSpec((ROWS, LANES), lambda p: (0, offset + p))

    half = PAIRS // 2
    return pl.pallas_call(
        attend_back_kernel,
        grid=(PAIRS,),
        out_shape=(shape((ROWS, D), bf16),) * 3,
        in_specs=[
            col(0),
            col(PAIRS),
            col(2 * PAIRS),
            col(0),
            pl.BlockSpec((1, 8, ROWS), lambda p: (jnp.minimum(p, half - 1), 0, 0)),
            pl.BlockSpec((1, 8, ROWS), lambda p: (jnp.maximum(p - half, 0), 0, 0)),
            pl.BlockSpec((1, 8, ROWS), lambda p: (p, 0, 0)),
            pl.BlockSpec((ROWS, ROWS), lambda p: (0, 0)),
        ],
        out_specs=(col(0),) * 3,
        compiler_params=params(PLANS["attend_back"][0]),
        cost_estimate=cost(20e9, 10e6),
        name="attend_back",
    )(triple, triple, triple, gctx, lse_a, lse_b, delta, bias)


def final_kernel(smem, small, get, outs, put, scratch):
    (core_ref,), (gain_ref, sb_ref, db_ref) = smem, small
    out_ref, *targets = outs
    gn_ref, small_ref, buf_ref, rows_ref, sem = scratch
    core = core_ref[0]
    lanes = [pl.ds(pl.multiple_of(h * HALF, LANES), HALF) for h in (core, 1 - core)]
    sent = []

    def send(source, t, at, size):
        copy = pltpu.make_async_copy(source, targets[t].at[pl.ds(at, size), :], sem.at[len(sent)])
        copy.start()
        sent.append(copy)

    small_ref[...] = jnp.zeros_like(small_ref)
    n1 = get(0)[...]
    for t in (1, 0):
        for i in range(3):
            buf_ref[t, i * D : (i + 1) * D, :] = dot_0(n1, get(1 + i)[:, lanes[t]]).astype(bf16)
            send(buf_ref.at[t, pl.ds(i * D, D), :], t, i * D, D)
        if t == 0:
            break
        for i in range(3):
            piece = get(1 + i)[...]
            part = dot_t(piece, get(4)[:, i * D : (i + 1) * D])
            if i == 0:
                gn_ref[...] = part
            else:
                gn_ref[...] += part
            if i != 1:
                small_ref[2 + i // 2 : 3 + i // 2, :] = jnp.sum(piece.astype(f32), axis=0, keepdims=True)
    gain = as_row(gain_ref)
    for r in range(0, ROWS, LANES):
        rows = slice(r, r + LANES)
        tok_ref, gh_ref = get(5, r // LANES), get(6, r // LANES)
        xhat, rstd = norm_stats(tok_ref[rows, :].astype(f32))
        gn = gn_ref[rows, :]
        small_ref[0:1, :] += jnp.sum(gn * xhat, axis=0, keepdims=True)
        small_ref[1:2, :] += jnp.sum(gn, axis=0, keepdims=True)
        gg = gn * gain
        mean_a = jnp.mean(gg, axis=-1, keepdims=True)
        mean_b = jnp.mean(gg * xhat, axis=-1, keepdims=True)
        out_ref[rows, :] = gh_ref[rows, :] + rstd * (gg - mean_a - xhat * mean_b)
        put(0, r // LANES)
    small_ref[8:16, :] = sb_ref[...]
    small_ref[16:24, :] = db_ref[...]
    for t in (1, 0):
        rows_ref[t] = small_ref[:, lanes[t]].astype(bf16)
        send(rows_ref.at[t], t, 4 * D, SMALL_ROWS)
    for t in (1, 0):
        buf_ref[t, 3 * D : 4 * D, :] = get(7)[:, lanes[t]]
        send(buf_ref.at[t, pl.ds(3 * D, D), :], t, 3 * D, D)
    for copy in sent:
        copy.wait()


def final_call(core, n1, tokens, gain, weight, gh, dw_out, small_b, db, parts):
    half = shape((AR_ROWS, HALF), bf16)
    work = [
        pltpu.VMEM((ROWS, D), f32),
        pltpu.VMEM((SMALL_ROWS, D), f32),
        pltpu.VMEM((2, 4 * D, HALF), bf16),
        pltpu.VMEM((2, SMALL_ROWS, HALF), bf16),
        pltpu.SemaphoreType.DMA((10,)),
    ]
    loads = [n1, *parts, weight, tokens, gh, dw_out]
    out, mine, theirs = staged_call(
        final_kernel, "final", [core], [gain, small_b, db], loads, (shape((ROWS, D), f32),),
        ((half, HB), (half, HB)), work, 2 * 2 * 2 * ROWS * D * 3 * D,
        cuts={5: (4, 0), 6: (4, 0)}, out_cuts={0: (4, 0)},
    )
    return mine, theirs, out


def split_kernel(order_ref, mine_ref, got_ref, *outs):
    for k in range(THIRDS):
        for i in range(4):
            rows = pl.ds(pl.multiple_of(k * 4 * AR_PIECE + order_ref[4 * k + i] * AR_PIECE, 16), AR_PIECE)
            total = mine_ref[rows, :].astype(f32) + got_ref[rows, :].astype(f32)
            outs[2 * k + i // 2][i % 2] = total.astype(bf16)


def split_call(order, mine, got):
    return pl.pallas_call(
        split_kernel,
        out_shape=(shape((2, AR_PIECE, HALF), bf16),) * 6,
        in_specs=[SM, VM, VM],
        out_specs=(VM,) * 6,
        compiler_params=params(PLANS["split"][0]),
        cost_estimate=cost(3e6, 8e6),
        name="split",
    )(order, mine, got)


def join_kernel(order_ref, *refs):
    out_ref = refs[-1]
    for k in range(THIRDS):
        for i in range(4):
            rows = pl.ds(pl.multiple_of(k * 4 * AR_PIECE + order_ref[4 * k + i] * AR_PIECE, 16), AR_PIECE)
            out_ref[rows, :] = refs[2 * k + i // 2][i % 2]


def join_call(order, pieces):
    return pl.pallas_call(
        join_kernel,
        out_shape=shape((AR_ROWS, HALF), bf16),
        in_specs=[SM] + [VM] * 6,
        out_specs=VM,
        compiler_params=params(PLANS["join"][0]),
        cost_estimate=cost(3e6, 5e6),
        name="join",
    )(order, *pieces)


def assemble_kernel(place_ref, *refs):
    ins, (qkv_ref, out_ref), vectors, shards, bias_ref = refs[:10], refs[10:12], refs[12:17], refs[17:20], refs[20]
    core, dp = place_ref[0], place_ref[1]
    zero = core == 0

    def halves(i):
        mine, theirs = ins[2 * i][...].astype(f32), ins[2 * i + 1][...].astype(f32)
        return jnp.where(zero, mine, theirs), jnp.where(zero, theirs, mine)

    for i in range(4):
        for j, value in enumerate(halves(i)):
            if i < 3:
                qkv_ref[:, i * D + j * HALF : i * D + (j + 1) * HALF] = value
            else:
                out_ref[:, j * HALF : (j + 1) * HALF] = value

    @pl.when(pl.program_id(0) == 0)
    def _():
        rows = jnp.concatenate([value[:24, :] for value in halves(4)], axis=1)
        for ref, r in zip(vectors, (0, 1, 2, 3, 8)):
            ref[...] = rows[r : r + 1, :].reshape(D)
        down = lax.broadcasted_iota(jnp.int32, (D, LANES), 0)
        lane = lax.broadcasted_iota(jnp.int32, (D, LANES), 1)

        def pick(offset):
            return dot(rows.astype(bf16), (down - offset == lane).astype(f32).astype(bf16))

        norms = pick(12 * dp)
        for i, ref in enumerate(shards):
            both = norms[9 + 2 * i : 11 + 2 * i, :12]
            ref[...] = jnp.where(zero, both[0:1, :], both[1:2, :])
        biases = pick(48 * (dp % 16))
        at = lax.broadcasted_iota(jnp.int32, (24, LANES), 0)
        here = jnp.where(at == 16 + 4 * core + dp // 16, biases, 0.0)
        bias_ref[...] = jnp.sum(here, axis=0, keepdims=True)[:, :48]


def assemble_call(place, mine, theirs):
    step = SMALL_ROWS
    specs, args = [], []
    for i in range(5):
        for ref in (mine, theirs):
            specs.append(pl.BlockSpec((step, HALF), (lambda r, i=i: (4 * i + r, 0)) if i < 4 else (lambda r: (16, 0))))
            args.append(ref)
    outs = pl.pallas_call(
        assemble_kernel,
        grid=(D // step,),
        out_shape=(shape((D, 3 * D), f32), shape((D, D), f32))
        + (shape((D,), f32),) * 5
        + (shape((1, 12), f32),) * 3
        + (shape((1, 48), f32),),
        in_specs=[SM] + specs,
        out_specs=(
            pl.BlockSpec((step, 3 * D), lambda r: (r, 0)),
            pl.BlockSpec((step, D), lambda r: (r, 0)),
        )
        + (VM,) * 9,
        compiler_params=params(PLANS["assemble"][0]),
        cost_estimate=cost(3e6, 15e6),
        name="assemble",
    )(place, *args)
    return outs[0], outs[1], outs[2:7], outs[7:10], outs[10]


AXES = ("y", "x", "z")
STRIDE = {"y": 16, "x": 4, "z": 1}
ORDERS = (("x", "y", "z"), ("y", "z", "x"), ("z", "x", "y"))
FLIPS = (1, 3)


def coordinate(index, axis):
    return (index // STRIDE[axis]) % 4


def pair_up(values, axis, step):
    pairs = []
    for dp in range(64):
        for core in range(2):
            place = coordinate(dp, axis)
            flip = FLIPS[step ^ core]
            other = dp + ((place ^ flip) - place) * STRIDE[axis]
            pairs.append((2 * dp + core, 2 * other + core))
    return lax.ppermute(values, ("dp", "expert"), pairs)


def exchange(values, axis, step):
    pairs = []
    for dp in range(64):
        for core in range(2):
            place = coordinate(dp, axis)
            other = dp + ((place ^ FLIPS[step]) - place) * STRIDE[axis]
            pairs.append((2 * dp + core, 2 * other + core))
    return lax.ppermute(values, ("dp", "expert"), pairs)


def swap_cores(values):
    return lax.ppermute(values, "expert", [(0, 1), (1, 0)])


def relative_table(dp, core):
    bits = lax.iota(jnp.int32, 64)
    flip0 = jnp.where(core == 0, FLIPS[0], FLIPS[1])
    flip1 = jnp.where(core == 0, FLIPS[1], FLIPS[0])
    tables = []
    for order in ORDERS:
        source = jnp.zeros((64,), jnp.int32)
        for i, axis in enumerate(order):
            low = (bits >> (2 * i)) & 1
            high = (bits >> (2 * i + 1)) & 1
            here = coordinate(dp, axis) ^ (low * flip0) ^ (high * flip1)
            source = source + here * STRIDE[axis]
        tables.append((source[:, None] == bits[None, :]).astype(bf16))
    return jnp.stack(tables)


def plus(left, right):
    return (left.astype(f32) + right.astype(f32)).astype(bf16)


def choose(flag, when, otherwise):
    return jnp.where(flag, when, otherwise)


def tie(values, deps):
    flat = lax.optimization_barrier((*values, *deps))
    return list(flat[: len(values)]), list(flat[len(values) :])


def near_sends(pieces):
    return [pair_up(pieces[k], ORDERS[k][2], 0) for k in range(3)]


def far_sends(pieces):
    return [pair_up(pieces[k], ORDERS[k][2], 1) for k in range(3)]


def gather_step(bufs, small, t, kernel):
    n = bufs[0].shape[1]
    sends = [jnp.concatenate([bufs[0].reshape(4 * n, D), small]), bufs[1], bufs[2]]
    got = [pair_up(sends[k], ORDERS[k][t // 2], t % 2) for k in range(3)]
    (small, *bufs), (kernel,) = tie([small, *bufs], [kernel])
    small = small + got[0][4 * n :]
    got[0] = got[0][: 4 * n].reshape(4, n, D)
    return [jnp.concatenate([bufs[k], got[k]], axis=1) for k in range(3)], small, kernel


def reduce_parts(bufs, live, axis, step):
    which = [k for k in range(3) if axis in ORDERS[k][:2]]
    keeps, sends = [], []
    for k in which:
        place = live[k].index((axis, step))
        left = len(live[k])
        live[k] = [bit for bit in live[k] if bit != (axis, step)]
        v = bufs[k].reshape(4, 2**place, 2, 2 ** (left - place - 1), 8, D)
        keeps.append(v[:, :, 0].reshape(-1, 8, D))
        sends.append(v[:, :, 1].reshape(-1, 8, D))
    return which, keeps, jnp.concatenate(sends)


def reduce_sums(bufs, live, which, keeps, got):
    bufs = list(bufs)
    at = 0
    for k, keep in zip(which, keeps):
        total = keep.astype(f32) + got[at : at + keep.shape[0]].astype(f32)
        at += keep.shape[0]
        bufs[k] = (total if not live[k] else total.astype(bf16)).reshape(4, -1, 8, D)
    return bufs


def all_sum(mine, theirs, dp, core, rest, live):
    flip0 = choose(core == 0, FLIPS[0], FLIPS[1])
    flip1 = choose(core == 0, FLIPS[1], FLIPS[0])
    order = []
    for k in range(3):
        at = coordinate(dp, ORDERS[k][0])
        order += [at, at ^ flip1, at ^ flip0, at ^ flip0 ^ flip1]
    order = jnp.stack(order).astype(jnp.int32)
    outs = split_call(order, mine, swap_cores(theirs))
    keep, bufs = list(outs[0::2]), list(outs[1::2])
    first = [None] * 3
    steps = [("z", 0), ("y", 1), ("y", 0), ("x", 1), ("x", 0)]
    for t in range(8):
        axes = [ORDERS[k][(0, 0, 1, 1, 2, 2, 0, 0)[t]] for k in range(3)]
        swap = exchange if 2 <= t < 6 else pair_up
        got = [swap(bufs[k], axes[k], (0, 1, 0, 1, 0, 1, 1, 0)[t]) for k in range(3)]
        if t < len(steps):
            which, kept, sent = reduce_parts(rest, live, *steps[t])
            back = pair_up(sent, *steps[t])
        if t == 7:
            break
        for k in range(3):
            own = keep if t < 2 else bufs
            if t <= len(steps) and (t or k):
                if k:
                    (own[k],), (bufs[k - 1],) = tie([own[k]], [bufs[k - 1]])
                else:
                    (own[0],), (rest[last[0]],) = tie([own[0]], [rest[last[0]]])
            if t == 0:
                first[k] = got[k]
                bufs[k] = plus(keep[k][1], got[k][1])
            elif t == 1:
                total = keep[k][0].astype(f32) + first[k][0].astype(f32) + got[k].astype(f32)
                bufs[k] = total.astype(bf16)
            elif t < 6:
                bufs[k] = plus(bufs[k], got[k])
            else:
                bufs[k] = jnp.stack([bufs[k], got[k]])
        if t < len(steps):
            (back,), (bufs[2],) = tie([back], [bufs[2]])
            rest = reduce_sums(rest, live, which, kept, back)
            last = which
    mine = join_call(order, [v for k in range(3) for v in (bufs[k], got[k])])
    return (*assemble_call(jnp.stack([core, dp]).astype(jnp.int32), mine, swap_cores(mine)), rest)


def body(
    tokens,
    item_kind,
    cotangent,
    norm1_gain,
    norm1_shift,
    qkv_weight,
    query_bias,
    value_bias,
    out_weight,
    out_bias,
    norm2_gain,
    norm2_shift,
    ffn_in,
    ffn_in_bias,
    ffn_out,
    ffn_out_bias,
):
    dp = lax.axis_index("dp")
    core = lax.axis_index("expert")
    small = jnp.zeros((3, 2, 64, 12), bf16)
    mine = jnp.stack([norm2_gain, norm2_shift, ffn_out_bias]).reshape(3, 1, 1, 12)
    small = lax.dynamic_update_slice(small, mine, (0, core, dp, 0)).reshape(6, D)
    hidden_bias = lax.dynamic_update_slice(
        jnp.zeros((2, 64, 48), bf16), ffn_in_bias.reshape(1, 1, 48), (core, dp, 0)
    ).reshape(8, D)
    small = jnp.concatenate([small, hidden_bias, jnp.zeros((2, D), bf16)])

    shard = jnp.stack([ffn_in[0].T, ffn_out[0]]).reshape(2, 3, 2, 8, D)
    stay = choose(core == 0, shard[:, :, 0], shard[:, :, 1])
    leave = choose(core == 0, shard[:, :, 1], shard[:, :, 0])
    came = swap_cores(jnp.concatenate([leave.reshape(48, D), small]))
    kinds = item_kind.reshape(1, ITEMS_DEV)
    vectors = [norm1_gain, norm1_shift, query_bias, value_bias]
    (tokens,), (came,) = tie([tokens], [came])
    small = small + came[48:]
    came_w = came[:48].reshape(2, 3, 8, D)
    both = choose(core == 0, jnp.stack([stay, came_w]), jnp.stack([came_w, stay]))
    bufs = [both[:, :, k].reshape(4, 8, D) for k in range(3)]
    n1, triple, bias, lang = qkv_call(kinds, tokens, vectors, qkv_weight)
    other_kinds = swap_cores(kinds)
    other_cot = swap_cores(cotangent)
    bufs, small, n1 = gather_step(bufs, small, 0, n1)
    (triple,), bufs = tie([triple], bufs)
    ctx_a, lse_a = attend_call(triple, bias, 0, 3)
    bufs, small, ctx_a = gather_step(bufs, small, 1, ctx_a)
    (triple,), bufs = tie([triple], bufs)
    ctx_b, lse_b = attend_call(triple, bias, 3, 3)
    bufs, small, ctx_b = gather_step(bufs, small, 2, ctx_b)
    (ctx_b,), bufs = tie([ctx_b], bufs)
    hidden, routed = out_call(ctx_a, ctx_b, out_weight, out_bias, tokens)
    other_routed = swap_cores(routed)
    (other_kinds,), (routed,) = tie([other_kinds], [routed])
    select, up, nv = select_call(jnp.concatenate([kinds, other_kinds]), cotangent, other_cot)
    bufs, small, up = gather_step(bufs, small, 3, up)
    near = near_sends([jnp.concatenate([bufs[0].reshape(4 * PIECE, D), small]), bufs[1], bufs[2]])
    (select,), bufs = tie([select], bufs)
    rows = sort_call(select, routed, other_routed)
    (near[0],), (rows,) = tie([near[0]], [rows])
    small = small + near[0][4 * PIECE :]
    small = small + pair_up(small, "z", 1)
    pairs = [jnp.concatenate([bufs[0].reshape(4 * PIECE, D), near[0]])]
    for k in (1, 2):
        (near[k],), (pairs[-1],) = tie([near[k]], [pairs[-1]])
        pairs.append(jnp.concatenate([bufs[k], near[k]]))
    far = far_sends(pairs)

    hidden_bias = small[6:14].reshape(2, 64, 3, 2, 8)
    hidden_bias = choose(core == 0, hidden_bias[:, :, :, 0], hidden_bias[:, :, :, 1])
    table = relative_table(dp, core)
    spread = jnp.einsum("kps,esku->ekpu", table, hidden_bias, preferred_element_type=f32)
    hidden_bias = spread.reshape(2, 3, 2, 2 * PIECE).transpose(2, 0, 1, 3).reshape(2, 2, HALF_HID)

    pick = lambda a, b: [v for k in range(3) for v in (a[k], b[k])]
    (n2, branch, gn2, db0), dw0 = expert_call(nv, rows, up, hidden_bias[0], pick(bufs, near), small=small)
    (back_own, back_other, db1), dw1 = expert_call(
        nv, n2, up, hidden_bias[1], far, sums=(select, branch, gn2)
    )

    got0 = near_sends(dw0[1::2])
    dw1_own, dw1_near = list(dw1[0::2]), list(dw1[1::2])
    (back_other, *dw1_near), got0 = tie([back_other, *dw1_near], got0)
    back_recv = swap_cores(back_other)
    got = near_sends(dw1_near)
    mixed, gh, gctx, dw_out, delta, small_b = post_call(
        back_own, back_recv, hidden, cotangent, lang, small, out_weight, ctx_a, ctx_b
    )
    dw1_own, (gh,) = tie(dw1_own, [gh])
    send = [plus(dw1_own[k], got[k]) for k in range(3)]
    (triple,), send = tie([triple], send)
    got = far_sends(send)
    parts = list(attend_back_call(triple, gctx, lse_a, lse_b, delta, bias))
    dw0_own, (parts[0],) = tie(dw0[0::2], [parts[0]])
    bufs = [
        (dw0_own[k].astype(f32) + got0[k].astype(f32) + got[k].astype(f32)).astype(bf16) for k in range(3)
    ]
    live = [[(ORDERS[k][i], t) for i in (1, 0) for t in (1, 0)] for k in range(3)]
    (gh,), bufs = tie([gh], bufs)
    which, kept, sent = reduce_parts(bufs, live, "z", 1)
    (gh,), (sent,) = tie([gh], [sent])
    back = pair_up(sent, "z", 1)

    (db0,), (gh,) = tie([db0], [gh])
    db = jnp.stack([db0, db1]).reshape(2, 2, 3, 256).transpose(2, 0, 3, 1).reshape(3, 2, 32, 8, 2)
    db = db.reshape(3, 64, 8, 2).astype(bf16)
    db = jnp.einsum("kps,kpue->esku", table, db, preferred_element_type=f32)
    zero = jnp.zeros_like(db)
    db = choose(core == 0, jnp.stack([db, zero], 3), jnp.stack([zero, db], 3)).reshape(8, D)

    mine, theirs, tokens_grad = final_call(
        core.reshape(1), n1, tokens, norm1_gain, qkv_weight, gh, dw_out, small_b, db, parts
    )

    (theirs,), (back,) = tie([theirs], [back])
    bufs = reduce_sums(bufs, live, which, kept, back)
    grad_qkv, grad_out, vectors, mine, bias_grad, bufs = all_sum(mine, theirs, dp, core, bufs, live)
    shards = jnp.stack(bufs).reshape(3, 2, 2, 8, D)
    stay = choose(core == 0, shards[:, 0], shards[:, 1])
    leave = choose(core == 0, shards[:, 1], shards[:, 0])
    came = swap_cores(leave)
    full = choose(core == 0, jnp.stack([stay, came], 2), jnp.stack([came, stay], 2))
    full = full.transpose(1, 0, 2, 3, 4).reshape(2, 48, D)

    return (
        mixed,
        tokens_grad,
        vectors[0],
        vectors[1],
        grad_qkv,
        vectors[2],
        vectors[3],
        grad_out,
        vectors[4],
        mine[0],
        mine[1],
        full[0].T[None],
        bias_grad,
        full[1][None],
        mine[2],
    )


def solution(mesh):
    both = ("dp", "expert")
    in_specs = (
        P(both, None),
        P(both),
        P(both, None),
        P(),
        P(),
        P(),
        P(),
        P(),
        P(),
        P(),
        P("expert", "dp"),
        P("expert", "dp"),
        P("expert", None, "dp"),
        P("expert", "dp"),
        P("expert", "dp", None),
        P("expert", "dp"),
    )
    out_specs = (
        P(both, None),
        P(both, None),
        P(),
        P(),
        P(),
        P(),
        P(),
        P(),
        P(),
        P("expert", "dp"),
        P("expert", "dp"),
        P("expert", None, "dp"),
        P("expert", "dp"),
        P("expert", "dp", None),
        P("expert", "dp"),
    )
    return jax.shard_map(body, mesh=mesh, in_specs=in_specs, out_specs=out_specs, check_vma=False)
```

```python
import functools

import jax
import jax.numpy as jnp
from jax import lax
from jax.experimental import pallas as pl
from jax.experimental.pallas import tpu as pltpu
from jax.sharding import PartitionSpec as P

HEADS = 12
IMG_LEN = 197
TXT_LEN = 40
ROWS = 512
CHIP_ROWS = 1024
D = 768
FF = 3072
ITEMS_DEV = 13
PAIRS = HEADS // 2
LANES = 128
BLOCK = 256
MASKED = -1e30
EPS = 1e-5
PLANS = {
    "qkv": (20, False),
    "attend": (16, False),
    "outproj": (12, False),
    "select": (20, False),
    "sort": (12, False),
    "expert": (56, True),
    "post": (56, True),
    "attend_back": (56, False),
    "final": (56, True),
    "split": (16, False),
    "join": (12, False),
    "assemble": (24, False),
}
AR_ROWS = 3264
SMALL_ROWS = AR_ROWS - 4 * D
AR_PIECE = AR_ROWS // 12
HALF = D // 2

bf16 = jnp.bfloat16
f32 = jnp.float32


def dot(left, right):
    return jnp.dot(left, right, preferred_element_type=f32)


def dot_t(left, right):
    return lax.dot_general(left, right, (((1,), (1,)), ((), ())), preferred_element_type=f32)


def dot_0(left, right):
    return lax.dot_general(left, right, (((0,), (0,)), ((), ())), preferred_element_type=f32)


def params(mebibytes):
    return pltpu.CompilerParams(vmem_limit_bytes=mebibytes * 1024 * 1024)


def cost(flops, byts, trans=0):
    return pl.CostEstimate(flops=int(flops), bytes_accessed=int(byts), transcendentals=int(trans))


def shape(dims, dtype):
    return jax.ShapeDtypeStruct(dims, dtype)


VM = pl.BlockSpec(memory_space=pltpu.VMEM)
SM = pl.BlockSpec(memory_space=pltpu.SMEM)
HB = pl.BlockSpec(memory_space=pl.ANY)


def staged_call(
    body, name, smem, small, loads, outs, plain=(), scratch=(), flops=1e9, raw=(), cuts=None, out_cuts=None, first=()
):
    n_out = len(outs)
    limit, staged = PLANS[name]
    big = HB if staged else VM
    cuts, out_cuts = cuts or {}, out_cuts or {}

    def plain_kernel(*refs):
        at = len(smem) + len(small)
        s_refs, v_refs = refs[: len(smem)], refs[len(smem) : at]
        ins, rest = refs[at : at + len(loads)], refs[at + len(loads) :]
        results, extra = rest[: n_out + len(plain)], rest[n_out + len(plain) :]
        body(s_refs, v_refs, lambda i, c=None: ins[i], results, lambda j, c=None: None, extra)

    def part(ref, c, count, axis):
        if count == 1:
            return ref
        size = ref.shape[axis] // count
        return ref.at[(slice(None),) * axis + (pl.ds(c * size, size),)]

    def kernel(*refs):
        refs = list(refs)
        take = lambda n: [refs.pop(0) for _ in range(n)]
        s_refs, v_refs, hbm, raw_refs = take(len(smem)), take(len(small)), take(len(loads)), take(len(raw))
        out_hbm = take(n_out)
        plain_refs, bufs, out_bufs, extra = take(len(plain)), take(len(loads)), take(n_out), take(len(scratch))
        in_sem, out_sem = refs
        copies, sent = {}, []
        for i in range(len(loads)):
            count, axis = cuts.get(i, (1, 0))
            for c in range(count):
                pieces = part(hbm[i], c, count, axis), part(bufs[i], c, count, axis)
                copies[i, c] = pltpu.make_async_copy(*pieces, in_sem.at[len(copies)])
        for key in sorted(copies, key=lambda key: (key[1], key[0]) if key[0] in first else (99, key)):
            copies[key].start()

        def get(i, c=None):
            for key in [key for key in copies if key[0] == i and c in (None, key[1])]:
                copies.pop(key).wait()
            return bufs[i]

        def put(j, c=None):
            count, axis = out_cuts.get(j, (1, 0))
            for piece in range(count) if c is None else [c]:
                pieces = part(out_bufs[j], piece, count, axis), part(out_hbm[j], piece, count, axis)
                copy = pltpu.make_async_copy(*pieces, out_sem.at[len(sent)])
                copy.start()
                sent.append(copy)

        body(s_refs, v_refs, get, out_bufs + plain_refs, put, ([raw_refs] if raw else []) + extra)
        assert not copies
        for copy in sent:
            copy.wait()

    n_in = sum(cuts.get(i, (1, 0))[0] for i in range(len(loads)))
    n_sent = sum(out_cuts.get(j, (1, 0))[0] for j in range(n_out))
    bytes_moved = sum(v.size * v.dtype.itemsize for v in (*loads, *outs))
    buffers = [pltpu.VMEM(v.shape, v.dtype) for v in (*loads, *outs)] if staged else []
    sems = [pltpu.SemaphoreType.DMA((n_in,)), pltpu.SemaphoreType.DMA((max(n_sent, 1),))] if staged else []
    return pl.pallas_call(
        kernel if staged else plain_kernel,
        out_shape=(*outs, *(struct for struct, _ in plain)),
        in_specs=[SM] * len(smem) + [VM] * len(small) + [big] * len(loads) + [HB] * len(raw),
        out_specs=(big,) * n_out + tuple(spec for _, spec in plain),
        scratch_shapes=buffers + list(scratch) + sems,
        compiler_params=params(limit),
        cost_estimate=cost(flops, bytes_moved),
        name=name,
    )(*smem, *small, *loads, *raw)


def as_row(ref):
    return ref[...].astype(f32).reshape(1, D)


def norm_stats(x):
    centred = x - jnp.mean(x, axis=-1, keepdims=True)
    rstd = lax.rsqrt(jnp.mean(centred * centred, axis=-1, keepdims=True) + EPS)
    return centred * rstd, rstd


def item_lengths(kind):
    vision = jnp.where(kind == 1, 0, IMG_LEN)
    language = jnp.where(kind == 0, 0, TXT_LEN)
    return vision, language


def qkv_kernel(smem, small, get, outs, put, scratch):
    (kind_ref,) = smem
    n1_ref, tri_ref, bias_ref, lang_ref = outs
    gain, shift, q_bias, v_bias = (as_row(ref) for ref in small)
    tok_ref = get(0)
    for r in range(0, ROWS, LANES):
        xhat, _ = norm_stats(tok_ref[r : r + LANES, :].astype(f32))
        n1_ref[r : r + LANES, :] = (xhat * gain + shift).astype(bf16)
    put(0)
    n1 = n1_ref[...]
    w_ref = get(1)
    q = dot(n1, w_ref[:, 0:D]) + q_bias
    tri_ref[:, 0:D] = q.astype(bf16) * jnp.asarray(0.125, bf16)
    tri_ref[:, D : 2 * D] = dot(n1, w_ref[:, D : 2 * D]).astype(bf16)
    tri_ref[:, 2 * D :] = (dot(n1, w_ref[:, 2 * D :]) + v_bias).astype(bf16)
    put(1)
    down = lax.broadcasted_iota(jnp.int32, (ROWS, LANES), 0)
    across = lax.broadcasted_iota(jnp.int32, (8, ROWS), 1)
    item_down = jnp.zeros((ROWS, LANES), jnp.int32)
    item_across = jnp.zeros((8, ROWS), jnp.int32)
    lang = jnp.zeros((ROWS, LANES), f32)
    start = 0
    for i in range(ITEMS_DEV):
        vision, language = item_lengths(kind_ref[0, i])
        middle = start + vision
        end = middle + language
        item_down += (down >= end).astype(jnp.int32)
        item_across += (across >= end).astype(jnp.int32)
        lang = jnp.where((down >= middle) & (down < end), 1.0, lang)
        start = end
    lang_ref[...] = lang
    put(3)
    for c in range(0, ROWS, LANES):
        same = item_down == item_across[0:1, c : c + LANES]
        bias_ref[:, c : c + LANES] = jnp.where(same, 0.0, MASKED)
    put(2)


def qkv_call(kinds, tokens, vectors, weight):
    outs = (shape((ROWS, D), bf16), shape((ROWS, 3 * D), bf16), shape((ROWS, ROWS), f32), shape((ROWS, LANES), f32))
    return staged_call(qkv_kernel, "qkv", [kinds], vectors, [tokens, weight], outs, flops=2 * ROWS * D * 3 * D * 2)


def half_lanes(head):
    lane = lax.broadcasted_iota(jnp.int32, (1, LANES), 1)
    return (lane < LANES // 2) if head == 0 else (lane >= LANES // 2)


def attend_kernel(q_ref, k_ref, v_ref, bias_ref, ctx_ref, lse_ref):
    q, k, v = q_ref[...], k_ref[...], v_ref[...]
    zero = jnp.zeros_like(q)
    rows = lax.broadcasted_iota(jnp.int32, (LANES, 1), 0)
    parts = []
    for head in range(2):
        qm = jnp.where(half_lanes(head), q, zero)
        s = dot_t(k, qm) + bias_ref[...]
        top = jnp.max(s, axis=0, keepdims=True)
        e = jnp.exp(s - top)
        total = jnp.sum(e, axis=0, keepdims=True)
        lse_ref[0, head : head + 1, :] = top + jnp.log(total)
        parts.append(dot_0(v, e.astype(bf16)) * (1.0 / total))
    ctx = jnp.where(rows < LANES // 2, parts[0], parts[1])
    ctx_ref[...] = ctx.T.astype(bf16)


def attend_call(triple, bias, first, count):
    def col(offset):
        return pl.BlockSpec((ROWS, LANES), lambda p: (0, offset + first + p))

    return pl.pallas_call(
        attend_kernel,
        grid=(count,),
        out_shape=(shape((ROWS, count * LANES), bf16), shape((count, 8, ROWS), f32)),
        in_specs=[col(0), col(PAIRS), col(2 * PAIRS), pl.BlockSpec((ROWS, ROWS), lambda p: (0, 0))],
        out_specs=(
            pl.BlockSpec((ROWS, LANES), lambda p: (0, p)),
            pl.BlockSpec((1, 8, ROWS), lambda p: (p, 0, 0)),
        ),
        compiler_params=params(PLANS["attend"][0]),
        cost_estimate=cost(count * 2 * 4e9, count * 6e6),
        name="attend",
    )(triple, triple, triple, bias)


def out_kernel(smem, small, get, outs, put, scratch):
    hid_ref, routed_ref = outs
    half = D // 2
    ca_ref, cb_ref, w_ref = get(0), get(1), get(2)
    h = dot(ca_ref[...], w_ref[:half, :]) + dot(cb_ref[...], w_ref[half:, :])
    h = get(3)[...].astype(f32) + h + as_row(small[0])
    routed_ref[...] = h.astype(bf16)
    put(1)
    hid_ref[...] = h
    put(0)


def out_call(ctx_a, ctx_b, weight, bias, tokens):
    outs = (shape((ROWS, D), f32), shape((ROWS, D), bf16))
    return staged_call(
        out_kernel, "outproj", [], [bias], [ctx_a, ctx_b, weight, tokens], outs, flops=2 * ROWS * D * D * 2
    )


def select_kernel(smem, small, get, outs, put, scratch):
    (kind_ref,) = smem
    sel_ref, up_ref, nv_ref = outs
    spans = []
    vision_total = 0
    for pack in range(2):
        start = 0
        for i in range(ITEMS_DEV):
            vision, language = item_lengths(kind_ref[pack, i])
            first = jnp.minimum(start, ROWS)
            middle = jnp.minimum(start + vision, ROWS)
            end = jnp.minimum(start + vision + language, ROWS)
            spans.append((pack, first, middle, end))
            vision_total = vision_total + middle - first
            start = start + vision + language
    nv_ref[0] = vision_total
    place = lax.broadcasted_iota(jnp.int32, (1, ROWS), 1)
    target = [jnp.zeros((1, ROWS), jnp.int32) for _ in range(2)]
    at_vision, at_language = 0, vision_total
    for pack, first, middle, end in spans:
        t = target[pack]
        t = jnp.where((place >= first) & (place < middle), place + (at_vision - first), t)
        t = jnp.where((place >= middle) & (place < end), place + (at_language - middle), t)
        target[pack] = t
        at_vision = at_vision + middle - first
        at_language = at_language + end - middle
    own, other = get(0)[...], get(1)[...]
    for r in range(0, CHIP_ROWS, BLOCK):
        down = lax.broadcasted_iota(jnp.int32, (BLOCK, ROWS), 0) + r
        for pack in range(2):
            sel_ref[r : r + BLOCK, pack * ROWS : (pack + 1) * ROWS] = (
                (down == target[pack]).astype(f32).astype(bf16)
            )
        up_ref[r : r + BLOCK, :] = (
            dot(sel_ref[r : r + BLOCK, :ROWS], own) + dot(sel_ref[r : r + BLOCK, ROWS:], other)
        ).astype(bf16)
    put(0)
    put(1)


def select_call(kinds, own, other):
    square = shape((CHIP_ROWS, CHIP_ROWS), bf16)
    outs = (square, shape((CHIP_ROWS, D), bf16))
    plain = ((shape((1,), jnp.int32), SM),)
    flops = 2 * 2 * CHIP_ROWS * CHIP_ROWS * D
    return staged_call(select_kernel, "select", [kinds], [], [own, other], outs, plain, flops=flops)


def sort_kernel(smem, small, get, outs, put, scratch):
    sel_ref = get(0)
    own, other = get(1)[...], get(2)[...]
    for r in range(0, CHIP_ROWS, BLOCK):
        x = dot(sel_ref[r : r + BLOCK, :ROWS], own) + dot(sel_ref[r : r + BLOCK, ROWS:], other)
        outs[0][r : r + BLOCK, :] = x.astype(bf16)
    put(0)


def sort_call(select, own, other):
    return staged_call(
        sort_kernel,
        "sort",
        [],
        [],
        [select, own, other],
        (shape((CHIP_ROWS, D), bf16),),
        flops=2 * CHIP_ROWS * CHIP_ROWS * D,
    )[0]


def gelu_parts(x):
    t = 1.0 / (1.0 + 0.2316418882663604 * jnp.abs(x))
    poly = 0.127414796 + t * (-0.142248368 + t * (0.7107068705 + t * (-0.7265760135 + t * 0.5307027145)))
    bell = jnp.exp2(x * x * -0.7213475204444817)
    tail = t * poly * bell
    phi = jnp.where(x >= 0, 1.0 - tail, tail)
    return x * phi, phi + (x * 0.3989422804014327) * bell


THIRDS = 3
PIECE = 128
HALF_HID = THIRDS * 2 * PIECE


def expert_kernel(first, smem, small, get, outs, put, scratch):
    (nv_ref,), bias_ref = smem, small[0]
    w_hbm, scratch = scratch[0], scratch[1:]
    if first:
        n2_ref, *sums_hbm, db_ref = outs[:4]
        dw_hbm = outs[4:]
    else:
        own_ref, other_ref, db_ref = outs[:3]
        dw_hbm = outs[3:]
    branch_ref, gn2_ref, sum_sem, scratch = scratch[0], scratch[1], scratch[2], scratch[3:]
    w_ref, acc_ref, out_ref, act_ref, gp_ref, in_sem, out_sem = scratch
    loads = [], []
    for k in range(THIRDS):
        for j in range(2):
            at = k * 2 * PIECE + j * PIECE
            ref = w_hbm[2 * k + j if first else k]
            for m in range(4):
                block = m if first else 4 * j + m
                part = ref.at[block] if len(ref.shape) == 3 else ref.at[pl.ds(block * PIECE, PIECE), :]
                copy = pltpu.make_async_copy(
                    part, w_ref.at[m, pl.ds(at, PIECE), :], in_sem.at[8 * k + 4 * j + m]
                )
                loads[m // 2].append(copy)
    for copy in loads[0] + loads[1]:
        copy.start()
    branch_ref[...] = jnp.zeros_like(branch_ref)
    gn2_ref[...] = jnp.zeros_like(gn2_ref)
    x_ref = get(0)
    if first:
        par = small[1][...].astype(f32)
        for r in range(0, CHIP_ROWS, LANES):
            xhat, _ = norm_stats(x_ref[r : r + LANES, :].astype(f32))
            vision = (lax.broadcasted_iota(jnp.int32, (LANES, 1), 0) + r) < nv_ref[0]
            gain = jnp.where(vision, par[0:1, :], par[1:2, :])
            shift = jnp.where(vision, par[2:3, :], par[3:4, :])
            n2_ref[r : r + LANES, :] = (xhat * gain + shift).astype(bf16)
        put(0)
    else:
        n2_ref = x_ref
    up_ref = get(1)
    db_ref[...] = jnp.zeros_like(db_ref)
    nv = nv_ref[0]
    stores = []
    for e in range(2):
        for copy in loads[e]:
            copy.wait()
        low = jnp.int32(0) if e == 0 else nv // BLOCK
        high = (nv + BLOCK - 1) // BLOCK if e == 0 else jnp.int32(CHIP_ROWS // BLOCK)
        acc_ref[...] = jnp.zeros_like(acc_ref)

        def visit(block, size, e=e):
            at = pl.multiple_of(block * BLOCK, BLOCK)
            rows = pl.ds(at, size)
            index = lax.broadcasted_iota(jnp.int32, (size, 1), 0) + at
            valid = (index < nv) if e == 0 else (index >= nv)
            n2 = n2_ref[rows, :]
            up = up_ref[rows, :]
            for k in range(THIRDS):
                hid = slice(k * BLOCK, (k + 1) * BLOCK)
                pre = dot_t(n2, w_ref[2 * e, hid, :]) + bias_ref[e : e + 1, hid].astype(f32)
                back = dot_t(up, w_ref[2 * e + 1, hid, :])
                active, slope = gelu_parts(pre)
                act = jnp.where(valid, active, 0.0).astype(bf16)
                gp = jnp.where(valid, back * slope, 0.0).astype(bf16)
                act_ref[:size, hid] = act
                gp_ref[:size, hid] = gp
                db_ref[e : e + 1, hid] += jnp.sum(gp.astype(f32), axis=0, keepdims=True)
            acc_ref[0] += dot_0(gp_ref[:size, :], n2)
            acc_ref[1] += dot_0(act_ref[:size, :], up)
            branch_ref[rows, :] += dot(act_ref[:size, :], w_ref[2 * e + 1])
            gn2_ref[rows, :] += dot(gp_ref[:size, :], w_ref[2 * e])
            if not first:
                return
            for b in range(size // BLOCK):
                done = pl.ds(pl.multiple_of(at + b * BLOCK, BLOCK), BLOCK)

                @pl.when((at + (b + 1) * BLOCK <= nv) if e == 0 else (at >= 0))
                def _(done=done):
                    for i, ref in enumerate((branch_ref, gn2_ref)):
                        pltpu.make_async_copy(ref.at[done, :], sums_hbm[i].at[done, :], sum_sem.at[i]).start()

        count = high - low

        def two(i, carry, visit=visit, low=low):
            visit(low + 2 * i, 2 * BLOCK)
            return carry

        lax.fori_loop(0, count // 2, two, 0)

        @pl.when(count % 2 == 1)
        def _(visit=visit, high=high):
            visit(high - 1, BLOCK)

        out_ref[2 * e] = acc_ref[0].astype(bf16)
        out_ref[2 * e + 1] = acc_ref[1].astype(bf16)
        for k in range(THIRDS):
            for j in range(2):
                at = k * 2 * PIECE + j * PIECE
                copy = pltpu.make_async_copy(
                    out_ref.at[pl.ds(2 * e, 2), pl.ds(at, PIECE), :],
                    dw_hbm[2 * k + j].at[pl.ds(2 * e, 2)],
                    out_sem.at[6 * e + 2 * k + j],
                )
                copy.start()
                stores.append(copy)
    if first:
        for i, ref in enumerate((branch_ref, gn2_ref)):
            pltpu.make_async_copy(ref, sums_hbm[i], sum_sem.at[i]).wait()
    else:
        sel_ref = get(2)
        for i, total in enumerate((branch_ref, gn2_ref)):
            y = (get(3 + i)[...] + total[...]).astype(bf16)
            other_ref[i] = dot_0(sel_ref[:, ROWS:], y).astype(bf16)
            own_ref[i] = dot_0(sel_ref[:, :ROWS], y).astype(bf16)
        put(1)
        put(0)
    for copy in stores:
        copy.wait()


def expert_call(nv, rows, up, bias, weights, small=None, sums=None):
    first = sums is None
    db = (shape((2, HALF_HID), f32), VM)
    part = shape((CHIP_ROWS, D), f32)
    back = shape((2, ROWS, D), bf16)
    pieces = ((shape((4, PIECE, D), bf16), HB),) * 6
    work = [
        pltpu.VMEM((CHIP_ROWS, D), f32),
        pltpu.VMEM((CHIP_ROWS, D), f32),
        pltpu.SemaphoreType.DMA((2,)),
        pltpu.VMEM((4, HALF_HID, D), bf16),
        pltpu.VMEM((2, HALF_HID, D), f32),
        pltpu.VMEM((4, HALF_HID, D), bf16),
        pltpu.VMEM((2 * BLOCK, HALF_HID), bf16),
        pltpu.VMEM((2 * BLOCK, HALF_HID), bf16),
        pltpu.SemaphoreType.DMA((24,)),
        pltpu.SemaphoreType.DMA((12,)),
    ]
    if first:
        outs = staged_call(
            functools.partial(expert_kernel, True), "expert", [nv], [bias, small], [rows, up],
            (shape((CHIP_ROWS, D), bf16),), ((part, HB), (part, HB), db, *pieces), work, 20e9, raw=weights,
        )
    else:
        outs = staged_call(
            functools.partial(expert_kernel, False), "expert", [nv], [bias], [rows, up, *sums],
            (back, back), (db, *pieces), work, 20e9, raw=weights,
        )
    return outs[:-6], outs[-6:]


def post_kernel(smem, small, get, outs, put, scratch):
    mixed_ref, gh_ref, gctx_ref, dw_ref, delta_ref, small_ref = outs
    g_ref, prod_ref = scratch
    par = small[0][...].astype(f32)
    gains, bouts = par[0:2, :], par[4:6, :]
    small_ref[...] = jnp.zeros_like(small_ref)
    for r in range(0, ROWS, LANES):
        rows = slice(r, r + LANES)
        own_ref, recv_ref, hid_ref, cot_ref, lang_ref = (get(i, r // LANES) for i in range(5))
        lang = lang_ref[rows, 0:1]
        is_lang = lang > 0.5
        branch = own_ref[0, rows, :].astype(f32) + recv_ref[0, rows, :].astype(f32)
        branch = branch + jnp.where(is_lang, bouts[1:2, :], bouts[0:1, :])
        mixed_ref[rows, :] = (hid_ref[rows, :] + branch.astype(bf16).astype(f32)).astype(bf16)
        gn2 = own_ref[1, rows, :].astype(f32) + recv_ref[1, rows, :].astype(f32)
        xhat, rstd = norm_stats(hid_ref[rows, :].astype(bf16).astype(f32))
        gg = gn2 * jnp.where(is_lang, gains[1:2, :], gains[0:1, :])
        mean_a = jnp.mean(gg, axis=-1, keepdims=True)
        mean_b = jnp.mean(gg * xhat, axis=-1, keepdims=True)
        grad_routed = (rstd * (gg - mean_a - xhat * mean_b)).astype(bf16).astype(f32)
        cot = cot_ref[rows, :].astype(f32)
        gh = cot + grad_routed
        gh_ref[rows, :] = gh
        put(0, r // LANES)
        put(1, r // LANES)
        g_ref[rows, :] = gh.astype(bf16)
        prod = gn2 * xhat
        for i, (value, mask) in enumerate(((gh, None), (prod, 0), (prod, 1), (gn2, 0), (gn2, 1), (cot, 0), (cot, 1))):
            if mask is not None:
                value = jnp.where(is_lang, value, 0.0) if mask == 1 else jnp.where(is_lang, 0.0, value)
            small_ref[i : i + 1, :] += jnp.sum(value, axis=0, keepdims=True)
    g = g_ref[...]
    half = D // 2
    w_ref, ca_ref, cb_ref = get(5), get(6), get(7)
    dw_ref[:half, :] = dot_0(ca_ref[...], g).astype(bf16)
    dw_ref[half:, :] = dot_0(cb_ref[...], g).astype(bf16)
    put(3)
    gctx_ref[...] = dot_t(g, w_ref[...]).astype(bf16)
    put(2)
    prod_ref[:, :half] = gctx_ref[:, :half].astype(f32) * ca_ref[...].astype(f32)
    prod_ref[:, half:] = gctx_ref[:, half:].astype(f32) * cb_ref[...].astype(f32)
    head = lax.broadcasted_iota(jnp.int32, (16, D), 0)
    lane = lax.broadcasted_iota(jnp.int32, (16, D), 1)
    pick = (lane // 64 == head).astype(f32).astype(bf16)
    prod = prod_ref[...]
    upper = prod.astype(bf16)
    lower = (prod - upper.astype(f32)).astype(bf16)
    delta = dot_t(pick, upper) + dot_t(pick, lower)
    delta_ref[...] = jnp.zeros_like(delta_ref)
    for h in range(HEADS):
        delta_ref[h // 2, h % 2 : h % 2 + 1, :] = delta[h : h + 1, :]


def post_call(own, recv, hidden, cot, lang, small, weight, ctx_a, ctx_b):
    rows = shape((ROWS, D), bf16)
    outs = (rows, shape((ROWS, D), f32), rows, shape((D, D), bf16))
    plain = ((shape((PAIRS, 8, ROWS), f32), VM), (shape((8, D), f32), VM))
    work = [pltpu.VMEM((ROWS, D), bf16), pltpu.VMEM((ROWS, D), f32)]
    loads = [own, recv, hidden, cot, lang, weight, ctx_a, ctx_b]
    cuts = {0: (4, 1), 1: (4, 1), 2: (4, 0), 3: (4, 0), 4: (4, 0)}
    return staged_call(
        post_kernel, "post", [], [small], loads, outs, plain, work, 6e9,
        cuts=cuts, out_cuts={0: (4, 0), 1: (4, 0)}, first=range(5),
    )


def attend_back_kernel(q_ref, k_ref, v_ref, g_ref, lse_a, lse_b, delta_ref, bias_ref, dq_ref, dk_ref, dv_ref):
    q, k, v, g = q_ref[...], k_ref[...], v_ref[...], g_ref[...]
    zero = jnp.zeros_like(q)
    lse = jnp.where(pl.program_id(0) < PAIRS // 2, lse_a[0], lse_b[0])
    parts = []
    dk = dv = 0.0
    for c in range(0, ROWS, BLOCK):
        cols = slice(c, c + BLOCK)
        dq = 0.0
        for head in range(2):
            lanes = half_lanes(head)
            qm, gm = (jnp.where(lanes, x[cols, :], zero[cols, :]) for x in (q, g))
            km = jnp.where(lanes, k, zero)
            s = dot_t(k, qm) + bias_ref[:, cols]
            p = jnp.exp(s - lse[head : head + 1, cols])
            dp = dot_t(v, gm)
            ds = (p * (dp - delta_ref[0, head : head + 1, cols])).astype(bf16)
            dv = dv + dot(p.astype(bf16), gm)
            dk = dk + dot(ds, qm)
            dq = dq + dot_0(ds, km)
        parts.append(dq)
    dq = jnp.concatenate(parts, axis=0)
    dq_ref[...] = (dq * 0.125).astype(bf16)
    dk_ref[...] = dk.astype(bf16)
    dv_ref[...] = dv.astype(bf16)


def attend_back_call(triple, gctx, lse_a, lse_b, delta, bias):
    def col(offset):
        return pl.BlockSpec((ROWS, LANES), lambda p: (0, offset + p))

    half = PAIRS // 2
    return pl.pallas_call(
        attend_back_kernel,
        grid=(PAIRS,),
        out_shape=(shape((ROWS, D), bf16),) * 3,
        in_specs=[
            col(0),
            col(PAIRS),
            col(2 * PAIRS),
            col(0),
            pl.BlockSpec((1, 8, ROWS), lambda p: (jnp.minimum(p, half - 1), 0, 0)),
            pl.BlockSpec((1, 8, ROWS), lambda p: (jnp.maximum(p - half, 0), 0, 0)),
            pl.BlockSpec((1, 8, ROWS), lambda p: (p, 0, 0)),
            pl.BlockSpec((ROWS, ROWS), lambda p: (0, 0)),
        ],
        out_specs=(col(0),) * 3,
        compiler_params=params(PLANS["attend_back"][0]),
        cost_estimate=cost(20e9, 10e6),
        name="attend_back",
    )(triple, triple, triple, gctx, lse_a, lse_b, delta, bias)


def final_kernel(smem, small, get, outs, put, scratch):
    (core_ref,), (gain_ref, sb_ref, db_ref) = smem, small
    out_ref, *targets = outs
    gn_ref, small_ref, buf_ref, rows_ref, sem = scratch
    core = core_ref[0]
    lanes = [pl.ds(pl.multiple_of(h * HALF, LANES), HALF) for h in (core, 1 - core)]
    sent = []

    def send(source, t, at, size):
        copy = pltpu.make_async_copy(source, targets[t].at[pl.ds(at, size), :], sem.at[len(sent)])
        copy.start()
        sent.append(copy)

    small_ref[...] = jnp.zeros_like(small_ref)
    n1 = get(0)[...]
    for t in (1, 0):
        for i in range(3):
            buf_ref[t, i * D : (i + 1) * D, :] = dot_0(n1, get(1 + i)[:, lanes[t]]).astype(bf16)
            send(buf_ref.at[t, pl.ds(i * D, D), :], t, i * D, D)
        if t == 0:
            break
        for i in range(3):
            piece = get(1 + i)[...]
            part = dot_t(piece, get(4)[:, i * D : (i + 1) * D])
            if i == 0:
                gn_ref[...] = part
            else:
                gn_ref[...] += part
            if i != 1:
                small_ref[2 + i // 2 : 3 + i // 2, :] = jnp.sum(piece.astype(f32), axis=0, keepdims=True)
    gain = as_row(gain_ref)
    for r in range(0, ROWS, LANES):
        rows = slice(r, r + LANES)
        tok_ref, gh_ref = get(5, r // LANES), get(6, r // LANES)
        xhat, rstd = norm_stats(tok_ref[rows, :].astype(f32))
        gn = gn_ref[rows, :]
        small_ref[0:1, :] += jnp.sum(gn * xhat, axis=0, keepdims=True)
        small_ref[1:2, :] += jnp.sum(gn, axis=0, keepdims=True)
        gg = gn * gain
        mean_a = jnp.mean(gg, axis=-1, keepdims=True)
        mean_b = jnp.mean(gg * xhat, axis=-1, keepdims=True)
        out_ref[rows, :] = gh_ref[rows, :] + rstd * (gg - mean_a - xhat * mean_b)
        put(0, r // LANES)
    small_ref[8:16, :] = sb_ref[...]
    small_ref[16:24, :] = db_ref[...]
    for t in (1, 0):
        rows_ref[t] = small_ref[:, lanes[t]].astype(bf16)
        send(rows_ref.at[t], t, 4 * D, SMALL_ROWS)
    for t in (1, 0):
        buf_ref[t, 3 * D : 4 * D, :] = get(7)[:, lanes[t]]
        send(buf_ref.at[t, pl.ds(3 * D, D), :], t, 3 * D, D)
    for copy in sent:
        copy.wait()


def final_call(core, n1, tokens, gain, weight, gh, dw_out, small_b, db, parts):
    half = shape((AR_ROWS, HALF), bf16)
    work = [
        pltpu.VMEM((ROWS, D), f32),
        pltpu.VMEM((SMALL_ROWS, D), f32),
        pltpu.VMEM((2, 4 * D, HALF), bf16),
        pltpu.VMEM((2, SMALL_ROWS, HALF), bf16),
        pltpu.SemaphoreType.DMA((10,)),
    ]
    loads = [n1, *parts, weight, tokens, gh, dw_out]
    out, mine, theirs = staged_call(
        final_kernel, "final", [core], [gain, small_b, db], loads, (shape((ROWS, D), f32),),
        ((half, HB), (half, HB)), work, 2 * 2 * 2 * ROWS * D * 3 * D,
        cuts={5: (4, 0), 6: (4, 0)}, out_cuts={0: (4, 0)},
    )
    return mine, theirs, out


def split_kernel(order_ref, mine_ref, got_ref, *outs):
    for k in range(THIRDS):
        for i in range(4):
            rows = pl.ds(pl.multiple_of(k * 4 * AR_PIECE + order_ref[4 * k + i] * AR_PIECE, 16), AR_PIECE)
            total = mine_ref[rows, :].astype(f32) + got_ref[rows, :].astype(f32)
            outs[2 * k + i // 2][i % 2] = total.astype(bf16)


def split_call(order, mine, got):
    return pl.pallas_call(
        split_kernel,
        out_shape=(shape((2, AR_PIECE, HALF), bf16),) * 6,
        in_specs=[SM, VM, VM],
        out_specs=(VM,) * 6,
        compiler_params=params(PLANS["split"][0]),
        cost_estimate=cost(3e6, 8e6),
        name="split",
    )(order, mine, got)


def join_kernel(order_ref, *refs):
    out_ref = refs[-1]
    for k in range(THIRDS):
        for i in range(4):
            rows = pl.ds(pl.multiple_of(k * 4 * AR_PIECE + order_ref[4 * k + i] * AR_PIECE, 16), AR_PIECE)
            out_ref[rows, :] = refs[2 * k + i // 2][i % 2]


def join_call(order, pieces):
    return pl.pallas_call(
        join_kernel,
        out_shape=shape((AR_ROWS, HALF), bf16),
        in_specs=[SM] + [VM] * 6,
        out_specs=VM,
        compiler_params=params(PLANS["join"][0]),
        cost_estimate=cost(3e6, 5e6),
        name="join",
    )(order, *pieces)


def assemble_kernel(place_ref, *refs):
    ins, (qkv_ref, out_ref), vectors, shards, bias_ref = refs[:10], refs[10:12], refs[12:17], refs[17:20], refs[20]
    core, dp = place_ref[0], place_ref[1]
    zero = core == 0

    def halves(i):
        mine, theirs = ins[2 * i][...].astype(f32), ins[2 * i + 1][...].astype(f32)
        return jnp.where(zero, mine, theirs), jnp.where(zero, theirs, mine)

    for i in range(4):
        for j, value in enumerate(halves(i)):
            if i < 3:
                qkv_ref[:, i * D + j * HALF : i * D + (j + 1) * HALF] = value
            else:
                out_ref[:, j * HALF : (j + 1) * HALF] = value

    @pl.when(pl.program_id(0) == 0)
    def _():
        rows = jnp.concatenate([value[:24, :] for value in halves(4)], axis=1)
        for ref, r in zip(vectors, (0, 1, 2, 3, 8)):
            ref[...] = rows[r : r + 1, :].reshape(D)
        down = lax.broadcasted_iota(jnp.int32, (D, LANES), 0)
        lane = lax.broadcasted_iota(jnp.int32, (D, LANES), 1)

        def pick(offset):
            return dot(rows.astype(bf16), (down - offset == lane).astype(f32).astype(bf16))

        norms = pick(12 * dp)
        for i, ref in enumerate(shards):
            both = norms[9 + 2 * i : 11 + 2 * i, :12]
            ref[...] = jnp.where(zero, both[0:1, :], both[1:2, :])
        biases = pick(48 * (dp % 16))
        at = lax.broadcasted_iota(jnp.int32, (24, LANES), 0)
        here = jnp.where(at == 16 + 4 * core + dp // 16, biases, 0.0)
        bias_ref[...] = jnp.sum(here, axis=0, keepdims=True)[:, :48]


def assemble_call(place, mine, theirs):
    step = SMALL_ROWS
    specs, args = [], []
    for i in range(5):
        for ref in (mine, theirs):
            specs.append(pl.BlockSpec((step, HALF), (lambda r, i=i: (4 * i + r, 0)) if i < 4 else (lambda r: (16, 0))))
            args.append(ref)
    outs = pl.pallas_call(
        assemble_kernel,
        grid=(D // step,),
        out_shape=(shape((D, 3 * D), f32), shape((D, D), f32))
        + (shape((D,), f32),) * 5
        + (shape((1, 12), f32),) * 3
        + (shape((1, 48), f32),),
        in_specs=[SM] + specs,
        out_specs=(
            pl.BlockSpec((step, 3 * D), lambda r: (r, 0)),
            pl.BlockSpec((step, D), lambda r: (r, 0)),
        )
        + (VM,) * 9,
        compiler_params=params(PLANS["assemble"][0]),
        cost_estimate=cost(3e6, 15e6),
        name="assemble",
    )(place, *args)
    return outs[0], outs[1], outs[2:7], outs[7:10], outs[10]


AXES = ("y", "x", "z")
STRIDE = {"y": 16, "x": 4, "z": 1}
ORDERS = (("x", "y", "z"), ("y", "z", "x"), ("z", "x", "y"))
FLIPS = (1, 3)


def coordinate(index, axis):
    return (index // STRIDE[axis]) % 4


def pair_up(values, axis, step):
    pairs = []
    for dp in range(64):
        for core in range(2):
            place = coordinate(dp, axis)
            flip = FLIPS[step ^ core]
            other = dp + ((place ^ flip) - place) * STRIDE[axis]
            pairs.append((2 * dp + core, 2 * other + core))
    return lax.ppermute(values, ("dp", "expert"), pairs)


def exchange(values, axis, step):
    pairs = []
    for dp in range(64):
        for core in range(2):
            place = coordinate(dp, axis)
            other = dp + ((place ^ FLIPS[step]) - place) * STRIDE[axis]
            pairs.append((2 * dp + core, 2 * other + core))
    return lax.ppermute(values, ("dp", "expert"), pairs)


def swap_cores(values):
    return lax.ppermute(values, "expert", [(0, 1), (1, 0)])


def relative_table(dp, core):
    bits = lax.iota(jnp.int32, 64)
    flip0 = jnp.where(core == 0, FLIPS[0], FLIPS[1])
    flip1 = jnp.where(core == 0, FLIPS[1], FLIPS[0])
    tables = []
    for order in ORDERS:
        source = jnp.zeros((64,), jnp.int32)
        for i, axis in enumerate(order):
            low = (bits >> (2 * i)) & 1
            high = (bits >> (2 * i + 1)) & 1
            here = coordinate(dp, axis) ^ (low * flip0) ^ (high * flip1)
            source = source + here * STRIDE[axis]
        tables.append((source[:, None] == bits[None, :]).astype(bf16))
    return jnp.stack(tables)


def plus(left, right):
    return (left.astype(f32) + right.astype(f32)).astype(bf16)


def choose(flag, when, otherwise):
    return jnp.where(flag, when, otherwise)


def tie(values, deps):
    flat = lax.optimization_barrier((*values, *deps))
    return list(flat[: len(values)]), list(flat[len(values) :])


def near_sends(pieces):
    return [pair_up(pieces[k], ORDERS[k][2], 0) for k in range(3)]


def far_sends(pieces):
    return [pair_up(pieces[k], ORDERS[k][2], 1) for k in range(3)]


def gather_step(bufs, small, t, kernel):
    n = bufs[0].shape[1]
    sends = [jnp.concatenate([bufs[0].reshape(4 * n, D), small]), bufs[1], bufs[2]]
    got = [pair_up(sends[k], ORDERS[k][t // 2], t % 2) for k in range(3)]
    (small, *bufs), (kernel,) = tie([small, *bufs], [kernel])
    small = small + got[0][4 * n :]
    got[0] = got[0][: 4 * n].reshape(4, n, D)
    return [jnp.concatenate([bufs[k], got[k]], axis=1) for k in range(3)], small, kernel


def reduce_parts(bufs, live, axis, step):
    which = [k for k in range(3) if axis in ORDERS[k][:2]]
    keeps, sends = [], []
    for k in which:
        place = live[k].index((axis, step))
        left = len(live[k])
        live[k] = [bit for bit in live[k] if bit != (axis, step)]
        v = bufs[k].reshape(4, 2**place, 2, 2 ** (left - place - 1), 8, D)
        keeps.append(v[:, :, 0].reshape(-1, 8, D))
        sends.append(v[:, :, 1].reshape(-1, 8, D))
    return which, keeps, jnp.concatenate(sends)


def reduce_sums(bufs, live, which, keeps, got):
    bufs = list(bufs)
    at = 0
    for k, keep in zip(which, keeps):
        total = keep.astype(f32) + got[at : at + keep.shape[0]].astype(f32)
        at += keep.shape[0]
        bufs[k] = (total if not live[k] else total.astype(bf16)).reshape(4, -1, 8, D)
    return bufs


def all_sum(mine, theirs, dp, core, rest, live):
    flip0, flip1 = FLIPS
    order = []
    for k in range(3):
        at = coordinate(dp, ORDERS[k][0])
        order += [at, at ^ flip1, at ^ flip0, at ^ flip0 ^ flip1]
    order = jnp.stack(order).astype(jnp.int32)
    outs = split_call(order, mine, swap_cores(theirs))
    keep, bufs = list(outs[0::2]), list(outs[1::2])
    first = [None] * 3
    steps = [("z", 0), ("y", 1), ("y", 0), ("x", 1), ("x", 0)]
    for t in range(8):
        axes = [ORDERS[k][(0, 0, 1, 1, 2, 2, 0, 0)[t]] for k in range(3)]
        got = [exchange(bufs[k], axes[k], (0, 1, 0, 1, 0, 1, 1, 0)[t]) for k in range(3)]
        if t < len(steps):
            which, kept, sent = reduce_parts(rest, live, *steps[t])
            back = pair_up(sent, *steps[t])
        if t == 7:
            break
        for k in range(3):
            own = keep if t < 2 else bufs
            if t <= len(steps) and (t or k):
                if k:
                    (own[k],), (bufs[k - 1],) = tie([own[k]], [bufs[k - 1]])
                else:
                    (own[0],), (rest[last[0]],) = tie([own[0]], [rest[last[0]]])
            if t == 0:
                first[k] = got[k]
                bufs[k] = plus(keep[k][1], got[k][1])
            elif t == 1:
                total = keep[k][0].astype(f32) + first[k][0].astype(f32) + got[k].astype(f32)
                bufs[k] = total.astype(bf16)
            elif t < 6:
                bufs[k] = plus(bufs[k], got[k])
            else:
                bufs[k] = jnp.stack([bufs[k], got[k]])
        if t < len(steps):
            (back,), (bufs[2],) = tie([back], [bufs[2]])
            rest = reduce_sums(rest, live, which, kept, back)
            last = which
    mine = join_call(order, [v for k in range(3) for v in (bufs[k], got[k])])
    return (*assemble_call(jnp.stack([core, dp]).astype(jnp.int32), mine, swap_cores(mine)), rest)


def body(
    tokens,
    item_kind,
    cotangent,
    norm1_gain,
    norm1_shift,
    qkv_weight,
    query_bias,
    value_bias,
    out_weight,
    out_bias,
    norm2_gain,
    norm2_shift,
    ffn_in,
    ffn_in_bias,
    ffn_out,
    ffn_out_bias,
):
    dp = lax.axis_index("dp")
    core = lax.axis_index("expert")
    small = jnp.zeros((3, 2, 64, 12), bf16)
    mine = jnp.stack([norm2_gain, norm2_shift, ffn_out_bias]).reshape(3, 1, 1, 12)
    small = lax.dynamic_update_slice(small, mine, (0, core, dp, 0)).reshape(6, D)
    hidden_bias = lax.dynamic_update_slice(
        jnp.zeros((2, 64, 48), bf16), ffn_in_bias.reshape(1, 1, 48), (core, dp, 0)
    ).reshape(8, D)
    small = jnp.concatenate([small, hidden_bias, jnp.zeros((2, D), bf16)])

    shard = jnp.stack([ffn_in[0].T, ffn_out[0]]).reshape(2, 3, 2, 8, D)
    stay = choose(core == 0, shard[:, :, 0], shard[:, :, 1])
    leave = choose(core == 0, shard[:, :, 1], shard[:, :, 0])
    came = swap_cores(jnp.concatenate([leave.reshape(48, D), small]))
    kinds = item_kind.reshape(1, ITEMS_DEV)
    vectors = [norm1_gain, norm1_shift, query_bias, value_bias]
    (tokens,), (came,) = tie([tokens], [came])
    small = small + came[48:]
    came_w = came[:48].reshape(2, 3, 8, D)
    both = choose(core == 0, jnp.stack([stay, came_w]), jnp.stack([came_w, stay]))
    bufs = [both[:, :, k].reshape(4, 8, D) for k in range(3)]
    n1, triple, bias, lang = qkv_call(kinds, tokens, vectors, qkv_weight)
    other_kinds = swap_cores(kinds)
    other_cot = swap_cores(cotangent)
    bufs, small, n1 = gather_step(bufs, small, 0, n1)
    (triple,), bufs = tie([triple], bufs)
    ctx_a, lse_a = attend_call(triple, bias, 0, 3)
    bufs, small, ctx_a = gather_step(bufs, small, 1, ctx_a)
    (triple,), bufs = tie([triple], bufs)
    ctx_b, lse_b = attend_call(triple, bias, 3, 3)
    bufs, small, ctx_b = gather_step(bufs, small, 2, ctx_b)
    (ctx_b,), bufs = tie([ctx_b], bufs)
    hidden, routed = out_call(ctx_a, ctx_b, out_weight, out_bias, tokens)
    other_routed = swap_cores(routed)
    (other_kinds,), (routed,) = tie([other_kinds], [routed])
    select, up, nv = select_call(jnp.concatenate([kinds, other_kinds]), cotangent, other_cot)
    bufs, small, up = gather_step(bufs, small, 3, up)
    near = near_sends([jnp.concatenate([bufs[0].reshape(4 * PIECE, D), small]), bufs[1], bufs[2]])
    (select,), bufs = tie([select], bufs)
    rows = sort_call(select, routed, other_routed)
    (near[0],), (rows,) = tie([near[0]], [rows])
    small = small + near[0][4 * PIECE :]
    small = small + pair_up(small, "z", 1)
    pairs = [jnp.concatenate([bufs[0].reshape(4 * PIECE, D), near[0]])]
    for k in (1, 2):
        (near[k],), (pairs[-1],) = tie([near[k]], [pairs[-1]])
        pairs.append(jnp.concatenate([bufs[k], near[k]]))
    far = far_sends(pairs)

    hidden_bias = small[6:14].reshape(2, 64, 3, 2, 8)
    hidden_bias = choose(core == 0, hidden_bias[:, :, :, 0], hidden_bias[:, :, :, 1])
    table = relative_table(dp, core)
    spread = jnp.einsum("kps,esku->ekpu", table, hidden_bias, preferred_element_type=f32)
    hidden_bias = spread.reshape(2, 3, 2, 2 * PIECE).transpose(2, 0, 1, 3).reshape(2, 2, HALF_HID)

    pick = lambda a, b: [v for k in range(3) for v in (a[k], b[k])]
    (n2, branch, gn2, db0), dw0 = expert_call(nv, rows, up, hidden_bias[0], pick(bufs, near), small=small)
    (back_own, back_other, db1), dw1 = expert_call(
        nv, n2, up, hidden_bias[1], far, sums=(select, branch, gn2)
    )

    got0 = near_sends(dw0[1::2])
    dw1_own, dw1_near = list(dw1[0::2]), list(dw1[1::2])
    (back_other, *dw1_near), got0 = tie([back_other, *dw1_near], got0)
    back_recv = swap_cores(back_other)
    got = near_sends(dw1_near)
    mixed, gh, gctx, dw_out, delta, small_b = post_call(
        back_own, back_recv, hidden, cotangent, lang, small, out_weight, ctx_a, ctx_b
    )
    dw1_own, (gh,) = tie(dw1_own, [gh])
    send = [plus(dw1_own[k], got[k]) for k in range(3)]
    (triple,), send = tie([triple], send)
    got = far_sends(send)
    parts = list(attend_back_call(triple, gctx, lse_a, lse_b, delta, bias))
    dw0_own, (parts[0],) = tie(dw0[0::2], [parts[0]])
    bufs = [
        (dw0_own[k].astype(f32) + got0[k].astype(f32) + got[k].astype(f32)).astype(bf16) for k in range(3)
    ]
    live = [[(ORDERS[k][i], t) for i in (1, 0) for t in (1, 0)] for k in range(3)]
    (gh,), bufs = tie([gh], bufs)
    which, kept, sent = reduce_parts(bufs, live, "z", 1)
    (gh,), (sent,) = tie([gh], [sent])
    back = pair_up(sent, "z", 1)

    (db0,), (gh,) = tie([db0], [gh])
    db = jnp.stack([db0, db1]).reshape(2, 2, 3, 256).transpose(2, 0, 3, 1).reshape(3, 2, 32, 8, 2)
    db = db.reshape(3, 64, 8, 2).astype(bf16)
    db = jnp.einsum("kps,kpue->esku", table, db, preferred_element_type=f32)
    zero = jnp.zeros_like(db)
    db = choose(core == 0, jnp.stack([db, zero], 3), jnp.stack([zero, db], 3)).reshape(8, D)

    mine, theirs, tokens_grad = final_call(
        core.reshape(1), n1, tokens, norm1_gain, qkv_weight, gh, dw_out, small_b, db, parts
    )

    (theirs,), (back,) = tie([theirs], [back])
    bufs = reduce_sums(bufs, live, which, kept, back)
    grad_qkv, grad_out, vectors, mine, bias_grad, bufs = all_sum(mine, theirs, dp, core, bufs, live)
    shards = jnp.stack(bufs).reshape(3, 2, 2, 8, D)
    stay = choose(core == 0, shards[:, 0], shards[:, 1])
    leave = choose(core == 0, shards[:, 1], shards[:, 0])
    came = swap_cores(leave)
    full = choose(core == 0, jnp.stack([stay, came], 2), jnp.stack([came, stay], 2))
    full = full.transpose(1, 0, 2, 3, 4).reshape(2, 48, D)

    return (
        mixed,
        tokens_grad,
        vectors[0],
        vectors[1],
        grad_qkv,
        vectors[2],
        vectors[3],
        grad_out,
        vectors[4],
        mine[0],
        mine[1],
        full[0].T[None],
        bias_grad,
        full[1][None],
        mine[2],
    )


def solution(mesh):
    both = ("dp", "expert")
    in_specs = (
        P(both, None),
        P(both),
        P(both, None),
        P(),
        P(),
        P(),
        P(),
        P(),
        P(),
        P(),
        P("expert", "dp"),
        P("expert", "dp"),
        P("expert", None, "dp"),
        P("expert", "dp"),
        P("expert", "dp", None),
        P("expert", "dp"),
    )
    out_specs = (
        P(both, None),
        P(both, None),
        P(),
        P(),
        P(),
        P(),
        P(),
        P(),
        P(),
        P("expert", "dp"),
        P("expert", "dp"),
        P("expert", None, "dp"),
        P("expert", "dp"),
        P("expert", "dp", None),
        P("expert", "dp"),
    )
    return jax.shard_map(body, mesh=mesh, in_specs=in_specs, out_specs=out_specs, check_vma=False)
```

```python
import functools

import jax
import jax.numpy as jnp
from jax import lax
from jax.experimental import pallas as pl
from jax.experimental.pallas import tpu as pltpu
from jax.sharding import PartitionSpec as P

HEADS = 12
IMG_LEN = 197
TXT_LEN = 40
ROWS = 512
CHIP_ROWS = 1024
D = 768
FF = 3072
ITEMS_DEV = 13
PAIRS = HEADS // 2
LANES = 128
BLOCK = 256
MASKED = -1e30
EPS = 1e-5
PLANS = {
    "qkv": (20, False),
    "attend": (16, False),
    "outproj": (12, False),
    "select": (20, False),
    "sort": (12, False),
    "expert": (56, True),
    "post": (56, True),
    "attend_back": (56, False),
    "final": (56, True),
    "split": (16, False),
    "join": (12, False),
    "assemble": (24, False),
}
AR_ROWS = 3264
SMALL_ROWS = AR_ROWS - 4 * D
AR_PIECE = AR_ROWS // 12
HALF = D // 2

bf16 = jnp.bfloat16
f32 = jnp.float32


def dot(left, right):
    return jnp.dot(left, right, preferred_element_type=f32)


def dot_t(left, right):
    return lax.dot_general(left, right, (((1,), (1,)), ((), ())), preferred_element_type=f32)


def dot_0(left, right):
    return lax.dot_general(left, right, (((0,), (0,)), ((), ())), preferred_element_type=f32)


def params(mebibytes):
    return pltpu.CompilerParams(vmem_limit_bytes=mebibytes * 1024 * 1024)


def cost(flops, byts, trans=0):
    return pl.CostEstimate(flops=int(flops), bytes_accessed=int(byts), transcendentals=int(trans))


def shape(dims, dtype):
    return jax.ShapeDtypeStruct(dims, dtype)


VM = pl.BlockSpec(memory_space=pltpu.VMEM)
SM = pl.BlockSpec(memory_space=pltpu.SMEM)
HB = pl.BlockSpec(memory_space=pl.ANY)


def staged_call(
    body, name, smem, small, loads, outs, plain=(), scratch=(), flops=1e9, raw=(), cuts=None, out_cuts=None, first=()
):
    n_out = len(outs)
    limit, staged = PLANS[name]
    big = HB if staged else VM
    cuts, out_cuts = cuts or {}, out_cuts or {}

    def plain_kernel(*refs):
        at = len(smem) + len(small)
        s_refs, v_refs = refs[: len(smem)], refs[len(smem) : at]
        ins, rest = refs[at : at + len(loads)], refs[at + len(loads) :]
        results, extra = rest[: n_out + len(plain)], rest[n_out + len(plain) :]
        body(s_refs, v_refs, lambda i, c=None: ins[i], results, lambda j, c=None: None, extra)

    def part(ref, c, count, axis):
        if count == 1:
            return ref
        size = ref.shape[axis] // count
        return ref.at[(slice(None),) * axis + (pl.ds(c * size, size),)]

    def kernel(*refs):
        refs = list(refs)
        take = lambda n: [refs.pop(0) for _ in range(n)]
        s_refs, v_refs, hbm, raw_refs = take(len(smem)), take(len(small)), take(len(loads)), take(len(raw))
        out_hbm = take(n_out)
        plain_refs, bufs, out_bufs, extra = take(len(plain)), take(len(loads)), take(n_out), take(len(scratch))
        in_sem, out_sem = refs
        copies, sent = {}, []
        for i in range(len(loads)):
            count, axis = cuts.get(i, (1, 0))
            for c in range(count):
                pieces = part(hbm[i], c, count, axis), part(bufs[i], c, count, axis)
                copies[i, c] = pltpu.make_async_copy(*pieces, in_sem.at[len(copies)])
        for key in sorted(copies, key=lambda key: (key[1], key[0]) if key[0] in first else (99, key)):
            copies[key].start()

        def get(i, c=None):
            for key in [key for key in copies if key[0] == i and c in (None, key[1])]:
                copies.pop(key).wait()
            return bufs[i]

        def put(j, c=None):
            count, axis = out_cuts.get(j, (1, 0))
            for piece in range(count) if c is None else [c]:
                pieces = part(out_bufs[j], piece, count, axis), part(out_hbm[j], piece, count, axis)
                copy = pltpu.make_async_copy(*pieces, out_sem.at[len(sent)])
                copy.start()
                sent.append(copy)

        body(s_refs, v_refs, get, out_bufs + plain_refs, put, ([raw_refs] if raw else []) + extra)
        assert not copies
        for copy in sent:
            copy.wait()

    n_in = sum(cuts.get(i, (1, 0))[0] for i in range(len(loads)))
    n_sent = sum(out_cuts.get(j, (1, 0))[0] for j in range(n_out))
    bytes_moved = sum(v.size * v.dtype.itemsize for v in (*loads, *outs))
    buffers = [pltpu.VMEM(v.shape, v.dtype) for v in (*loads, *outs)] if staged else []
    sems = [pltpu.SemaphoreType.DMA((n_in,)), pltpu.SemaphoreType.DMA((max(n_sent, 1),))] if staged else []
    return pl.pallas_call(
        kernel if staged else plain_kernel,
        out_shape=(*outs, *(struct for struct, _ in plain)),
        in_specs=[SM] * len(smem) + [VM] * len(small) + [big] * len(loads) + [HB] * len(raw),
        out_specs=(big,) * n_out + tuple(spec for _, spec in plain),
        scratch_shapes=buffers + list(scratch) + sems,
        compiler_params=params(limit),
        cost_estimate=cost(flops, bytes_moved),
        name=name,
    )(*smem, *small, *loads, *raw)


def as_row(ref):
    return ref[...].astype(f32).reshape(1, D)


def norm_stats(x):
    centred = x - jnp.mean(x, axis=-1, keepdims=True)
    rstd = lax.rsqrt(jnp.mean(centred * centred, axis=-1, keepdims=True) + EPS)
    return centred * rstd, rstd


def item_lengths(kind):
    vision = jnp.where(kind == 1, 0, IMG_LEN)
    language = jnp.where(kind == 0, 0, TXT_LEN)
    return vision, language


def qkv_kernel(smem, small, get, outs, put, scratch):
    (kind_ref,) = smem
    n1_ref, tri_ref, bias_ref, lang_ref = outs
    gain, shift, q_bias, v_bias = (as_row(ref) for ref in small)
    tok_ref = get(0)
    for r in range(0, ROWS, LANES):
        xhat, _ = norm_stats(tok_ref[r : r + LANES, :].astype(f32))
        n1_ref[r : r + LANES, :] = (xhat * gain + shift).astype(bf16)
    put(0)
    n1 = n1_ref[...]
    w_ref = get(1)
    q = dot(n1, w_ref[:, 0:D]) + q_bias
    tri_ref[:, 0:D] = q.astype(bf16) * jnp.asarray(0.125, bf16)
    tri_ref[:, D : 2 * D] = dot(n1, w_ref[:, D : 2 * D]).astype(bf16)
    tri_ref[:, 2 * D :] = (dot(n1, w_ref[:, 2 * D :]) + v_bias).astype(bf16)
    put(1)
    down = lax.broadcasted_iota(jnp.int32, (ROWS, LANES), 0)
    across = lax.broadcasted_iota(jnp.int32, (8, ROWS), 1)
    item_down = jnp.zeros((ROWS, LANES), jnp.int32)
    item_across = jnp.zeros((8, ROWS), jnp.int32)
    lang = jnp.zeros((ROWS, LANES), f32)
    start = 0
    for i in range(ITEMS_DEV):
        vision, language = item_lengths(kind_ref[0, i])
        middle = start + vision
        end = middle + language
        item_down += (down >= end).astype(jnp.int32)
        item_across += (across >= end).astype(jnp.int32)
        lang = jnp.where((down >= middle) & (down < end), 1.0, lang)
        start = end
    lang_ref[...] = lang
    put(3)
    for c in range(0, ROWS, LANES):
        same = item_down == item_across[0:1, c : c + LANES]
        bias_ref[:, c : c + LANES] = jnp.where(same, 0.0, MASKED)
    put(2)


def qkv_call(kinds, tokens, vectors, weight):
    outs = (shape((ROWS, D), bf16), shape((ROWS, 3 * D), bf16), shape((ROWS, ROWS), f32), shape((ROWS, LANES), f32))
    return staged_call(qkv_kernel, "qkv", [kinds], vectors, [tokens, weight], outs, flops=2 * ROWS * D * 3 * D * 2)


def half_lanes(head):
    lane = lax.broadcasted_iota(jnp.int32, (1, LANES), 1)
    return (lane < LANES // 2) if head == 0 else (lane >= LANES // 2)


def attend_kernel(q_ref, k_ref, v_ref, bias_ref, ctx_ref, lse_ref):
    q, k, v = q_ref[...], k_ref[...], v_ref[...]
    zero = jnp.zeros_like(q)
    rows = lax.broadcasted_iota(jnp.int32, (LANES, 1), 0)
    parts = []
    for head in range(2):
        qm = jnp.where(half_lanes(head), q, zero)
        s = dot_t(k, qm) + bias_ref[...]
        top = jnp.max(s, axis=0, keepdims=True)
        e = jnp.exp(s - top)
        total = jnp.sum(e, axis=0, keepdims=True)
        lse_ref[0, head : head + 1, :] = top + jnp.log(total)
        parts.append(dot_0(v, e.astype(bf16)) * (1.0 / total))
    ctx = jnp.where(rows < LANES // 2, parts[0], parts[1])
    ctx_ref[...] = ctx.T.astype(bf16)


def attend_call(triple, bias, first, count):
    def col(offset):
        return pl.BlockSpec((ROWS, LANES), lambda p: (0, offset + first + p))

    return pl.pallas_call(
        attend_kernel,
        grid=(count,),
        out_shape=(shape((ROWS, count * LANES), bf16), shape((count, 8, ROWS), f32)),
        in_specs=[col(0), col(PAIRS), col(2 * PAIRS), pl.BlockSpec((ROWS, ROWS), lambda p: (0, 0))],
        out_specs=(
            pl.BlockSpec((ROWS, LANES), lambda p: (0, p)),
            pl.BlockSpec((1, 8, ROWS), lambda p: (p, 0, 0)),
        ),
        compiler_params=params(PLANS["attend"][0]),
        cost_estimate=cost(count * 2 * 4e9, count * 6e6),
        name="attend",
    )(triple, triple, triple, bias)


def out_kernel(smem, small, get, outs, put, scratch):
    hid_ref, routed_ref = outs
    half = D // 2
    ca_ref, cb_ref, w_ref = get(0), get(1), get(2)
    h = dot(ca_ref[...], w_ref[:half, :]) + dot(cb_ref[...], w_ref[half:, :])
    h = get(3)[...].astype(f32) + h + as_row(small[0])
    routed_ref[...] = h.astype(bf16)
    put(1)
    hid_ref[...] = h
    put(0)


def out_call(ctx_a, ctx_b, weight, bias, tokens):
    outs = (shape((ROWS, D), f32), shape((ROWS, D), bf16))
    return staged_call(
        out_kernel, "outproj", [], [bias], [ctx_a, ctx_b, weight, tokens], outs, flops=2 * ROWS * D * D * 2
    )


def select_kernel(smem, small, get, outs, put, scratch):
    (kind_ref,) = smem
    sel_ref, up_ref, nv_ref = outs
    spans = []
    vision_total = 0
    for pack in range(2):
        start = 0
        for i in range(ITEMS_DEV):
            vision, language = item_lengths(kind_ref[pack, i])
            first = jnp.minimum(start, ROWS)
            middle = jnp.minimum(start + vision, ROWS)
            end = jnp.minimum(start + vision + language, ROWS)
            spans.append((pack, first, middle, end))
            vision_total = vision_total + middle - first
            start = start + vision + language
    nv_ref[0] = vision_total
    place = lax.broadcasted_iota(jnp.int32, (1, ROWS), 1)
    target = [jnp.zeros((1, ROWS), jnp.int32) for _ in range(2)]
    at_vision, at_language = 0, vision_total
    for pack, first, middle, end in spans:
        t = target[pack]
        t = jnp.where((place >= first) & (place < middle), place + (at_vision - first), t)
        t = jnp.where((place >= middle) & (place < end), place + (at_language - middle), t)
        target[pack] = t
        at_vision = at_vision + middle - first
        at_language = at_language + end - middle
    own, other = get(0)[...], get(1)[...]
    for r in range(0, CHIP_ROWS, BLOCK):
        down = lax.broadcasted_iota(jnp.int32, (BLOCK, ROWS), 0) + r
        for pack in range(2):
            sel_ref[r : r + BLOCK, pack * ROWS : (pack + 1) * ROWS] = (
                (down == target[pack]).astype(f32).astype(bf16)
            )
        up_ref[r : r + BLOCK, :] = (
            dot(sel_ref[r : r + BLOCK, :ROWS], own) + dot(sel_ref[r : r + BLOCK, ROWS:], other)
        ).astype(bf16)
    put(0)
    put(1)


def select_call(kinds, own, other):
    square = shape((CHIP_ROWS, CHIP_ROWS), bf16)
    outs = (square, shape((CHIP_ROWS, D), bf16))
    plain = ((shape((1,), jnp.int32), SM),)
    flops = 2 * 2 * CHIP_ROWS * CHIP_ROWS * D
    return staged_call(select_kernel, "select", [kinds], [], [own, other], outs, plain, flops=flops)


def sort_kernel(smem, small, get, outs, put, scratch):
    sel_ref = get(0)
    own, other = get(1)[...], get(2)[...]
    for r in range(0, CHIP_ROWS, BLOCK):
        x = dot(sel_ref[r : r + BLOCK, :ROWS], own) + dot(sel_ref[r : r + BLOCK, ROWS:], other)
        outs[0][r : r + BLOCK, :] = x.astype(bf16)
    put(0)


def sort_call(select, own, other):
    return staged_call(
        sort_kernel,
        "sort",
        [],
        [],
        [select, own, other],
        (shape((CHIP_ROWS, D), bf16),),
        flops=2 * CHIP_ROWS * CHIP_ROWS * D,
    )[0]


def gelu_parts(x):
    t = 1.0 / (1.0 + 0.2316418882663604 * jnp.abs(x))
    poly = 0.127414796 + t * (-0.142248368 + t * (0.7107068705 + t * (-0.7265760135 + t * 0.5307027145)))
    bell = jnp.exp2(x * x * -0.7213475204444817)
    tail = t * poly * bell
    phi = jnp.where(x >= 0, 1.0 - tail, tail)
    return x * phi, phi + (x * 0.3989422804014327) * bell


THIRDS = 3
PIECE = 128
HALF_HID = THIRDS * 2 * PIECE


def expert_kernel(first, smem, small, get, outs, put, scratch):
    (nv_ref,), bias_ref = smem, small[0]
    w_hbm, scratch = scratch[0], scratch[1:]
    if first:
        n2_ref, *sums_hbm, db_ref = outs[:4]
        dw_hbm = outs[4:]
    else:
        own_ref, other_ref, db_ref = outs[:3]
        dw_hbm = outs[3:]
    branch_ref, gn2_ref, sum_sem, scratch = scratch[0], scratch[1], scratch[2], scratch[3:]
    w_ref, acc_ref, out_ref, act_ref, gp_ref, in_sem, out_sem = scratch
    loads = [], []
    for k in range(THIRDS):
        for j in range(2):
            at = k * 2 * PIECE + j * PIECE
            ref = w_hbm[2 * k + j if first else k]
            for m in range(4):
                block = m if first else 4 * j + m
                part = ref.at[block] if len(ref.shape) == 3 else ref.at[pl.ds(block * PIECE, PIECE), :]
                copy = pltpu.make_async_copy(
                    part, w_ref.at[m, pl.ds(at, PIECE), :], in_sem.at[8 * k + 4 * j + m]
                )
                loads[m // 2].append(copy)
    for copy in loads[0] + loads[1]:
        copy.start()
    branch_ref[...] = jnp.zeros_like(branch_ref)
    gn2_ref[...] = jnp.zeros_like(gn2_ref)
    x_ref = get(0)
    if first:
        par = small[1][...].astype(f32)
        for r in range(0, CHIP_ROWS, LANES):
            xhat, _ = norm_stats(x_ref[r : r + LANES, :].astype(f32))
            vision = (lax.broadcasted_iota(jnp.int32, (LANES, 1), 0) + r) < nv_ref[0]
            gain = jnp.where(vision, par[0:1, :], par[1:2, :])
            shift = jnp.where(vision, par[2:3, :], par[3:4, :])
            n2_ref[r : r + LANES, :] = (xhat * gain + shift).astype(bf16)
        put(0)
    else:
        n2_ref = x_ref
    up_ref = get(1)
    db_ref[...] = jnp.zeros_like(db_ref)
    nv = nv_ref[0]
    stores = []
    for e in range(2):
        for copy in loads[e]:
            copy.wait()
        low = jnp.int32(0) if e == 0 else nv // BLOCK
        high = (nv + BLOCK - 1) // BLOCK if e == 0 else jnp.int32(CHIP_ROWS // BLOCK)
        acc_ref[...] = jnp.zeros_like(acc_ref)

        def visit(block, size, e=e):
            at = pl.multiple_of(block * BLOCK, BLOCK)
            rows = pl.ds(at, size)
            index = lax.broadcasted_iota(jnp.int32, (size, 1), 0) + at
            valid = (index < nv) if e == 0 else (index >= nv)
            n2 = n2_ref[rows, :]
            up = up_ref[rows, :]
            for k in range(THIRDS):
                hid = slice(k * BLOCK, (k + 1) * BLOCK)
                pre = dot_t(n2, w_ref[2 * e, hid, :]) + bias_ref[e : e + 1, hid].astype(f32)
                back = dot_t(up, w_ref[2 * e + 1, hid, :])
                active, slope = gelu_parts(pre)
                act = jnp.where(valid, active, 0.0).astype(bf16)
                gp = jnp.where(valid, back * slope, 0.0).astype(bf16)
                act_ref[:size, hid] = act
                gp_ref[:size, hid] = gp
                db_ref[e : e + 1, hid] += jnp.sum(gp.astype(f32), axis=0, keepdims=True)
            acc_ref[0] += dot_0(gp_ref[:size, :], n2)
            acc_ref[1] += dot_0(act_ref[:size, :], up)
            branch_ref[rows, :] += dot(act_ref[:size, :], w_ref[2 * e + 1])
            gn2_ref[rows, :] += dot(gp_ref[:size, :], w_ref[2 * e])
            if not first:
                return
            for b in range(size // BLOCK):
                done = pl.ds(pl.multiple_of(at + b * BLOCK, BLOCK), BLOCK)

                @pl.when((at + (b + 1) * BLOCK <= nv) if e == 0 else (at >= 0))
                def _(done=done):
                    for i, ref in enumerate((branch_ref, gn2_ref)):
                        pltpu.make_async_copy(ref.at[done, :], sums_hbm[i].at[done, :], sum_sem.at[i]).start()

        count = high - low

        def two(i, carry, visit=visit, low=low):
            visit(low + 2 * i, 2 * BLOCK)
            return carry

        lax.fori_loop(0, count // 2, two, 0)

        @pl.when(count % 2 == 1)
        def _(visit=visit, high=high):
            visit(high - 1, BLOCK)

        out_ref[2 * e] = acc_ref[0].astype(bf16)
        out_ref[2 * e + 1] = acc_ref[1].astype(bf16)
        for k in range(THIRDS):
            for j in range(2):
                at = k * 2 * PIECE + j * PIECE
                copy = pltpu.make_async_copy(
                    out_ref.at[pl.ds(2 * e, 2), pl.ds(at, PIECE), :],
                    dw_hbm[2 * k + j].at[pl.ds(2 * e, 2)],
                    out_sem.at[6 * e + 2 * k + j],
                )
                copy.start()
                stores.append(copy)
    if first:
        for i, ref in enumerate((branch_ref, gn2_ref)):
            pltpu.make_async_copy(ref, sums_hbm[i], sum_sem.at[i]).wait()
    else:
        sel_ref = get(2)
        for i, total in enumerate((branch_ref, gn2_ref)):
            y = (get(3 + i)[...] + total[...]).astype(bf16)
            other_ref[i] = dot_0(sel_ref[:, ROWS:], y).astype(bf16)
            own_ref[i] = dot_0(sel_ref[:, :ROWS], y).astype(bf16)
        put(1)
        put(0)
    for copy in stores:
        copy.wait()


def expert_call(nv, rows, up, bias, weights, small=None, sums=None):
    first = sums is None
    db = (shape((2, HALF_HID), f32), VM)
    part = shape((CHIP_ROWS, D), f32)
    back = shape((2, ROWS, D), bf16)
    pieces = ((shape((4, PIECE, D), bf16), HB),) * 6
    work = [
        pltpu.VMEM((CHIP_ROWS, D), f32),
        pltpu.VMEM((CHIP_ROWS, D), f32),
        pltpu.SemaphoreType.DMA((2,)),
        pltpu.VMEM((4, HALF_HID, D), bf16),
        pltpu.VMEM((2, HALF_HID, D), f32),
        pltpu.VMEM((4, HALF_HID, D), bf16),
        pltpu.VMEM((2 * BLOCK, HALF_HID), bf16),
        pltpu.VMEM((2 * BLOCK, HALF_HID), bf16),
        pltpu.SemaphoreType.DMA((24,)),
        pltpu.SemaphoreType.DMA((12,)),
    ]
    if first:
        outs = staged_call(
            functools.partial(expert_kernel, True), "expert", [nv], [bias, small], [rows, up],
            (shape((CHIP_ROWS, D), bf16),), ((part, HB), (part, HB), db, *pieces), work, 20e9, raw=weights,
        )
    else:
        outs = staged_call(
            functools.partial(expert_kernel, False), "expert", [nv], [bias], [rows, up, *sums],
            (back, back), (db, *pieces), work, 20e9, raw=weights,
        )
    return outs[:-6], outs[-6:]


def post_kernel(smem, small, get, outs, put, scratch):
    mixed_ref, gh_ref, gctx_ref, dw_ref, delta_ref, small_ref = outs
    g_ref, prod_ref = scratch
    par = small[0][...].astype(f32)
    gains, bouts = par[0:2, :], par[4:6, :]
    small_ref[...] = jnp.zeros_like(small_ref)
    for r in range(0, ROWS, LANES):
        rows = slice(r, r + LANES)
        own_ref, recv_ref, hid_ref, cot_ref, lang_ref = (get(i, r // LANES) for i in range(5))
        lang = lang_ref[rows, 0:1]
        is_lang = lang > 0.5
        branch = own_ref[0, rows, :].astype(f32) + recv_ref[0, rows, :].astype(f32)
        branch = branch + jnp.where(is_lang, bouts[1:2, :], bouts[0:1, :])
        mixed_ref[rows, :] = (hid_ref[rows, :] + branch.astype(bf16).astype(f32)).astype(bf16)
        gn2 = own_ref[1, rows, :].astype(f32) + recv_ref[1, rows, :].astype(f32)
        xhat, rstd = norm_stats(hid_ref[rows, :].astype(bf16).astype(f32))
        gg = gn2 * jnp.where(is_lang, gains[1:2, :], gains[0:1, :])
        mean_a = jnp.mean(gg, axis=-1, keepdims=True)
        mean_b = jnp.mean(gg * xhat, axis=-1, keepdims=True)
        grad_routed = (rstd * (gg - mean_a - xhat * mean_b)).astype(bf16).astype(f32)
        cot = cot_ref[rows, :].astype(f32)
        gh = cot + grad_routed
        gh_ref[rows, :] = gh
        put(0, r // LANES)
        put(1, r // LANES)
        g_ref[rows, :] = gh.astype(bf16)
        prod = gn2 * xhat
        for i, (value, mask) in enumerate(((gh, None), (prod, 0), (prod, 1), (gn2, 0), (gn2, 1), (cot, 0), (cot, 1))):
            if mask is not None:
                value = jnp.where(is_lang, value, 0.0) if mask == 1 else jnp.where(is_lang, 0.0, value)
            small_ref[i : i + 1, :] += jnp.sum(value, axis=0, keepdims=True)
    g = g_ref[...]
    half = D // 2
    w_ref, ca_ref, cb_ref = get(5), get(6), get(7)
    dw_ref[:half, :] = dot_0(ca_ref[...], g).astype(bf16)
    dw_ref[half:, :] = dot_0(cb_ref[...], g).astype(bf16)
    put(3)
    gctx_ref[...] = dot_t(g, w_ref[...]).astype(bf16)
    put(2)
    prod_ref[:, :half] = gctx_ref[:, :half].astype(f32) * ca_ref[...].astype(f32)
    prod_ref[:, half:] = gctx_ref[:, half:].astype(f32) * cb_ref[...].astype(f32)
    head = lax.broadcasted_iota(jnp.int32, (16, D), 0)
    lane = lax.broadcasted_iota(jnp.int32, (16, D), 1)
    pick = (lane // 64 == head).astype(f32).astype(bf16)
    prod = prod_ref[...]
    upper = prod.astype(bf16)
    lower = (prod - upper.astype(f32)).astype(bf16)
    delta = dot_t(pick, upper) + dot_t(pick, lower)
    delta_ref[...] = jnp.zeros_like(delta_ref)
    for h in range(HEADS):
        delta_ref[h // 2, h % 2 : h % 2 + 1, :] = delta[h : h + 1, :]


def post_call(own, recv, hidden, cot, lang, small, weight, ctx_a, ctx_b):
    rows = shape((ROWS, D), bf16)
    outs = (rows, shape((ROWS, D), f32), rows, shape((D, D), bf16))
    plain = ((shape((PAIRS, 8, ROWS), f32), VM), (shape((8, D), f32), VM))
    work = [pltpu.VMEM((ROWS, D), bf16), pltpu.VMEM((ROWS, D), f32)]
    loads = [own, recv, hidden, cot, lang, weight, ctx_a, ctx_b]
    cuts = {0: (4, 1), 1: (4, 1), 2: (4, 0), 3: (4, 0), 4: (4, 0)}
    return staged_call(
        post_kernel, "post", [], [small], loads, outs, plain, work, 6e9,
        cuts=cuts, out_cuts={0: (4, 0), 1: (4, 0)}, first=range(5),
    )


def attend_back_kernel(q_ref, k_ref, v_ref, g_ref, lse_a, lse_b, delta_ref, bias_ref, dq_ref, dk_ref, dv_ref):
    q, k, v, g = q_ref[...], k_ref[...], v_ref[...], g_ref[...]
    zero = jnp.zeros_like(q)
    lse = jnp.where(pl.program_id(0) < PAIRS // 2, lse_a[0], lse_b[0])
    parts = []
    dk = dv = 0.0
    for c in range(0, ROWS, BLOCK):
        cols = slice(c, c + BLOCK)
        dq = 0.0
        for head in range(2):
            lanes = half_lanes(head)
            qm, gm = (jnp.where(lanes, x[cols, :], zero[cols, :]) for x in (q, g))
            km = jnp.where(lanes, k, zero)
            s = dot_t(k, qm) + bias_ref[:, cols]
            p = jnp.exp(s - lse[head : head + 1, cols])
            dp = dot_t(v, gm)
            ds = (p * (dp - delta_ref[0, head : head + 1, cols])).astype(bf16)
            dv = dv + dot(p.astype(bf16), gm)
            dk = dk + dot(ds, qm)
            dq = dq + dot_0(ds, km)
        parts.append(dq)
    dq = jnp.concatenate(parts, axis=0)
    dq_ref[...] = (dq * 0.125).astype(bf16)
    dk_ref[...] = dk.astype(bf16)
    dv_ref[...] = dv.astype(bf16)


def attend_back_call(triple, gctx, lse_a, lse_b, delta, bias):
    def col(offset):
        return pl.BlockSpec((ROWS, LANES), lambda p: (0, offset + p))

    half = PAIRS // 2
    return pl.pallas_call(
        attend_back_kernel,
        grid=(PAIRS,),
        out_shape=(shape((ROWS, D), bf16),) * 3,
        in_specs=[
            col(0),
            col(PAIRS),
            col(2 * PAIRS),
            col(0),
            pl.BlockSpec((1, 8, ROWS), lambda p: (jnp.minimum(p, half - 1), 0, 0)),
            pl.BlockSpec((1, 8, ROWS), lambda p: (jnp.maximum(p - half, 0), 0, 0)),
            pl.BlockSpec((1, 8, ROWS), lambda p: (p, 0, 0)),
            pl.BlockSpec((ROWS, ROWS), lambda p: (0, 0)),
        ],
        out_specs=(col(0),) * 3,
        compiler_params=params(PLANS["attend_back"][0]),
        cost_estimate=cost(20e9, 10e6),
        name="attend_back",
    )(triple, triple, triple, gctx, lse_a, lse_b, delta, bias)


def final_kernel(smem, small, get, outs, put, scratch):
    (core_ref,), (gain_ref, sb_ref, db_ref) = smem, small
    out_ref, *targets = outs
    gn_ref, small_ref, buf_ref, rows_ref, sem = scratch
    core = core_ref[0]
    lanes = [pl.ds(pl.multiple_of(h * HALF, LANES), HALF) for h in (core, 1 - core)]
    sent = []

    def send(source, t, at, size):
        copy = pltpu.make_async_copy(source, targets[t].at[pl.ds(at, size), :], sem.at[len(sent)])
        copy.start()
        sent.append(copy)

    small_ref[...] = jnp.zeros_like(small_ref)
    n1 = get(0)[...]
    for t in (1, 0):
        for i in range(3):
            buf_ref[t, i * D : (i + 1) * D, :] = dot_0(n1, get(1 + i)[:, lanes[t]]).astype(bf16)
            send(buf_ref.at[t, pl.ds(i * D, D), :], t, i * D, D)
        if t == 0:
            break
        for i in range(3):
            piece = get(1 + i)[...]
            part = dot_t(piece, get(4)[:, i * D : (i + 1) * D])
            if i == 0:
                gn_ref[...] = part
            else:
                gn_ref[...] += part
            if i != 1:
                small_ref[2 + i // 2 : 3 + i // 2, :] = jnp.sum(piece.astype(f32), axis=0, keepdims=True)
    for t in (1, 0):
        buf_ref[t, 3 * D : 4 * D, :] = get(7)[:, lanes[t]]
        send(buf_ref.at[t, pl.ds(3 * D, D), :], t, 3 * D, D)
    gain = as_row(gain_ref)
    for r in range(0, ROWS, LANES):
        rows = slice(r, r + LANES)
        tok_ref, gh_ref = get(5, r // LANES), get(6, r // LANES)
        xhat, rstd = norm_stats(tok_ref[rows, :].astype(f32))
        gn = gn_ref[rows, :]
        small_ref[0:1, :] += jnp.sum(gn * xhat, axis=0, keepdims=True)
        small_ref[1:2, :] += jnp.sum(gn, axis=0, keepdims=True)
        gg = gn * gain
        mean_a = jnp.mean(gg, axis=-1, keepdims=True)
        mean_b = jnp.mean(gg * xhat, axis=-1, keepdims=True)
        out_ref[rows, :] = gh_ref[rows, :] + rstd * (gg - mean_a - xhat * mean_b)
        put(0, r // LANES)
    small_ref[8:16, :] = sb_ref[...]
    small_ref[16:24, :] = db_ref[...]
    for t in (1, 0):
        rows_ref[t] = small_ref[:, lanes[t]].astype(bf16)
        send(rows_ref.at[t], t, 4 * D, SMALL_ROWS)
    for copy in sent:
        copy.wait()


def final_call(core, n1, tokens, gain, weight, gh, dw_out, small_b, db, parts):
    half = shape((AR_ROWS, HALF), bf16)
    work = [
        pltpu.VMEM((ROWS, D), f32),
        pltpu.VMEM((SMALL_ROWS, D), f32),
        pltpu.VMEM((2, 4 * D, HALF), bf16),
        pltpu.VMEM((2, SMALL_ROWS, HALF), bf16),
        pltpu.SemaphoreType.DMA((10,)),
    ]
    loads = [n1, *parts, weight, tokens, gh, dw_out]
    out, mine, theirs = staged_call(
        final_kernel, "final", [core], [gain, small_b, db], loads, (shape((ROWS, D), f32),),
        ((half, HB), (half, HB)), work, 2 * 2 * 2 * ROWS * D * 3 * D,
        cuts={5: (4, 0), 6: (4, 0)}, out_cuts={0: (4, 0)},
    )
    return mine, theirs, out


def split_kernel(order_ref, mine_ref, got_ref, *outs):
    for k in range(THIRDS):
        for i in range(4):
            rows = pl.ds(pl.multiple_of(k * 4 * AR_PIECE + order_ref[4 * k + i] * AR_PIECE, 16), AR_PIECE)
            total = mine_ref[rows, :].astype(f32) + got_ref[rows, :].astype(f32)
            outs[2 * k + i // 2][i % 2] = total.astype(bf16)


def split_call(order, mine, got):
    return pl.pallas_call(
        split_kernel,
        out_shape=(shape((2, AR_PIECE, HALF), bf16),) * 6,
        in_specs=[SM, VM, VM],
        out_specs=(VM,) * 6,
        compiler_params=params(PLANS["split"][0]),
        cost_estimate=cost(3e6, 8e6),
        name="split",
    )(order, mine, got)


def join_kernel(order_ref, *refs):
    out_ref = refs[-1]
    for k in range(THIRDS):
        for i in range(4):
            rows = pl.ds(pl.multiple_of(k * 4 * AR_PIECE + order_ref[4 * k + i] * AR_PIECE, 16), AR_PIECE)
            out_ref[rows, :] = refs[2 * k + i // 2][i % 2]


def join_call(order, pieces):
    return pl.pallas_call(
        join_kernel,
        out_shape=shape((AR_ROWS, HALF), bf16),
        in_specs=[SM] + [VM] * 6,
        out_specs=VM,
        compiler_params=params(PLANS["join"][0]),
        cost_estimate=cost(3e6, 5e6),
        name="join",
    )(order, *pieces)


def assemble_kernel(place_ref, *refs):
    ins, (qkv_ref, out_ref), vectors, shards, bias_ref = refs[:10], refs[10:12], refs[12:17], refs[17:20], refs[20]
    core, dp = place_ref[0], place_ref[1]
    zero = core == 0

    def halves(i):
        mine, theirs = ins[2 * i][...].astype(f32), ins[2 * i + 1][...].astype(f32)
        return jnp.where(zero, mine, theirs), jnp.where(zero, theirs, mine)

    for i in range(4):
        for j, value in enumerate(halves(i)):
            if i < 3:
                qkv_ref[:, i * D + j * HALF : i * D + (j + 1) * HALF] = value
            else:
                out_ref[:, j * HALF : (j + 1) * HALF] = value

    @pl.when(pl.program_id(0) == 0)
    def _():
        rows = jnp.concatenate([value[:24, :] for value in halves(4)], axis=1)
        for ref, r in zip(vectors, (0, 1, 2, 3, 8)):
            ref[...] = rows[r : r + 1, :].reshape(D)
        down = lax.broadcasted_iota(jnp.int32, (D, LANES), 0)
        lane = lax.broadcasted_iota(jnp.int32, (D, LANES), 1)

        def pick(offset):
            return dot(rows.astype(bf16), (down - offset == lane).astype(f32).astype(bf16))

        norms = pick(12 * dp)
        for i, ref in enumerate(shards):
            both = norms[9 + 2 * i : 11 + 2 * i, :12]
            ref[...] = jnp.where(zero, both[0:1, :], both[1:2, :])
        biases = pick(48 * (dp % 16))
        at = lax.broadcasted_iota(jnp.int32, (24, LANES), 0)
        here = jnp.where(at == 16 + 4 * core + dp // 16, biases, 0.0)
        bias_ref[...] = jnp.sum(here, axis=0, keepdims=True)[:, :48]


def assemble_call(place, mine, theirs):
    step = SMALL_ROWS
    specs, args = [], []
    for i in range(5):
        for ref in (mine, theirs):
            specs.append(pl.BlockSpec((step, HALF), (lambda r, i=i: (4 * i + r, 0)) if i < 4 else (lambda r: (16, 0))))
            args.append(ref)
    outs = pl.pallas_call(
        assemble_kernel,
        grid=(D // step,),
        out_shape=(shape((D, 3 * D), f32), shape((D, D), f32))
        + (shape((D,), f32),) * 5
        + (shape((1, 12), f32),) * 3
        + (shape((1, 48), f32),),
        in_specs=[SM] + specs,
        out_specs=(
            pl.BlockSpec((step, 3 * D), lambda r: (r, 0)),
            pl.BlockSpec((step, D), lambda r: (r, 0)),
        )
        + (VM,) * 9,
        compiler_params=params(PLANS["assemble"][0]),
        cost_estimate=cost(3e6, 15e6),
        name="assemble",
    )(place, *args)
    return outs[0], outs[1], outs[2:7], outs[7:10], outs[10]


AXES = ("y", "x", "z")
STRIDE = {"y": 16, "x": 4, "z": 1}
ORDERS = (("x", "y", "z"), ("y", "z", "x"), ("z", "x", "y"))
FLIPS = (1, 3)


def coordinate(index, axis):
    return (index // STRIDE[axis]) % 4


def pair_up(values, axis, step):
    pairs = []
    for dp in range(64):
        for core in range(2):
            place = coordinate(dp, axis)
            flip = FLIPS[step ^ core]
            other = dp + ((place ^ flip) - place) * STRIDE[axis]
            pairs.append((2 * dp + core, 2 * other + core))
    return lax.ppermute(values, ("dp", "expert"), pairs)


def exchange(values, axis, step):
    pairs = []
    for dp in range(64):
        for core in range(2):
            place = coordinate(dp, axis)
            other = dp + ((place ^ FLIPS[step]) - place) * STRIDE[axis]
            pairs.append((2 * dp + core, 2 * other + core))
    return lax.ppermute(values, ("dp", "expert"), pairs)


def swap_cores(values):
    return lax.ppermute(values, "expert", [(0, 1), (1, 0)])


def relative_table(dp, core):
    bits = lax.iota(jnp.int32, 64)
    flip0 = jnp.where(core == 0, FLIPS[0], FLIPS[1])
    flip1 = jnp.where(core == 0, FLIPS[1], FLIPS[0])
    tables = []
    for order in ORDERS:
        source = jnp.zeros((64,), jnp.int32)
        for i, axis in enumerate(order):
            low = (bits >> (2 * i)) & 1
            high = (bits >> (2 * i + 1)) & 1
            here = coordinate(dp, axis) ^ (low * flip0) ^ (high * flip1)
            source = source + here * STRIDE[axis]
        tables.append((source[:, None] == bits[None, :]).astype(bf16))
    return jnp.stack(tables)


def plus(left, right):
    return (left.astype(f32) + right.astype(f32)).astype(bf16)


def choose(flag, when, otherwise):
    return jnp.where(flag, when, otherwise)


def tie(values, deps):
    flat = lax.optimization_barrier((*values, *deps))
    return list(flat[: len(values)]), list(flat[len(values) :])


def near_sends(pieces):
    return [pair_up(pieces[k], ORDERS[k][2], 0) for k in range(3)]


def far_sends(pieces):
    return [pair_up(pieces[k], ORDERS[k][2], 1) for k in range(3)]


def gather_step(bufs, small, t, kernel):
    n = bufs[0].shape[1]
    sends = [jnp.concatenate([bufs[0].reshape(4 * n, D), small]), bufs[1], bufs[2]]
    got = [pair_up(sends[k], ORDERS[k][t // 2], t % 2) for k in range(3)]
    (small, *bufs), (kernel,) = tie([small, *bufs], [kernel])
    small = small + got[0][4 * n :]
    got[0] = got[0][: 4 * n].reshape(4, n, D)
    return [jnp.concatenate([bufs[k], got[k]], axis=1) for k in range(3)], small, kernel


def reduce_parts(bufs, live, axis, step):
    which = [k for k in range(3) if axis in ORDERS[k][:2]]
    keeps, sends = [], []
    for k in which:
        place = live[k].index((axis, step))
        left = len(live[k])
        live[k] = [bit for bit in live[k] if bit != (axis, step)]
        v = bufs[k].reshape(4, 2**place, 2, 2 ** (left - place - 1), 8, D)
        keeps.append(v[:, :, 0].reshape(-1, 8, D))
        sends.append(v[:, :, 1].reshape(-1, 8, D))
    return which, keeps, jnp.concatenate(sends)


def reduce_sums(bufs, live, which, keeps, got):
    bufs = list(bufs)
    at = 0
    for k, keep in zip(which, keeps):
        total = keep.astype(f32) + got[at : at + keep.shape[0]].astype(f32)
        at += keep.shape[0]
        bufs[k] = (total if not live[k] else total.astype(bf16)).reshape(4, -1, 8, D)
    return bufs


def all_sum(mine, theirs, dp, core, rest, live, finish):
    flip0 = choose(core == 0, FLIPS[0], FLIPS[1])
    flip1 = choose(core == 0, FLIPS[1], FLIPS[0])
    order = []
    for k in range(3):
        at = coordinate(dp, ORDERS[k][0])
        order += [at, at ^ flip1, at ^ flip0, at ^ flip0 ^ flip1]
    order = jnp.stack(order).astype(jnp.int32)
    outs = split_call(order, mine, swap_cores(theirs))
    keep, bufs = list(outs[0::2]), list(outs[1::2])
    first = [None] * 3
    steps = [("z", 0), ("y", 1), ("y", 0), ("x", 1), ("x", 0)]
    for t in range(8):
        axes = [ORDERS[k][(0, 0, 1, 1, 2, 2, 0, 0)[t]] for k in range(3)]
        swap = exchange if 2 <= t < 6 else pair_up
        got = [swap(bufs[k], axes[k], (0, 1, 0, 1, 0, 1, 1, 0)[t]) for k in range(3)]
        if t < len(steps):
            which, kept, sent = reduce_parts(rest, live, *steps[t])
            back = pair_up(sent, *steps[t])
        if t == 7:
            break
        if t == 6:
            stay, came = finish(rest)
            (bufs[2],), (came,) = tie([bufs[2]], [came])
        for k in range(3):
            own = keep if t < 2 else bufs
            if t <= len(steps) and (t or k):
                if k:
                    (own[k],), (bufs[k - 1],) = tie([own[k]], [bufs[k - 1]])
                else:
                    (own[0],), (rest[last[0]],) = tie([own[0]], [rest[last[0]]])
            if t == 0:
                first[k] = got[k]
                bufs[k] = plus(keep[k][1], got[k][1])
            elif t == 1:
                total = keep[k][0].astype(f32) + first[k][0].astype(f32) + got[k].astype(f32)
                bufs[k] = total.astype(bf16)
            elif t < 6:
                bufs[k] = plus(bufs[k], got[k])
            else:
                bufs[k] = jnp.stack([bufs[k], got[k]])
        if t < len(steps):
            (back,), (bufs[2],) = tie([back], [bufs[2]])
            rest = reduce_sums(rest, live, which, kept, back)
            last = which
    mine = join_call(order, [v for k in range(3) for v in (bufs[k], got[k])])
    return (*assemble_call(jnp.stack([core, dp]).astype(jnp.int32), mine, swap_cores(mine)), stay, came)


def body(
    tokens,
    item_kind,
    cotangent,
    norm1_gain,
    norm1_shift,
    qkv_weight,
    query_bias,
    value_bias,
    out_weight,
    out_bias,
    norm2_gain,
    norm2_shift,
    ffn_in,
    ffn_in_bias,
    ffn_out,
    ffn_out_bias,
):
    dp = lax.axis_index("dp")
    core = lax.axis_index("expert")
    small = jnp.zeros((3, 2, 64, 12), bf16)
    mine = jnp.stack([norm2_gain, norm2_shift, ffn_out_bias]).reshape(3, 1, 1, 12)
    small = lax.dynamic_update_slice(small, mine, (0, core, dp, 0)).reshape(6, D)
    hidden_bias = lax.dynamic_update_slice(
        jnp.zeros((2, 64, 48), bf16), ffn_in_bias.reshape(1, 1, 48), (core, dp, 0)
    ).reshape(8, D)
    small = jnp.concatenate([small, hidden_bias, jnp.zeros((2, D), bf16)])

    shard = jnp.stack([ffn_in[0].T, ffn_out[0]]).reshape(2, 3, 2, 8, D)
    stay = choose(core == 0, shard[:, :, 0], shard[:, :, 1])
    leave = choose(core == 0, shard[:, :, 1], shard[:, :, 0])
    came = swap_cores(jnp.concatenate([leave.reshape(48, D), small]))
    kinds = item_kind.reshape(1, ITEMS_DEV)
    vectors = [norm1_gain, norm1_shift, query_bias, value_bias]
    (tokens,), (came,) = tie([tokens], [came])
    small = small + came[48:]
    came_w = came[:48].reshape(2, 3, 8, D)
    both = choose(core == 0, jnp.stack([stay, came_w]), jnp.stack([came_w, stay]))
    bufs = [both[:, :, k].reshape(4, 8, D) for k in range(3)]
    n1, triple, bias, lang = qkv_call(kinds, tokens, vectors, qkv_weight)
    other_kinds = swap_cores(kinds)
    other_cot = swap_cores(cotangent)
    bufs, small, n1 = gather_step(bufs, small, 0, n1)
    (triple,), bufs = tie([triple], bufs)
    ctx_a, lse_a = attend_call(triple, bias, 0, 3)
    bufs, small, ctx_a = gather_step(bufs, small, 1, ctx_a)
    (triple,), bufs = tie([triple], bufs)
    ctx_b, lse_b = attend_call(triple, bias, 3, 3)
    bufs, small, ctx_b = gather_step(bufs, small, 2, ctx_b)
    (ctx_b,), bufs = tie([ctx_b], bufs)
    hidden, routed = out_call(ctx_a, ctx_b, out_weight, out_bias, tokens)
    other_routed = swap_cores(routed)
    (other_kinds,), (routed,) = tie([other_kinds], [routed])
    select, up, nv = select_call(jnp.concatenate([kinds, other_kinds]), cotangent, other_cot)
    bufs, small, up = gather_step(bufs, small, 3, up)
    near = near_sends([jnp.concatenate([bufs[0].reshape(4 * PIECE, D), small]), bufs[1], bufs[2]])
    (select,), bufs = tie([select], bufs)
    rows = sort_call(select, routed, other_routed)
    (near[0],), (rows,) = tie([near[0]], [rows])
    small = small + near[0][4 * PIECE :]
    small = small + pair_up(small, "z", 1)
    pairs = [jnp.concatenate([bufs[0].reshape(4 * PIECE, D), near[0]])]
    for k in (1, 2):
        (near[k],), (pairs[-1],) = tie([near[k]], [pairs[-1]])
        pairs.append(jnp.concatenate([bufs[k], near[k]]))
    far = far_sends(pairs)

    hidden_bias = small[6:14].reshape(2, 64, 3, 2, 8)
    hidden_bias = choose(core == 0, hidden_bias[:, :, :, 0], hidden_bias[:, :, :, 1])
    table = relative_table(dp, core)
    spread = jnp.einsum("kps,esku->ekpu", table, hidden_bias, preferred_element_type=f32)
    hidden_bias = spread.reshape(2, 3, 2, 2 * PIECE).transpose(2, 0, 1, 3).reshape(2, 2, HALF_HID)

    pick = lambda a, b: [v for k in range(3) for v in (a[k], b[k])]
    (n2, branch, gn2, db0), dw0 = expert_call(nv, rows, up, hidden_bias[0], pick(bufs, near), small=small)
    (back_own, back_other, db1), dw1 = expert_call(
        nv, n2, up, hidden_bias[1], far, sums=(select, branch, gn2)
    )

    got0 = near_sends(dw0[1::2])
    dw1_own, dw1_near = list(dw1[0::2]), list(dw1[1::2])
    (back_other, *dw1_near), got0 = tie([back_other, *dw1_near], got0)
    back_recv = swap_cores(back_other)
    got = near_sends(dw1_near)
    mixed, gh, gctx, dw_out, delta, small_b = post_call(
        back_own, back_recv, hidden, cotangent, lang, small, out_weight, ctx_a, ctx_b
    )
    dw1_own, (gh,) = tie(dw1_own, [gh])
    send = [plus(dw1_own[k], got[k]) for k in range(3)]
    (triple,), send = tie([triple], send)
    got = far_sends(send)
    parts = list(attend_back_call(triple, gctx, lse_a, lse_b, delta, bias))
    dw0_own, (parts[0],) = tie(dw0[0::2], [parts[0]])
    bufs = [
        (dw0_own[k].astype(f32) + got0[k].astype(f32) + got[k].astype(f32)).astype(bf16) for k in range(3)
    ]
    live = [[(ORDERS[k][i], t) for i in (1, 0) for t in (1, 0)] for k in range(3)]
    (gh,), bufs = tie([gh], bufs)
    which, kept, sent = reduce_parts(bufs, live, "z", 1)
    (gh,), (sent,) = tie([gh], [sent])
    back = pair_up(sent, "z", 1)

    (db0,), (gh,) = tie([db0], [gh])
    db = jnp.stack([db0, db1]).reshape(2, 2, 3, 256).transpose(2, 0, 3, 1).reshape(3, 2, 32, 8, 2)
    db = db.reshape(3, 64, 8, 2).astype(bf16)
    db = jnp.einsum("kps,kpue->esku", table, db, preferred_element_type=f32)
    zero = jnp.zeros_like(db)
    db = choose(core == 0, jnp.stack([db, zero], 3), jnp.stack([zero, db], 3)).reshape(8, D)

    mine, theirs, tokens_grad = final_call(
        core.reshape(1), n1, tokens, norm1_gain, qkv_weight, gh, dw_out, small_b, db, parts
    )

    (theirs,), (back,) = tie([theirs], [back])
    bufs = reduce_sums(bufs, live, which, kept, back)

    def finish(bufs):
        shards = jnp.stack(bufs).reshape(3, 2, 2, 8, D)
        stay = choose(core == 0, shards[:, 0], shards[:, 1])
        return stay, swap_cores(choose(core == 0, shards[:, 1], shards[:, 0]))

    grad_qkv, grad_out, vectors, mine, bias_grad, stay, came = all_sum(mine, theirs, dp, core, bufs, live, finish)
    full = choose(core == 0, jnp.stack([stay, came], 2), jnp.stack([came, stay], 2))
    full = full.transpose(1, 0, 2, 3, 4).reshape(2, 48, D)

    return (
        mixed,
        tokens_grad,
        vectors[0],
        vectors[1],
        grad_qkv,
        vectors[2],
        vectors[3],
        grad_out,
        vectors[4],
        mine[0],
        mine[1],
        full[0].T[None],
        bias_grad,
        full[1][None],
        mine[2],
    )


def solution(mesh):
    both = ("dp", "expert")
    in_specs = (
        P(both, None),
        P(both),
        P(both, None),
        P(),
        P(),
        P(),
        P(),
        P(),
        P(),
        P(),
        P("expert", "dp"),
        P("expert", "dp"),
        P("expert", None, "dp"),
        P("expert", "dp"),
        P("expert", "dp", None),
        P("expert", "dp"),
    )
    out_specs = (
        P(both, None),
        P(both, None),
        P(),
        P(),
        P(),
        P(),
        P(),
        P(),
        P(),
        P("expert", "dp"),
        P("expert", "dp"),
        P("expert", None, "dp"),
        P("expert", "dp"),
        P("expert", "dp", None),
        P("expert", "dp"),
    )
    return jax.shard_map(body, mesh=mesh, in_specs=in_specs, out_specs=out_specs, check_vma=False)
```

```python
import functools

import jax
import jax.numpy as jnp
from jax import lax
from jax.experimental import pallas as pl
from jax.experimental.pallas import tpu as pltpu
from jax.sharding import PartitionSpec as P

HEADS = 12
IMG_LEN = 197
TXT_LEN = 40
ROWS = 512
CHIP_ROWS = 1024
D = 768
FF = 3072
ITEMS_DEV = 13
PAIRS = HEADS // 2
LANES = 128
BLOCK = 256
MASKED = -1e30
EPS = 1e-5
PLANS = {
    "qkv": (20, False),
    "attend": (16, False),
    "outproj": (12, False),
    "select": (20, False),
    "sort": (12, False),
    "expert": (56, True),
    "post": (56, True),
    "attend_back": (56, False),
    "final": (56, True),
    "split": (16, False),
    "join": (12, False),
    "assemble": (24, False),
}
AR_ROWS = 3264
SMALL_ROWS = AR_ROWS - 4 * D
AR_PIECE = AR_ROWS // 12
HALF = D // 2

bf16 = jnp.bfloat16
f32 = jnp.float32


def dot(left, right):
    return jnp.dot(left, right, preferred_element_type=f32)


def dot_t(left, right):
    return lax.dot_general(left, right, (((1,), (1,)), ((), ())), preferred_element_type=f32)


def dot_0(left, right):
    return lax.dot_general(left, right, (((0,), (0,)), ((), ())), preferred_element_type=f32)


def params(mebibytes):
    return pltpu.CompilerParams(vmem_limit_bytes=mebibytes * 1024 * 1024)


def cost(flops, byts, trans=0):
    return pl.CostEstimate(flops=int(flops), bytes_accessed=int(byts), transcendentals=int(trans))


def shape(dims, dtype):
    return jax.ShapeDtypeStruct(dims, dtype)


VM = pl.BlockSpec(memory_space=pltpu.VMEM)
SM = pl.BlockSpec(memory_space=pltpu.SMEM)
HB = pl.BlockSpec(memory_space=pl.ANY)


def staged_call(
    body, name, smem, small, loads, outs, plain=(), scratch=(), flops=1e9, raw=(), cuts=None, out_cuts=None, first=()
):
    n_out = len(outs)
    limit, staged = PLANS[name]
    big = HB if staged else VM
    cuts, out_cuts = cuts or {}, out_cuts or {}

    def plain_kernel(*refs):
        at = len(smem) + len(small)
        s_refs, v_refs = refs[: len(smem)], refs[len(smem) : at]
        ins, rest = refs[at : at + len(loads)], refs[at + len(loads) :]
        results, extra = rest[: n_out + len(plain)], rest[n_out + len(plain) :]
        body(s_refs, v_refs, lambda i, c=None: ins[i], results, lambda j, c=None: None, extra)

    def part(ref, c, count, axis):
        if count == 1:
            return ref
        size = ref.shape[axis] // count
        return ref.at[(slice(None),) * axis + (pl.ds(c * size, size),)]

    def kernel(*refs):
        refs = list(refs)
        take = lambda n: [refs.pop(0) for _ in range(n)]
        s_refs, v_refs, hbm, raw_refs = take(len(smem)), take(len(small)), take(len(loads)), take(len(raw))
        out_hbm = take(n_out)
        plain_refs, bufs, out_bufs, extra = take(len(plain)), take(len(loads)), take(n_out), take(len(scratch))
        in_sem, out_sem = refs
        copies, sent = {}, []
        for i in range(len(loads)):
            count, axis = cuts.get(i, (1, 0))
            for c in range(count):
                pieces = part(hbm[i], c, count, axis), part(bufs[i], c, count, axis)
                copies[i, c] = pltpu.make_async_copy(*pieces, in_sem.at[len(copies)])
        for key in sorted(copies, key=lambda key: (key[1], key[0]) if key[0] in first else (99, key)):
            copies[key].start()

        def get(i, c=None):
            for key in [key for key in copies if key[0] == i and c in (None, key[1])]:
                copies.pop(key).wait()
            return bufs[i]

        def put(j, c=None):
            count, axis = out_cuts.get(j, (1, 0))
            for piece in range(count) if c is None else [c]:
                pieces = part(out_bufs[j], piece, count, axis), part(out_hbm[j], piece, count, axis)
                copy = pltpu.make_async_copy(*pieces, out_sem.at[len(sent)])
                copy.start()
                sent.append(copy)

        body(s_refs, v_refs, get, out_bufs + plain_refs, put, ([raw_refs] if raw else []) + extra)
        assert not copies
        for copy in sent:
            copy.wait()

    n_in = sum(cuts.get(i, (1, 0))[0] for i in range(len(loads)))
    n_sent = sum(out_cuts.get(j, (1, 0))[0] for j in range(n_out))
    bytes_moved = sum(v.size * v.dtype.itemsize for v in (*loads, *outs))
    buffers = [pltpu.VMEM(v.shape, v.dtype) for v in (*loads, *outs)] if staged else []
    sems = [pltpu.SemaphoreType.DMA((n_in,)), pltpu.SemaphoreType.DMA((max(n_sent, 1),))] if staged else []
    return pl.pallas_call(
        kernel if staged else plain_kernel,
        out_shape=(*outs, *(struct for struct, _ in plain)),
        in_specs=[SM] * len(smem) + [VM] * len(small) + [big] * len(loads) + [HB] * len(raw),
        out_specs=(big,) * n_out + tuple(spec for _, spec in plain),
        scratch_shapes=buffers + list(scratch) + sems,
        compiler_params=params(limit),
        cost_estimate=cost(flops, bytes_moved),
        name=name,
    )(*smem, *small, *loads, *raw)


def as_row(ref):
    return ref[...].astype(f32).reshape(1, D)


def norm_stats(x):
    centred = x - jnp.mean(x, axis=-1, keepdims=True)
    rstd = lax.rsqrt(jnp.mean(centred * centred, axis=-1, keepdims=True) + EPS)
    return centred * rstd, rstd


def item_lengths(kind):
    vision = jnp.where(kind == 1, 0, IMG_LEN)
    language = jnp.where(kind == 0, 0, TXT_LEN)
    return vision, language


def qkv_kernel(smem, small, get, outs, put, scratch):
    (kind_ref,) = smem
    n1_ref, tri_ref, bias_ref, lang_ref = outs
    gain, shift, q_bias, v_bias = (as_row(ref) for ref in small)
    tok_ref = get(0)
    for r in range(0, ROWS, LANES):
        xhat, _ = norm_stats(tok_ref[r : r + LANES, :].astype(f32))
        n1_ref[r : r + LANES, :] = (xhat * gain + shift).astype(bf16)
    put(0)
    n1 = n1_ref[...]
    w_ref = get(1)
    q = dot(n1, w_ref[:, 0:D]) + q_bias
    tri_ref[:, 0:D] = q.astype(bf16) * jnp.asarray(0.125, bf16)
    tri_ref[:, D : 2 * D] = dot(n1, w_ref[:, D : 2 * D]).astype(bf16)
    tri_ref[:, 2 * D :] = (dot(n1, w_ref[:, 2 * D :]) + v_bias).astype(bf16)
    put(1)
    down = lax.broadcasted_iota(jnp.int32, (ROWS, LANES), 0)
    across = lax.broadcasted_iota(jnp.int32, (8, ROWS), 1)
    item_down = jnp.zeros((ROWS, LANES), jnp.int32)
    item_across = jnp.zeros((8, ROWS), jnp.int32)
    lang = jnp.zeros((ROWS, LANES), f32)
    start = 0
    for i in range(ITEMS_DEV):
        vision, language = item_lengths(kind_ref[0, i])
        middle = start + vision
        end = middle + language
        item_down += (down >= end).astype(jnp.int32)
        item_across += (across >= end).astype(jnp.int32)
        lang = jnp.where((down >= middle) & (down < end), 1.0, lang)
        start = end
    lang_ref[...] = lang
    put(3)
    for c in range(0, ROWS, LANES):
        same = item_down == item_across[0:1, c : c + LANES]
        bias_ref[:, c : c + LANES] = jnp.where(same, 0.0, MASKED)
    put(2)


def qkv_call(kinds, tokens, vectors, weight):
    outs = (shape((ROWS, D), bf16), shape((ROWS, 3 * D), bf16), shape((ROWS, ROWS), f32), shape((ROWS, LANES), f32))
    return staged_call(qkv_kernel, "qkv", [kinds], vectors, [tokens, weight], outs, flops=2 * ROWS * D * 3 * D * 2)


def half_lanes(head):
    lane = lax.broadcasted_iota(jnp.int32, (1, LANES), 1)
    return (lane < LANES // 2) if head == 0 else (lane >= LANES // 2)


def attend_kernel(q_ref, k_ref, v_ref, bias_ref, ctx_ref, lse_ref):
    q, k, v = q_ref[...], k_ref[...], v_ref[...]
    zero = jnp.zeros_like(q)
    rows = lax.broadcasted_iota(jnp.int32, (LANES, 1), 0)
    parts = []
    for head in range(2):
        qm = jnp.where(half_lanes(head), q, zero)
        s = dot_t(k, qm) + bias_ref[...]
        top = jnp.max(s, axis=0, keepdims=True)
        e = jnp.exp(s - top)
        total = jnp.sum(e, axis=0, keepdims=True)
        lse_ref[0, head : head + 1, :] = top + jnp.log(total)
        parts.append(dot_0(v, e.astype(bf16)) * (1.0 / total))
    ctx = jnp.where(rows < LANES // 2, parts[0], parts[1])
    ctx_ref[...] = ctx.T.astype(bf16)


def attend_call(triple, bias, first, count):
    def col(offset):
        return pl.BlockSpec((ROWS, LANES), lambda p: (0, offset + first + p))

    return pl.pallas_call(
        attend_kernel,
        grid=(count,),
        out_shape=(shape((ROWS, count * LANES), bf16), shape((count, 8, ROWS), f32)),
        in_specs=[col(0), col(PAIRS), col(2 * PAIRS), pl.BlockSpec((ROWS, ROWS), lambda p: (0, 0))],
        out_specs=(
            pl.BlockSpec((ROWS, LANES), lambda p: (0, p)),
            pl.BlockSpec((1, 8, ROWS), lambda p: (p, 0, 0)),
        ),
        compiler_params=params(PLANS["attend"][0]),
        cost_estimate=cost(count * 2 * 4e9, count * 6e6),
        name="attend",
    )(triple, triple, triple, bias)


def out_kernel(smem, small, get, outs, put, scratch):
    hid_ref, routed_ref = outs
    half = D // 2
    ca_ref, cb_ref, w_ref = get(0), get(1), get(2)
    h = dot(ca_ref[...], w_ref[:half, :]) + dot(cb_ref[...], w_ref[half:, :])
    h = get(3)[...].astype(f32) + h + as_row(small[0])
    routed_ref[...] = h.astype(bf16)
    put(1)
    hid_ref[...] = h
    put(0)


def out_call(ctx_a, ctx_b, weight, bias, tokens):
    outs = (shape((ROWS, D), f32), shape((ROWS, D), bf16))
    return staged_call(
        out_kernel, "outproj", [], [bias], [ctx_a, ctx_b, weight, tokens], outs, flops=2 * ROWS * D * D * 2
    )


def select_kernel(smem, small, get, outs, put, scratch):
    (kind_ref,) = smem
    sel_ref, up_ref, nv_ref = outs
    spans = []
    vision_total = 0
    for pack in range(2):
        start = 0
        for i in range(ITEMS_DEV):
            vision, language = item_lengths(kind_ref[pack, i])
            first = jnp.minimum(start, ROWS)
            middle = jnp.minimum(start + vision, ROWS)
            end = jnp.minimum(start + vision + language, ROWS)
            spans.append((pack, first, middle, end))
            vision_total = vision_total + middle - first
            start = start + vision + language
    nv_ref[0] = vision_total
    place = lax.broadcasted_iota(jnp.int32, (1, ROWS), 1)
    target = [jnp.zeros((1, ROWS), jnp.int32) for _ in range(2)]
    at_vision, at_language = 0, vision_total
    for pack, first, middle, end in spans:
        t = target[pack]
        t = jnp.where((place >= first) & (place < middle), place + (at_vision - first), t)
        t = jnp.where((place >= middle) & (place < end), place + (at_language - middle), t)
        target[pack] = t
        at_vision = at_vision + middle - first
        at_language = at_language + end - middle
    own, other = get(0)[...], get(1)[...]
    for r in range(0, CHIP_ROWS, BLOCK):
        down = lax.broadcasted_iota(jnp.int32, (BLOCK, ROWS), 0) + r
        for pack in range(2):
            sel_ref[r : r + BLOCK, pack * ROWS : (pack + 1) * ROWS] = (
                (down == target[pack]).astype(f32).astype(bf16)
            )
        up_ref[r : r + BLOCK, :] = (
            dot(sel_ref[r : r + BLOCK, :ROWS], own) + dot(sel_ref[r : r + BLOCK, ROWS:], other)
        ).astype(bf16)
    put(0)
    put(1)


def select_call(kinds, own, other):
    square = shape((CHIP_ROWS, CHIP_ROWS), bf16)
    outs = (square, shape((CHIP_ROWS, D), bf16))
    plain = ((shape((1,), jnp.int32), SM),)
    flops = 2 * 2 * CHIP_ROWS * CHIP_ROWS * D
    return staged_call(select_kernel, "select", [kinds], [], [own, other], outs, plain, flops=flops)


def sort_kernel(smem, small, get, outs, put, scratch):
    sel_ref = get(0)
    own, other = get(1)[...], get(2)[...]
    for r in range(0, CHIP_ROWS, BLOCK):
        x = dot(sel_ref[r : r + BLOCK, :ROWS], own) + dot(sel_ref[r : r + BLOCK, ROWS:], other)
        outs[0][r : r + BLOCK, :] = x.astype(bf16)
    put(0)


def sort_call(select, own, other):
    return staged_call(
        sort_kernel,
        "sort",
        [],
        [],
        [select, own, other],
        (shape((CHIP_ROWS, D), bf16),),
        flops=2 * CHIP_ROWS * CHIP_ROWS * D,
    )[0]


def gelu_parts(x):
    t = 1.0 / (1.0 + 0.2316418882663604 * jnp.abs(x))
    poly = 0.127414796 + t * (-0.142248368 + t * (0.7107068705 + t * (-0.7265760135 + t * 0.5307027145)))
    bell = jnp.exp2(x * x * -0.7213475204444817)
    tail = t * poly * bell
    phi = jnp.where(x >= 0, 1.0 - tail, tail)
    return x * phi, phi + (x * 0.3989422804014327) * bell


THIRDS = 3
PIECE = 128
HALF_HID = THIRDS * 2 * PIECE


def expert_kernel(first, smem, small, get, outs, put, scratch):
    (nv_ref,), bias_ref = smem, small[0]
    w_hbm, scratch = scratch[0], scratch[1:]
    if first:
        n2_ref, *sums_hbm, db_ref = outs[:4]
        dw_hbm = outs[4:]
    else:
        own_ref, other_ref, db_ref = outs[:3]
        dw_hbm = outs[3:]
    branch_ref, gn2_ref, sum_sem, scratch = scratch[0], scratch[1], scratch[2], scratch[3:]
    w_ref, acc_ref, out_ref, act_ref, gp_ref, in_sem, out_sem = scratch
    loads = [], []
    for k in range(THIRDS):
        for j in range(2):
            at = k * 2 * PIECE + j * PIECE
            ref = w_hbm[2 * k + j if first else k]
            for m in range(4):
                block = m if first else 4 * j + m
                part = ref.at[block] if len(ref.shape) == 3 else ref.at[pl.ds(block * PIECE, PIECE), :]
                copy = pltpu.make_async_copy(
                    part, w_ref.at[m, pl.ds(at, PIECE), :], in_sem.at[8 * k + 4 * j + m]
                )
                loads[m // 2].append(copy)
    for copy in loads[0] + loads[1]:
        copy.start()
    branch_ref[...] = jnp.zeros_like(branch_ref)
    gn2_ref[...] = jnp.zeros_like(gn2_ref)
    x_ref = get(0)
    if first:
        par = small[1][...].astype(f32)
        for r in range(0, CHIP_ROWS, LANES):
            xhat, _ = norm_stats(x_ref[r : r + LANES, :].astype(f32))
            vision = (lax.broadcasted_iota(jnp.int32, (LANES, 1), 0) + r) < nv_ref[0]
            gain = jnp.where(vision, par[0:1, :], par[1:2, :])
            shift = jnp.where(vision, par[2:3, :], par[3:4, :])
            n2_ref[r : r + LANES, :] = (xhat * gain + shift).astype(bf16)
        put(0)
    else:
        n2_ref = x_ref
    up_ref = get(1)
    db_ref[...] = jnp.zeros_like(db_ref)
    nv = nv_ref[0]
    stores = []
    for e in range(2):
        for copy in loads[e]:
            copy.wait()
        low = jnp.int32(0) if e == 0 else nv // BLOCK
        high = (nv + BLOCK - 1) // BLOCK if e == 0 else jnp.int32(CHIP_ROWS // BLOCK)
        acc_ref[...] = jnp.zeros_like(acc_ref)

        def visit(block, size, e=e):
            at = pl.multiple_of(block * BLOCK, BLOCK)
            rows = pl.ds(at, size)
            index = lax.broadcasted_iota(jnp.int32, (size, 1), 0) + at
            valid = (index < nv) if e == 0 else (index >= nv)
            n2 = n2_ref[rows, :]
            up = up_ref[rows, :]
            for k in range(THIRDS):
                hid = slice(k * BLOCK, (k + 1) * BLOCK)
                pre = dot_t(n2, w_ref[2 * e, hid, :]) + bias_ref[e : e + 1, hid].astype(f32)
                back = dot_t(up, w_ref[2 * e + 1, hid, :])
                active, slope = gelu_parts(pre)
                act = jnp.where(valid, active, 0.0).astype(bf16)
                gp = jnp.where(valid, back * slope, 0.0).astype(bf16)
                act_ref[:size, hid] = act
                gp_ref[:size, hid] = gp
                db_ref[e : e + 1, hid] += jnp.sum(gp.astype(f32), axis=0, keepdims=True)
            acc_ref[0] += dot_0(gp_ref[:size, :], n2)
            acc_ref[1] += dot_0(act_ref[:size, :], up)
            branch_ref[rows, :] += dot(act_ref[:size, :], w_ref[2 * e + 1])
            gn2_ref[rows, :] += dot(gp_ref[:size, :], w_ref[2 * e])
            if not first:
                return
            for b in range(size // BLOCK):
                done = pl.ds(pl.multiple_of(at + b * BLOCK, BLOCK), BLOCK)

                @pl.when((at + (b + 1) * BLOCK <= nv) if e == 0 else (at >= 0))
                def _(done=done):
                    for i, ref in enumerate((branch_ref, gn2_ref)):
                        pltpu.make_async_copy(ref.at[done, :], sums_hbm[i].at[done, :], sum_sem.at[i]).start()

        count = high - low

        def two(i, carry, visit=visit, low=low):
            visit(low + 2 * i, 2 * BLOCK)
            return carry

        lax.fori_loop(0, count // 2, two, 0)

        @pl.when(count % 2 == 1)
        def _(visit=visit, high=high):
            visit(high - 1, BLOCK)

        out_ref[2 * e] = acc_ref[0].astype(bf16)
        out_ref[2 * e + 1] = acc_ref[1].astype(bf16)
        for k in range(THIRDS):
            for j in range(2):
                at = k * 2 * PIECE + j * PIECE
                copy = pltpu.make_async_copy(
                    out_ref.at[pl.ds(2 * e, 2), pl.ds(at, PIECE), :],
                    dw_hbm[2 * k + j].at[pl.ds(2 * e, 2)],
                    out_sem.at[6 * e + 2 * k + j],
                )
                copy.start()
                stores.append(copy)
    if first:
        for i, ref in enumerate((branch_ref, gn2_ref)):
            pltpu.make_async_copy(ref, sums_hbm[i], sum_sem.at[i]).wait()
    else:
        sel_ref = get(2)
        for i, total in enumerate((branch_ref, gn2_ref)):
            y = (get(3 + i)[...] + total[...]).astype(bf16)
            other_ref[i] = dot_0(sel_ref[:, ROWS:], y).astype(bf16)
            own_ref[i] = dot_0(sel_ref[:, :ROWS], y).astype(bf16)
        put(1)
        put(0)
    for copy in stores:
        copy.wait()


def expert_call(nv, rows, up, bias, weights, small=None, sums=None):
    first = sums is None
    db = (shape((2, HALF_HID), f32), VM)
    part = shape((CHIP_ROWS, D), f32)
    back = shape((2, ROWS, D), bf16)
    pieces = ((shape((4, PIECE, D), bf16), HB),) * 6
    work = [
        pltpu.VMEM((CHIP_ROWS, D), f32),
        pltpu.VMEM((CHIP_ROWS, D), f32),
        pltpu.SemaphoreType.DMA((2,)),
        pltpu.VMEM((4, HALF_HID, D), bf16),
        pltpu.VMEM((2, HALF_HID, D), f32),
        pltpu.VMEM((4, HALF_HID, D), bf16),
        pltpu.VMEM((2 * BLOCK, HALF_HID), bf16),
        pltpu.VMEM((2 * BLOCK, HALF_HID), bf16),
        pltpu.SemaphoreType.DMA((24,)),
        pltpu.SemaphoreType.DMA((12,)),
    ]
    if first:
        outs = staged_call(
            functools.partial(expert_kernel, True), "expert", [nv], [bias, small], [rows, up],
            (shape((CHIP_ROWS, D), bf16),), ((part, HB), (part, HB), db, *pieces), work, 20e9, raw=weights,
        )
    else:
        outs = staged_call(
            functools.partial(expert_kernel, False), "expert", [nv], [bias], [rows, up, *sums],
            (back, back), (db, *pieces), work, 20e9, raw=weights,
        )
    return outs[:-6], outs[-6:]


def post_kernel(smem, small, get, outs, put, scratch):
    mixed_ref, gh_ref, gctx_ref, dw_ref, delta_ref, small_ref = outs
    g_ref, prod_ref = scratch
    par = small[0][...].astype(f32)
    gains, bouts = par[0:2, :], par[4:6, :]
    small_ref[...] = jnp.zeros_like(small_ref)
    for r in range(0, ROWS, LANES):
        rows = slice(r, r + LANES)
        own_ref, recv_ref, hid_ref, cot_ref, lang_ref = (get(i, r // LANES) for i in range(5))
        lang = lang_ref[rows, 0:1]
        is_lang = lang > 0.5
        branch = own_ref[0, rows, :].astype(f32) + recv_ref[0, rows, :].astype(f32)
        branch = branch + jnp.where(is_lang, bouts[1:2, :], bouts[0:1, :])
        mixed_ref[rows, :] = (hid_ref[rows, :] + branch.astype(bf16).astype(f32)).astype(bf16)
        gn2 = own_ref[1, rows, :].astype(f32) + recv_ref[1, rows, :].astype(f32)
        xhat, rstd = norm_stats(hid_ref[rows, :].astype(bf16).astype(f32))
        gg = gn2 * jnp.where(is_lang, gains[1:2, :], gains[0:1, :])
        mean_a = jnp.mean(gg, axis=-1, keepdims=True)
        mean_b = jnp.mean(gg * xhat, axis=-1, keepdims=True)
        grad_routed = (rstd * (gg - mean_a - xhat * mean_b)).astype(bf16).astype(f32)
        cot = cot_ref[rows, :].astype(f32)
        gh = cot + grad_routed
        gh_ref[rows, :] = gh
        put(0, r // LANES)
        put(1, r // LANES)
        g_ref[rows, :] = gh.astype(bf16)
        prod = gn2 * xhat
        for i, (value, mask) in enumerate(((gh, None), (prod, 0), (prod, 1), (gn2, 0), (gn2, 1), (cot, 0), (cot, 1))):
            if mask is not None:
                value = jnp.where(is_lang, value, 0.0) if mask == 1 else jnp.where(is_lang, 0.0, value)
            small_ref[i : i + 1, :] += jnp.sum(value, axis=0, keepdims=True)
    g = g_ref[...]
    half = D // 2
    w_ref, ca_ref, cb_ref = get(5), get(6), get(7)
    dw_ref[:half, :] = dot_0(ca_ref[...], g).astype(bf16)
    dw_ref[half:, :] = dot_0(cb_ref[...], g).astype(bf16)
    put(3)
    gctx_ref[...] = dot_t(g, w_ref[...]).astype(bf16)
    put(2)
    prod_ref[:, :half] = gctx_ref[:, :half].astype(f32) * ca_ref[...].astype(f32)
    prod_ref[:, half:] = gctx_ref[:, half:].astype(f32) * cb_ref[...].astype(f32)
    head = lax.broadcasted_iota(jnp.int32, (16, D), 0)
    lane = lax.broadcasted_iota(jnp.int32, (16, D), 1)
    pick = (lane // 64 == head).astype(f32).astype(bf16)
    prod = prod_ref[...]
    upper = prod.astype(bf16)
    lower = (prod - upper.astype(f32)).astype(bf16)
    delta = dot_t(pick, upper) + dot_t(pick, lower)
    delta_ref[...] = jnp.zeros_like(delta_ref)
    for h in range(HEADS):
        delta_ref[h // 2, h % 2 : h % 2 + 1, :] = delta[h : h + 1, :]


def post_call(own, recv, hidden, cot, lang, small, weight, ctx_a, ctx_b):
    rows = shape((ROWS, D), bf16)
    outs = (rows, shape((ROWS, D), f32), rows, shape((D, D), bf16))
    plain = ((shape((PAIRS, 8, ROWS), f32), VM), (shape((8, D), f32), VM))
    work = [pltpu.VMEM((ROWS, D), bf16), pltpu.VMEM((ROWS, D), f32)]
    loads = [own, recv, hidden, cot, lang, weight, ctx_a, ctx_b]
    cuts = {0: (4, 1), 1: (4, 1), 2: (4, 0), 3: (4, 0), 4: (4, 0)}
    return staged_call(
        post_kernel, "post", [], [small], loads, outs, plain, work, 6e9,
        cuts=cuts, out_cuts={0: (4, 0), 1: (4, 0)}, first=range(5),
    )


def attend_back_kernel(q_ref, k_ref, v_ref, g_ref, lse_a, lse_b, delta_ref, bias_ref, dq_ref, dk_ref, dv_ref):
    q, k, v, g = q_ref[...], k_ref[...], v_ref[...], g_ref[...]
    zero = jnp.zeros_like(q)
    lse = jnp.where(pl.program_id(0) < PAIRS // 2, lse_a[0], lse_b[0])
    parts = []
    dk = dv = 0.0
    for c in range(0, ROWS, BLOCK):
        cols = slice(c, c + BLOCK)
        dq = 0.0
        for head in range(2):
            lanes = half_lanes(head)
            qm, gm = (jnp.where(lanes, x[cols, :], zero[cols, :]) for x in (q, g))
            km = jnp.where(lanes, k, zero)
            s = dot_t(k, qm) + bias_ref[:, cols]
            p = jnp.exp(s - lse[head : head + 1, cols])
            dp = dot_t(v, gm)
            ds = (p * (dp - delta_ref[0, head : head + 1, cols])).astype(bf16)
            dv = dv + dot(p.astype(bf16), gm)
            dk = dk + dot(ds, qm)
            dq = dq + dot_0(ds, km)
        parts.append(dq)
    dq = jnp.concatenate(parts, axis=0)
    dq_ref[...] = (dq * 0.125).astype(bf16)
    dk_ref[...] = dk.astype(bf16)
    dv_ref[...] = dv.astype(bf16)


def attend_back_call(triple, gctx, lse_a, lse_b, delta, bias):
    def col(offset):
        return pl.BlockSpec((ROWS, LANES), lambda p: (0, offset + p))

    half = PAIRS // 2
    return pl.pallas_call(
        attend_back_kernel,
        grid=(PAIRS,),
        out_shape=(shape((ROWS, D), bf16),) * 3,
        in_specs=[
            col(0),
            col(PAIRS),
            col(2 * PAIRS),
            col(0),
            pl.BlockSpec((1, 8, ROWS), lambda p: (jnp.minimum(p, half - 1), 0, 0)),
            pl.BlockSpec((1, 8, ROWS), lambda p: (jnp.maximum(p - half, 0), 0, 0)),
            pl.BlockSpec((1, 8, ROWS), lambda p: (p, 0, 0)),
            pl.BlockSpec((ROWS, ROWS), lambda p: (0, 0)),
        ],
        out_specs=(col(0),) * 3,
        compiler_params=params(PLANS["attend_back"][0]),
        cost_estimate=cost(20e9, 10e6),
        name="attend_back",
    )(triple, triple, triple, gctx, lse_a, lse_b, delta, bias)


def final_kernel(smem, small, get, outs, put, scratch):
    (core_ref,), (gain_ref, sb_ref, db_ref) = smem, small
    out_ref, *targets = outs
    gn_ref, small_ref, buf_ref, rows_ref, sem = scratch
    core = core_ref[0]
    lanes = [pl.ds(pl.multiple_of(h * HALF, LANES), HALF) for h in (core, 1 - core)]
    sent = []

    def send(source, t, at, size):
        copy = pltpu.make_async_copy(source, targets[t].at[pl.ds(at, size), :], sem.at[len(sent)])
        copy.start()
        sent.append(copy)

    small_ref[...] = jnp.zeros_like(small_ref)
    n1 = get(0)[...]
    for t in (1, 0):
        for i in range(3):
            buf_ref[t, i * D : (i + 1) * D, :] = dot_0(n1, get(1 + i)[:, lanes[t]]).astype(bf16)
            send(buf_ref.at[t, pl.ds(i * D, D), :], t, i * D, D)
        if t == 0:
            break
        for i in range(3):
            piece = get(1 + i)[...]
            part = dot_t(piece, get(4)[:, i * D : (i + 1) * D])
            if i == 0:
                gn_ref[...] = part
            else:
                gn_ref[...] += part
            if i != 1:
                small_ref[2 + i // 2 : 3 + i // 2, :] = jnp.sum(piece.astype(f32), axis=0, keepdims=True)
    for t in (1, 0):
        buf_ref[t, 3 * D : 4 * D, :] = get(7)[:, lanes[t]]
        send(buf_ref.at[t, pl.ds(3 * D, D), :], t, 3 * D, D)
    gain = as_row(gain_ref)
    for r in range(0, ROWS, LANES):
        rows = slice(r, r + LANES)
        tok_ref, gh_ref = get(5, r // LANES), get(6, r // LANES)
        xhat, rstd = norm_stats(tok_ref[rows, :].astype(f32))
        gn = gn_ref[rows, :]
        small_ref[0:1, :] += jnp.sum(gn * xhat, axis=0, keepdims=True)
        small_ref[1:2, :] += jnp.sum(gn, axis=0, keepdims=True)
        gg = gn * gain
        mean_a = jnp.mean(gg, axis=-1, keepdims=True)
        mean_b = jnp.mean(gg * xhat, axis=-1, keepdims=True)
        out_ref[rows, :] = gh_ref[rows, :] + rstd * (gg - mean_a - xhat * mean_b)
        put(0, r // LANES)
    small_ref[8:16, :] = sb_ref[...]
    small_ref[16:24, :] = db_ref[...]
    for t in (1, 0):
        rows_ref[t] = small_ref[:, lanes[t]].astype(bf16)
        send(rows_ref.at[t], t, 4 * D, SMALL_ROWS)
    for copy in sent:
        copy.wait()


def final_call(core, n1, tokens, gain, weight, gh, dw_out, small_b, db, parts):
    half = shape((AR_ROWS, HALF), bf16)
    work = [
        pltpu.VMEM((ROWS, D), f32),
        pltpu.VMEM((SMALL_ROWS, D), f32),
        pltpu.VMEM((2, 4 * D, HALF), bf16),
        pltpu.VMEM((2, SMALL_ROWS, HALF), bf16),
        pltpu.SemaphoreType.DMA((10,)),
    ]
    loads = [n1, *parts, weight, tokens, gh, dw_out]
    out, mine, theirs = staged_call(
        final_kernel, "final", [core], [gain, small_b, db], loads, (shape((ROWS, D), f32),),
        ((half, HB), (half, HB)), work, 2 * 2 * 2 * ROWS * D * 3 * D,
        cuts={5: (4, 0), 6: (4, 0)}, out_cuts={0: (4, 0)},
    )
    return mine, theirs, out


def split_kernel(order_ref, mine_ref, got_ref, *outs):
    for k in range(THIRDS):
        for i in range(4):
            rows = pl.ds(pl.multiple_of(k * 4 * AR_PIECE + order_ref[4 * k + i] * AR_PIECE, 16), AR_PIECE)
            total = mine_ref[rows, :].astype(f32) + got_ref[rows, :].astype(f32)
            outs[2 * k + i // 2][i % 2] = total.astype(bf16)


def split_call(order, mine, got):
    return pl.pallas_call(
        split_kernel,
        out_shape=(shape((2, AR_PIECE, HALF), bf16),) * 6,
        in_specs=[SM, VM, VM],
        out_specs=(VM,) * 6,
        compiler_params=params(PLANS["split"][0]),
        cost_estimate=cost(3e6, 8e6),
        name="split",
    )(order, mine, got)


def join_kernel(order_ref, *refs):
    out_ref = refs[-1]
    for k in range(THIRDS):
        for i in range(4):
            rows = pl.ds(pl.multiple_of(k * 4 * AR_PIECE + order_ref[4 * k + i] * AR_PIECE, 16), AR_PIECE)
            out_ref[rows, :] = refs[2 * k + i // 2][i % 2]


def join_call(order, pieces):
    return pl.pallas_call(
        join_kernel,
        out_shape=shape((AR_ROWS, HALF), bf16),
        in_specs=[SM] + [VM] * 6,
        out_specs=VM,
        compiler_params=params(PLANS["join"][0]),
        cost_estimate=cost(3e6, 5e6),
        name="join",
    )(order, *pieces)


def assemble_kernel(place_ref, *refs):
    ins, (qkv_ref, out_ref), vectors, shards, bias_ref = refs[:10], refs[10:12], refs[12:17], refs[17:20], refs[20]
    core, dp = place_ref[0], place_ref[1]
    zero = core == 0

    def halves(i):
        mine, theirs = ins[2 * i][...].astype(f32), ins[2 * i + 1][...].astype(f32)
        return jnp.where(zero, mine, theirs), jnp.where(zero, theirs, mine)

    for i in range(4):
        for j, value in enumerate(halves(i)):
            if i < 3:
                qkv_ref[:, i * D + j * HALF : i * D + (j + 1) * HALF] = value
            else:
                out_ref[:, j * HALF : (j + 1) * HALF] = value

    @pl.when(pl.program_id(0) == 0)
    def _():
        rows = jnp.concatenate([value[:24, :] for value in halves(4)], axis=1)
        for ref, r in zip(vectors, (0, 1, 2, 3, 8)):
            ref[...] = rows[r : r + 1, :].reshape(D)
        down = lax.broadcasted_iota(jnp.int32, (D, LANES), 0)
        lane = lax.broadcasted_iota(jnp.int32, (D, LANES), 1)

        def pick(offset):
            return dot(rows.astype(bf16), (down - offset == lane).astype(f32).astype(bf16))

        norms = pick(12 * dp)
        for i, ref in enumerate(shards):
            both = norms[9 + 2 * i : 11 + 2 * i, :12]
            ref[...] = jnp.where(zero, both[0:1, :], both[1:2, :])
        biases = pick(48 * (dp % 16))
        at = lax.broadcasted_iota(jnp.int32, (24, LANES), 0)
        here = jnp.where(at == 16 + 4 * core + dp // 16, biases, 0.0)
        bias_ref[...] = jnp.sum(here, axis=0, keepdims=True)[:, :48]


def assemble_call(place, mine, theirs):
    step = SMALL_ROWS
    specs, args = [], []
    for i in range(5):
        for ref in (mine, theirs):
            specs.append(pl.BlockSpec((step, HALF), (lambda r, i=i: (4 * i + r, 0)) if i < 4 else (lambda r: (16, 0))))
            args.append(ref)
    outs = pl.pallas_call(
        assemble_kernel,
        grid=(D // step,),
        out_shape=(shape((D, 3 * D), f32), shape((D, D), f32))
        + (shape((D,), f32),) * 5
        + (shape((1, 12), f32),) * 3
        + (shape((1, 48), f32),),
        in_specs=[SM] + specs,
        out_specs=(
            pl.BlockSpec((step, 3 * D), lambda r: (r, 0)),
            pl.BlockSpec((step, D), lambda r: (r, 0)),
        )
        + (VM,) * 9,
        compiler_params=params(PLANS["assemble"][0]),
        cost_estimate=cost(3e6, 15e6),
        name="assemble",
    )(place, *args)
    return outs[0], outs[1], outs[2:7], outs[7:10], outs[10]


AXES = ("y", "x", "z")
STRIDE = {"y": 16, "x": 4, "z": 1}
ORDERS = (("x", "y", "z"), ("y", "z", "x"), ("z", "x", "y"))
FLIPS = (1, 3)


def coordinate(index, axis):
    return (index // STRIDE[axis]) % 4


def pair_up(values, axis, step):
    pairs = []
    for dp in range(64):
        for core in range(2):
            place = coordinate(dp, axis)
            flip = FLIPS[step ^ core]
            other = dp + ((place ^ flip) - place) * STRIDE[axis]
            pairs.append((2 * dp + core, 2 * other + core))
    return lax.ppermute(values, ("dp", "expert"), pairs)


def exchange(values, axis, step):
    pairs = []
    for dp in range(64):
        for core in range(2):
            place = coordinate(dp, axis)
            other = dp + ((place ^ FLIPS[step]) - place) * STRIDE[axis]
            pairs.append((2 * dp + core, 2 * other + core))
    return lax.ppermute(values, ("dp", "expert"), pairs)


def swap_cores(values):
    return lax.ppermute(values, "expert", [(0, 1), (1, 0)])


def relative_table(dp, core):
    bits = lax.iota(jnp.int32, 64)
    flip0 = jnp.where(core == 0, FLIPS[0], FLIPS[1])
    flip1 = jnp.where(core == 0, FLIPS[1], FLIPS[0])
    tables = []
    for order in ORDERS:
        source = jnp.zeros((64,), jnp.int32)
        for i, axis in enumerate(order):
            low = (bits >> (2 * i)) & 1
            high = (bits >> (2 * i + 1)) & 1
            here = coordinate(dp, axis) ^ (low * flip0) ^ (high * flip1)
            source = source + here * STRIDE[axis]
        tables.append((source[:, None] == bits[None, :]).astype(bf16))
    return jnp.stack(tables)


def plus(left, right):
    return (left.astype(f32) + right.astype(f32)).astype(bf16)


def choose(flag, when, otherwise):
    return jnp.where(flag, when, otherwise)


def tie(values, deps):
    flat = lax.optimization_barrier((*values, *deps))
    return list(flat[: len(values)]), list(flat[len(values) :])


def near_sends(pieces):
    return [pair_up(pieces[k], ORDERS[k][2], 0) for k in range(3)]


def far_sends(pieces):
    return [pair_up(pieces[k], ORDERS[k][2], 1) for k in range(3)]


def gather_step(bufs, small, t, kernel):
    n = bufs[0].shape[1]
    sends = [jnp.concatenate([bufs[0].reshape(4 * n, D), small]), bufs[1], bufs[2]]
    got = [pair_up(sends[k], ORDERS[k][t // 2], t % 2) for k in range(3)]
    (small, *bufs), (kernel,) = tie([small, *bufs], [kernel])
    small = small + got[0][4 * n :]
    got[0] = got[0][: 4 * n].reshape(4, n, D)
    return [jnp.concatenate([bufs[k], got[k]], axis=1) for k in range(3)], small, kernel


def reduce_parts(bufs, live, axis, step):
    which = [k for k in range(3) if axis in ORDERS[k][:2]]
    keeps, sends = [], []
    for k in which:
        place = live[k].index((axis, step))
        left = len(live[k])
        live[k] = [bit for bit in live[k] if bit != (axis, step)]
        v = bufs[k].reshape(4, 2**place, 2, 2 ** (left - place - 1), 8, D)
        keeps.append(v[:, :, 0].reshape(-1, 8, D))
        sends.append(v[:, :, 1].reshape(-1, 8, D))
    return which, keeps, jnp.concatenate(sends)


def reduce_sums(bufs, live, which, keeps, got):
    bufs = list(bufs)
    at = 0
    for k, keep in zip(which, keeps):
        total = keep.astype(f32) + got[at : at + keep.shape[0]].astype(f32)
        at += keep.shape[0]
        bufs[k] = (total if not live[k] else total.astype(bf16)).reshape(4, -1, 8, D)
    return bufs


def all_sum(mine, theirs, dp, core, rest, live, finish):
    flip0 = choose(core == 0, FLIPS[0], FLIPS[1])
    flip1 = choose(core == 0, FLIPS[1], FLIPS[0])
    order = []
    for k in range(3):
        at = coordinate(dp, ORDERS[k][0])
        order += [at, at ^ flip1, at ^ flip0, at ^ flip0 ^ flip1]
    order = jnp.stack(order).astype(jnp.int32)
    outs = split_call(order, mine, swap_cores(theirs))
    keep, bufs = list(outs[0::2]), list(outs[1::2])
    first = [None] * 3
    steps = [("z", 0), ("y", 1), ("y", 0), ("x", 1), ("x", 0)]
    for t in range(8):
        axes = [ORDERS[k][(0, 0, 1, 1, 2, 2, 0, 0)[t]] for k in range(3)]
        swap = exchange if 2 <= t < 6 else pair_up
        got = [swap(bufs[k], axes[k], (0, 1, 0, 1, 0, 1, 1, 0)[t]) for k in range(3)]
        if t < len(steps):
            which, kept, sent = reduce_parts(rest, live, *steps[t])
            back = pair_up(sent, *steps[t])
        if t == 7:
            break
        if t == 6:
            stay, came = finish(rest)
            (bufs[2],), (came,) = tie([bufs[2]], [came])
        for k in range(3):
            own = keep if t < 2 else bufs
            if t < len(steps) and (t or k):
                if k:
                    (own[k],), (bufs[k - 1],) = tie([own[k]], [bufs[k - 1]])
                else:
                    (own[0],), (rest[last[0]],) = tie([own[0]], [rest[last[0]]])
            if t == 0:
                first[k] = got[k]
                bufs[k] = plus(keep[k][1], got[k][1])
            elif t == 1:
                total = keep[k][0].astype(f32) + first[k][0].astype(f32) + got[k].astype(f32)
                bufs[k] = total.astype(bf16)
            elif t < 6:
                bufs[k] = plus(bufs[k], got[k])
            else:
                bufs[k] = jnp.stack([bufs[k], got[k]])
        if t < len(steps):
            (back,), (bufs[2],) = tie([back], [bufs[2]])
            rest = reduce_sums(rest, live, which, kept, back)
            last = which
    mine = join_call(order, [v for k in range(3) for v in (bufs[k], got[k])])
    return (*assemble_call(jnp.stack([core, dp]).astype(jnp.int32), mine, swap_cores(mine)), stay, came)


def body(
    tokens,
    item_kind,
    cotangent,
    norm1_gain,
    norm1_shift,
    qkv_weight,
    query_bias,
    value_bias,
    out_weight,
    out_bias,
    norm2_gain,
    norm2_shift,
    ffn_in,
    ffn_in_bias,
    ffn_out,
    ffn_out_bias,
):
    dp = lax.axis_index("dp")
    core = lax.axis_index("expert")
    small = jnp.zeros((3, 2, 64, 12), bf16)
    mine = jnp.stack([norm2_gain, norm2_shift, ffn_out_bias]).reshape(3, 1, 1, 12)
    small = lax.dynamic_update_slice(small, mine, (0, core, dp, 0)).reshape(6, D)
    hidden_bias = lax.dynamic_update_slice(
        jnp.zeros((2, 64, 48), bf16), ffn_in_bias.reshape(1, 1, 48), (core, dp, 0)
    ).reshape(8, D)
    small = jnp.concatenate([small, hidden_bias, jnp.zeros((2, D), bf16)])

    shard = jnp.stack([ffn_in[0].T, ffn_out[0]]).reshape(2, 3, 2, 8, D)
    stay = choose(core == 0, shard[:, :, 0], shard[:, :, 1])
    leave = choose(core == 0, shard[:, :, 1], shard[:, :, 0])
    came = swap_cores(jnp.concatenate([leave.reshape(48, D), small]))
    kinds = item_kind.reshape(1, ITEMS_DEV)
    vectors = [norm1_gain, norm1_shift, query_bias, value_bias]
    (tokens,), (came,) = tie([tokens], [came])
    small = small + came[48:]
    came_w = came[:48].reshape(2, 3, 8, D)
    both = choose(core == 0, jnp.stack([stay, came_w]), jnp.stack([came_w, stay]))
    bufs = [both[:, :, k].reshape(4, 8, D) for k in range(3)]
    n1, triple, bias, lang = qkv_call(kinds, tokens, vectors, qkv_weight)
    other_kinds = swap_cores(kinds)
    other_cot = swap_cores(cotangent)
    bufs, small, n1 = gather_step(bufs, small, 0, n1)
    (triple,), bufs = tie([triple], bufs)
    ctx_a, lse_a = attend_call(triple, bias, 0, 3)
    bufs, small, ctx_a = gather_step(bufs, small, 1, ctx_a)
    (triple,), bufs = tie([triple], bufs)
    ctx_b, lse_b = attend_call(triple, bias, 3, 3)
    bufs, small, ctx_b = gather_step(bufs, small, 2, ctx_b)
    (ctx_b,), bufs = tie([ctx_b], bufs)
    hidden, routed = out_call(ctx_a, ctx_b, out_weight, out_bias, tokens)
    other_routed = swap_cores(routed)
    (other_kinds,), (routed,) = tie([other_kinds], [routed])
    select, up, nv = select_call(jnp.concatenate([kinds, other_kinds]), cotangent, other_cot)
    bufs, small, up = gather_step(bufs, small, 3, up)
    near = near_sends([jnp.concatenate([bufs[0].reshape(4 * PIECE, D), small]), bufs[1], bufs[2]])
    (select,), bufs = tie([select], bufs)
    rows = sort_call(select, routed, other_routed)
    (near[0],), (rows,) = tie([near[0]], [rows])
    small = small + near[0][4 * PIECE :]
    small = small + pair_up(small, "z", 1)
    pairs = [jnp.concatenate([bufs[0].reshape(4 * PIECE, D), near[0]])]
    for k in (1, 2):
        (near[k],), (pairs[-1],) = tie([near[k]], [pairs[-1]])
        pairs.append(jnp.concatenate([bufs[k], near[k]]))
    far = far_sends(pairs)

    hidden_bias = small[6:14].reshape(2, 64, 3, 2, 8)
    hidden_bias = choose(core == 0, hidden_bias[:, :, :, 0], hidden_bias[:, :, :, 1])
    table = relative_table(dp, core)
    spread = jnp.einsum("kps,esku->ekpu", table, hidden_bias, preferred_element_type=f32)
    hidden_bias = spread.reshape(2, 3, 2, 2 * PIECE).transpose(2, 0, 1, 3).reshape(2, 2, HALF_HID)

    pick = lambda a, b: [v for k in range(3) for v in (a[k], b[k])]
    (n2, branch, gn2, db0), dw0 = expert_call(nv, rows, up, hidden_bias[0], pick(bufs, near), small=small)
    (back_own, back_other, db1), dw1 = expert_call(
        nv, n2, up, hidden_bias[1], far, sums=(select, branch, gn2)
    )

    got0 = near_sends(dw0[1::2])
    dw1_own, dw1_near = list(dw1[0::2]), list(dw1[1::2])
    (back_other, *dw1_near), got0 = tie([back_other, *dw1_near], got0)
    back_recv = swap_cores(back_other)
    got = near_sends(dw1_near)
    mixed, gh, gctx, dw_out, delta, small_b = post_call(
        back_own, back_recv, hidden, cotangent, lang, small, out_weight, ctx_a, ctx_b
    )
    dw1_own, (gh,) = tie(dw1_own, [gh])
    send = [plus(dw1_own[k], got[k]) for k in range(3)]
    (triple,), send = tie([triple], send)
    got = far_sends(send)
    parts = list(attend_back_call(triple, gctx, lse_a, lse_b, delta, bias))
    dw0_own, (parts[0],) = tie(dw0[0::2], [parts[0]])
    bufs = [
        (dw0_own[k].astype(f32) + got0[k].astype(f32) + got[k].astype(f32)).astype(bf16) for k in range(3)
    ]
    live = [[(ORDERS[k][i], t) for i in (1, 0) for t in (1, 0)] for k in range(3)]
    (gh,), bufs = tie([gh], bufs)
    which, kept, sent = reduce_parts(bufs, live, "z", 1)
    (gh,), (sent,) = tie([gh], [sent])
    back = pair_up(sent, "z", 1)

    (db0,), (gh,) = tie([db0], [gh])
    db = jnp.stack([db0, db1]).reshape(2, 2, 3, 256).transpose(2, 0, 3, 1).reshape(3, 2, 32, 8, 2)
    db = db.reshape(3, 64, 8, 2).astype(bf16)
    db = jnp.einsum("kps,kpue->esku", table, db, preferred_element_type=f32)
    zero = jnp.zeros_like(db)
    db = choose(core == 0, jnp.stack([db, zero], 3), jnp.stack([zero, db], 3)).reshape(8, D)

    mine, theirs, tokens_grad = final_call(
        core.reshape(1), n1, tokens, norm1_gain, qkv_weight, gh, dw_out, small_b, db, parts
    )

    (theirs,), (back,) = tie([theirs], [back])
    bufs = reduce_sums(bufs, live, which, kept, back)

    def finish(bufs):
        shards = jnp.stack(bufs).reshape(3, 2, 2, 8, D)
        stay = choose(core == 0, shards[:, 0], shards[:, 1])
        return stay, swap_cores(choose(core == 0, shards[:, 1], shards[:, 0]))

    grad_qkv, grad_out, vectors, mine, bias_grad, stay, came = all_sum(mine, theirs, dp, core, bufs, live, finish)
    full = choose(core == 0, jnp.stack([stay, came], 2), jnp.stack([came, stay], 2))
    full = full.transpose(1, 0, 2, 3, 4).reshape(2, 48, D)

    return (
        mixed,
        tokens_grad,
        vectors[0],
        vectors[1],
        grad_qkv,
        vectors[2],
        vectors[3],
        grad_out,
        vectors[4],
        mine[0],
        mine[1],
        full[0].T[None],
        bias_grad,
        full[1][None],
        mine[2],
    )


def solution(mesh):
    both = ("dp", "expert")
    in_specs = (
        P(both, None),
        P(both),
        P(both, None),
        P(),
        P(),
        P(),
        P(),
        P(),
        P(),
        P(),
        P("expert", "dp"),
        P("expert", "dp"),
        P("expert", None, "dp"),
        P("expert", "dp"),
        P("expert", "dp", None),
        P("expert", "dp"),
    )
    out_specs = (
        P(both, None),
        P(both, None),
        P(),
        P(),
        P(),
        P(),
        P(),
        P(),
        P(),
        P("expert", "dp"),
        P("expert", "dp"),
        P("expert", None, "dp"),
        P("expert", "dp"),
        P("expert", "dp", None),
        P("expert", "dp"),
    )
    return jax.shard_map(body, mesh=mesh, in_specs=in_specs, out_specs=out_specs, check_vma=False)
```
